128 devices in a mesh: dp: 128 (over z, y, x, core).
Axes of the slice: x: 4, y: 4, z: 4, core: 2. Of those that a mesh axis runs over, the one named last changes fastest.
Arguments:
- tokens: bfloat16 [2, 16384, 960], P(None, 'dp'), may hold values from -6 to 6
- segment_ids: int32 [2, 16384], P(None, 'dp'), may hold values from 0 to 128, as said below
- attn_weight: bfloat16 [2560, 960], P('dp'), may hold values from -0.25 to 0.25
- gate_up: bfloat16 [2, 2560, 960], P(None, 'dp'), may hold values from -0.1875 to 0.1875
- down_weight: bfloat16 [2560, 960], P('dp'), may hold values from -0.125 to 0.125
- norm_gains: bfloat16 [1920], P('dp'), may hold values from 0.5 to 1.5
- cotangent: bfloat16 [2, 16384, 960], P(None, 'dp'), may hold values from -6 to 6
Outputs:
- layer_output: bfloat16 [2, 16384, 960], P(None, 'dp')
- input_grad: bfloat16 [2, 16384, 960], P(None, 'dp')
- attn_grad: float32 [2560, 960], P('dp')
- gate_up_grad: float32 [2, 2560, 960], P(None, 'dp')
- down_grad: float32 [2560, 960], P('dp')
- gains_grad: float32 [1920], P('dp')
The draws below stay inside these ranges and needn't reach their ends.
Inputs may be any that keep to these rules, and one draw needn't show every extreme that they name: `segment_ids`: within each micro-batch every aligned block of 128 slots (one device's slots) holds whole sequences numbered 0, 1, 2, ... in order, never falling; slots numbered 128 are padding at the block's end; every block is at least half full, and in every draw some block is one sequence of 128 tokens.
All inputs are finite; a program needn't handle non-finite values.
Results may differ from the reference program's by a relative error of at most 0.015.
Values may be sent and summed in bfloat16 or wider, within the bound.
No kernel may reach another device: no remote copies, remote signals or barrier semaphores. Data moves between devices by JAX's collectives and lax.ppermute only.
A program may use at most 192 MiB of HBM per device.

```python
import jax
import jax.numpy as jnp
from jax import lax

D = 960
HEADS = 15
KV_HEADS = 5
HEAD_DIM = 64
FF = 2560
TOK_MB = 128
MICRO = 2
ATT_ROWS = 2560
TOKENS_MB = 16384


def draw_segment_ids(key, part):
    key = jax.random.fold_in(key, 7)
    start_key, fill_key = jax.random.split(key)
    blocks = TOKENS_MB // TOK_MB
    places = jnp.arange(TOK_MB)
    starts = jax.random.randint(start_key, (MICRO, blocks, TOK_MB), 0, max(TOK_MB // 4, 2)) == 0
    leading = (jnp.arange(MICRO)[:, None, None] == 0) & (jnp.arange(blocks)[None, :, None] == 0)
    starts = jnp.where(leading, False, starts) | (places == 0)
    filled = jax.random.randint(fill_key, (MICRO, blocks, 1), TOK_MB // 2, TOK_MB)
    filled = jnp.where(jnp.arange(blocks)[None, :, None] == 0, TOK_MB, filled)
    numbers = jnp.cumsum(starts.astype(jnp.int32), axis=-1) - 1
    numbers = jnp.where(places < filled, numbers, TOK_MB)
    return numbers.reshape(MICRO, TOKENS_MB).astype(jnp.int32)


def levels(key, shape, cuts, least, top_value):
    gain = 1.0
    for axis_at, parts in cuts:
        draws = jax.random.uniform(jax.random.fold_in(jax.random.fold_in(key, 6), axis_at), (parts,), jnp.float32, least / len(cuts), top_value / len(cuts))
        gain = gain * jnp.repeat(jnp.exp(draws), shape[axis_at] // parts).reshape((-1,) + (1,) * (len(shape) - 1 - axis_at))
    return gain


def centred(rng, extent, deviation, reach, cuts=(), dtype=jnp.bfloat16):
    gain = levels(rng, extent, cuts, -0.22, 0.18) if cuts else 1.0
    drawn = jax.random.normal(rng, extent, jnp.float32) * deviation * gain
    return jnp.minimum(jnp.maximum(drawn, -reach), reach).astype(dtype)


def setup_inputs(seed: int = 0) -> dict:
    splits = jax.random.split(jax.random.key(seed), 8)
    return {
        "tokens": centred(splits[0], (MICRO, TOKENS_MB, D), 1.0, 6.0, ((1, 128),)),
        "segment_ids": draw_segment_ids(jax.random.fold_in(splits[7], 71), 0),
        "attn_weight": centred(splits[2], (ATT_ROWS, D), (D // 2) ** -0.5, 0.25, ((0, 128),)),
        "gate_up": centred(splits[3], (2, FF, D), D ** -0.5, 0.1875, ((1, 128),)),
        "down_weight": centred(splits[4], (FF, D), FF ** -0.5, 0.125, ((0, 128),)),
        "norm_gains": jnp.clip(1.0 + 0.1 * jax.random.normal(splits[5], (2 * D,), jnp.float32), 0.5, 1.5).astype(jnp.bfloat16),
        "cotangent": centred(splits[6], (MICRO, TOKENS_MB, D), 1.0, 6.0, ((1, 128),)),
    }


EPS = 1e-05
THETA = 100000.0
NEG_FILL = -1e+30

@jax.custom_vjp
def low(v):
    return lax.optimization_barrier(v.astype(jnp.bfloat16)).astype(jnp.float32)

@jax.custom_vjp
def low_back(v):
    return v

def low_keep(v):
    return (low(v), None)

def low_pass(kept, grad):
    return (grad,)

def back_keep(v):
    return (v, None)

def back_low(kept, grad):
    return (low(grad),)
low.defvjp(low_keep, low_pass)
low_back.defvjp(back_keep, back_low)

def rope_tables(seg_blocks):
    count = seg_blocks.shape[-1]
    places = jnp.arange(count)
    allowed = (seg_blocks[..., :, None] == seg_blocks[..., None, :]) & (places[None, :] <= places[:, None])
    position = lax.optimization_barrier(jnp.sum(allowed.astype(jnp.float32), axis=-1)) - 1.0
    freqs = THETA ** (-2.0 * jnp.arange(HEAD_DIM // 2).astype(jnp.float32) / HEAD_DIM)
    angles = position[..., None] * freqs
    return (jnp.cos(angles), jnp.sin(angles))

def rotate(values, cosine_table, sine_table):
    half_dim = values.shape[-1] // 2
    former = values[..., :half_dim]
    latter = values[..., half_dim:]
    cosine = cosine_table[..., None, :]
    sine = sine_table[..., None, :]
    return jnp.concatenate([former * cosine - latter * sine, latter * cosine + former * sine], axis=-1)

def attend(pieces):
    queries, keys_rot, values, seg_row = pieces
    count = seg_row.shape[0]
    places = jnp.arange(count)
    allowed = (seg_row[:, None] == seg_row[None, :]) & (places[None, :] <= places[:, None])
    raw = low_back(jnp.einsum('qkgd,tkd->kgqt', queries, keys_rot, precision=lax.Precision.HIGHEST))
    scores = jnp.where(allowed, raw * HEAD_DIM ** (-0.5), NEG_FILL)
    row_max = lax.optimization_barrier(jnp.max(scores, axis=-1, keepdims=True))
    expd = jnp.exp(scores - row_max)
    probs = low(expd / lax.optimization_barrier(jnp.sum(expd, axis=-1, keepdims=True)))
    return jnp.einsum('kgqt,tkd->qkgd', probs, values, precision=lax.Precision.HIGHEST)

def layer(inputs, attn_full, gate_full, down_full, gain_full, seg_blocks, live_blocks):
    highest = lax.Precision.HIGHEST
    blocks, count = seg_blocks.shape
    kv_width = KV_HEADS * HEAD_DIM
    qkv_rows = D + 2 * kv_width
    group = HEADS // KV_HEADS
    flat_rows = inputs.reshape(-1, D)
    live_rows = live_blocks.reshape(-1, 1)
    normed_one = low(flat_rows * lax.rsqrt(lax.optimization_barrier(jnp.mean(flat_rows * flat_rows, axis=-1, keepdims=True)) + EPS) * gain_full[:D])
    projected = low_back(jnp.dot(normed_one, attn_full[:qkv_rows].T, precision=highest))
    cosine_table, sine_table = rope_tables(seg_blocks)
    cosine_table = cosine_table.reshape(-1, HEAD_DIM // 2)
    sine_table = sine_table.reshape(-1, HEAD_DIM // 2)
    queries = low(rotate(projected[:, :D].reshape(-1, HEADS, HEAD_DIM), cosine_table, sine_table))
    keys_rot = low(rotate(projected[:, D:D + kv_width].reshape(-1, KV_HEADS, HEAD_DIM), cosine_table, sine_table))
    values = low(projected[:, D + kv_width:].reshape(-1, KV_HEADS, HEAD_DIM))
    queries = queries.reshape(blocks, count, KV_HEADS, group, HEAD_DIM)
    keys_rot = keys_rot.reshape(blocks, count, KV_HEADS, HEAD_DIM)
    values = values.reshape(blocks, count, KV_HEADS, HEAD_DIM)
    attended = lax.map(jax.checkpoint(attend), (queries, keys_rot, values, seg_blocks))
    attended = low(low_back(attended.reshape(-1, D)))
    branch_attn = low_back(jnp.dot(attended, attn_full[qkv_rows:], precision=highest))
    hidden_res = flat_rows + live_rows * branch_attn
    normed_two = low(hidden_res * lax.rsqrt(lax.optimization_barrier(jnp.mean(hidden_res * hidden_res, axis=-1, keepdims=True)) + EPS) * gain_full[D:])
    gate_vals = low_back(jnp.dot(normed_two, gate_full[0].T, precision=highest))
    up_vals = low_back(jnp.dot(normed_two, gate_full[1].T, precision=highest))
    product = low(gate_vals * jax.nn.sigmoid(gate_vals) * up_vals)
    branch_mlp = low_back(jnp.dot(product, down_full, precision=highest))
    return (hidden_res + live_rows * branch_mlp).reshape(inputs.shape)

def reference(tokens, segment_ids, attn_weight, gate_up, down_weight, norm_gains, cotangent):
    seg_blocks = segment_ids.reshape(-1, TOK_MB)
    live_blocks = (seg_blocks < TOK_MB).astype(jnp.float32)

    def forward(inputs, attn_full, gate_full, down_full, gain_full):
        return layer(inputs, attn_full, gate_full, down_full, gain_full, seg_blocks, live_blocks)
    result, pullback = jax.vjp(forward, tokens.astype(jnp.float32), attn_weight.astype(jnp.float32), gate_up.astype(jnp.float32), down_weight.astype(jnp.float32), norm_gains.astype(jnp.float32))
    grad_in, grad_attn, grad_gate, grad_down, grad_gain = pullback(cotangent.astype(jnp.float32))
    return (result.astype(jnp.bfloat16), grad_in.astype(jnp.bfloat16), grad_attn, grad_gate, grad_down, grad_gain)
```

```python
import jax
import jax.numpy as jnp
from jax import lax
from jax.experimental import pallas as pl
from jax.experimental.pallas import tpu as pltpu
from jax.sharding import Mesh, PartitionSpec as P

HEADS = 15
KV_HEADS = 5
GROUP = HEADS // KV_HEADS
HEAD_DIM = 64
MICRO = 2
WIDTH = 960
TOK = 128
BLOCK = 80
EPS = 1e-05
THETA = 100000.0
NEG_FILL = -1e30
AXES = ("z", "y", "x", "c")
BF = jnp.bfloat16
F32 = jnp.float32


def flat(z, y, x, c):
    return (((z % 4) * 4 + y % 4) * 4 + x % 4) * 2 + c % 2


def everywhere():
    return [(z, y, x, c) for z in range(4) for y in range(4) for x in range(4) for c in range(2)]


def shift_x(step):
    return [(flat(*d), flat(d[0], d[1], d[2] + step, d[3])) for d in everywhere()]


def shift_core():
    return [(flat(*d), flat(d[0], d[1], d[2], d[3] + 1)) for d in everywhere()]


def shift_plane(step, inner):
    pairs = []
    for z, y, x, c in everywhere():
        along_y = (c == 0) == inner
        pairs.append((flat(z, y, x, c), flat(z, y + step, x, c) if along_y else flat(z + step, y, x, c)))
    return pairs


def permute(value, pairs):
    return lax.ppermute(value, AXES, pairs)


def fetch(value, make):
    return [value] + [permute(value, make(-r)) for r in (1, 3, 2)]


def fetch_ordered(value, make):
    got = fetch(value, make)
    return [got[0], got[1], got[3], got[2]]


def place_kernel(where_ref, *refs):
    own, sib = refs[0:4], refs[4:8]
    qkv, out, gains, sem, gsem = refs[8:13]
    z, y, c = where_ref[0], where_ref[1], where_ref[2]
    gain_copies = []
    pairs = []
    for r2 in range(4):
        for r1 in range(4):
            k = r2 * 4 + r1
            for which, group in enumerate((own, sib)):
                core = c if which == 0 else 1 - c
                rz = jnp.where(core == 0, r2, r1)
                ry = jnp.where(core == 0, r1, r2)
                row = lax.rem(z + rz, 4) * 4 + lax.rem(y + ry, 4)
                source = group[r2].at[r1, pl.ds(0, BLOCK)]
                first = pltpu.make_async_copy(source, qkv.at[jnp.minimum(row, 9), core], sem.at[which, k])
                second = pltpu.make_async_copy(source, out.at[jnp.maximum(row, 10) - 10, core], sem.at[which, k])
                pairs.append((row < 10, first, second))
                if which == 0:
                    gain_copies.append(
                        pltpu.make_async_copy(
                            group[r2].at[r1, pl.ds(BLOCK, 16)], gains.at[row], gsem.at[k]
                        )
                    )
    for early, first, second in pairs:
        pl.when(early)(first.start)
        pl.when(jnp.logical_not(early))(second.start)
    for copy in gain_copies:
        copy.start()
    for early, first, second in pairs:
        pl.when(early)(first.wait)
        pl.when(jnp.logical_not(early))(second.wait)
    for copy in gain_copies:
        copy.wait()


def place(where, own, sib):
    anywhere = pl.BlockSpec(memory_space=pl.ANY)
    local = pl.BlockSpec(memory_space=pltpu.VMEM)
    return pl.pallas_call(
        place_kernel,
        in_specs=[pl.BlockSpec(memory_space=pltpu.SMEM)] + [anywhere] * 8,
        out_specs=[local] * 3,
        out_shape=[
            jax.ShapeDtypeStruct((10, 2, BLOCK, WIDTH), BF),
            jax.ShapeDtypeStruct((6, 2, BLOCK, WIDTH), BF),
            jax.ShapeDtypeStruct((16, 16, WIDTH), BF),
        ],
        scratch_shapes=[pltpu.SemaphoreType.DMA((2, 16)), pltpu.SemaphoreType.DMA((16,))],
        compiler_params=pltpu.CompilerParams(vmem_limit_bytes=8 * 2**20),
        name="place_rows",
    )(where, *own, *sib)


def attn_grads_kernel(where_ref, proj, att, normed, branch, gains, ours, theirs):
    z, y, c = where_ref[0], where_ref[1], where_ref[2]
    jobs = [(proj, 0, 640, normed), (proj, 640, 640, normed), (proj, 1280, 320, normed)]
    jobs += [(att, 0, 640, branch), (att, 640, 320, branch)]
    row = 0
    for source, start, size, right in jobs:
        block = lax.dot_general(
            source[:, start : start + size], right[...], (((0,), (0,)), ((), ())), preferred_element_type=F32
        ).astype(BF)
        for k in range(size // 160):
            rz = lax.rem(row // 4 - z + 4, 4)
            ry = lax.rem(row % 4 - y + 4, 4)
            zy, yz = rz * 4 + ry, ry * 4 + rz
            lower = block[160 * k : 160 * k + 80]
            upper = block[160 * k + 80 : 160 * k + 160]

            @pl.when(c == 0)
            def _(lower=lower, upper=upper, zy=zy, yz=yz):
                ours[zy] = lower
                theirs[yz] = upper

            @pl.when(c != 0)
            def _(lower=lower, upper=upper, zy=zy, yz=yz):
                ours[yz] = upper
                theirs[zy] = lower

            row += 1
    theirs[16] = jnp.zeros((BLOCK, WIDTH), BF)
    theirs[16, 0:16] = gains[...]


def attn_grads(where, proj, att, normed, branch, gains):
    local = pl.BlockSpec(memory_space=pltpu.VMEM)
    return pl.pallas_call(
        attn_grads_kernel,
        in_specs=[pl.BlockSpec(memory_space=pltpu.SMEM)] + [local] * 5,
        out_specs=[local] * 2,
        out_shape=[
            jax.ShapeDtypeStruct((16, BLOCK, WIDTH), BF),
            jax.ShapeDtypeStruct((17, BLOCK, WIDTH), BF),
        ],
        compiler_params=pltpu.CompilerParams(vmem_limit_bytes=12 * 2**20),
        name="attn_grads",
    )(where, proj, att, normed, branch, gains)


def ffn_kernel(count, first, normed, cot, *refs):
    chunks, refs = refs[:count], refs[count:]
    if first:
        branch, back = 0.0, 0.0
    else:
        branch, back = refs[0][...], refs[1][...]
        refs = refs[2:]
    grads, branch_out, back_out = refs[:count], refs[count], refs[count + 1]
    half = 4 * BLOCK
    for chunk, grad in zip(chunks, grads):
        pair = chunk[0:2].reshape(2 * half, WIDTH)
        down = chunk[2].reshape(half, WIDTH)
        both = dot(pair, normed[...], NT)
        grad_prod = dot(down, cot[...], NT)
        gate, up = both[:half], both[half:]
        sigma = 1.0 / (1.0 + jnp.exp(-gate))
        gated = gate * sigma
        product = (gated * up).astype(BF)
        grad_gate = (grad_prod * up * sigma * (1.0 + gate * (1.0 - sigma))).astype(BF)
        grad_up = (grad_prod * gated).astype(BF)
        grad_pair = jnp.concatenate([grad_gate, grad_up], axis=0)
        back = back + dot(grad_pair, pair, TN)
        grad[0:2] = dot(grad_pair, normed[...], NN).astype(BF).reshape(2, 4, BLOCK, WIDTH)
        grad[2] = dot(product, cot[...], NN).astype(BF).reshape(4, BLOCK, WIDTH)
        branch = branch + dot(product, down, TN)
    branch_out[...] = branch
    back_out[...] = back


def ffn(normed, cot, chunks, sums):
    local = pl.BlockSpec(memory_space=pltpu.VMEM)
    count, tokens = len(chunks), normed.shape[0]
    sums = list(sums)
    held = len(sums)
    out = pl.pallas_call(
        lambda *refs: ffn_kernel(count, held == 0, *refs),
        in_specs=[local] * (2 + count + held),
        out_specs=[local] * (count + 2),
        out_shape=[jax.ShapeDtypeStruct((3, 4, BLOCK, WIDTH), BF)] * count
        + [jax.ShapeDtypeStruct((tokens, WIDTH), F32)] * 2,
        input_output_aliases={2 + count + i: count + i for i in range(held)},
        compiler_params=pltpu.CompilerParams(vmem_limit_bytes=16 * 2**20),
        cost_estimate=pl.CostEstimate(
            flops=count * 18 * tokens * 4 * BLOCK * WIDTH,
            transcendentals=count * tokens * 4 * BLOCK,
            bytes_accessed=count * 12 * 4 * BLOCK * WIDTH,
        ),
        name="ffn_chunks",
    )(normed, cot, *chunks, *sums)
    return out[:count], out[count:]


def rope_tables(seg):
    places = jnp.arange(TOK)
    allowed = (seg[:, :, None] == seg[:, None, :]) & (places[None, :] <= places[:, None])
    position = jnp.sum(allowed.astype(F32), axis=-1) - 1.0
    freqs = THETA ** (-2.0 * jnp.arange(HEAD_DIM // 2).astype(F32) / HEAD_DIM)
    angles = position[..., None] * freqs
    return jnp.cos(angles)[:, :, None, :], jnp.sin(angles)[:, :, None, :], allowed


def rotate(values, cosine, sine):
    half = HEAD_DIM // 2
    former, latter = values[..., :half], values[..., half:]
    return jnp.concatenate([former * cosine - latter * sine, latter * cosine + former * sine], axis=-1)


def inv_rms(values):
    return lax.rsqrt(jnp.mean(values * values, axis=-1, keepdims=True) + EPS)


def norm_back(grad_normed, source, inverse, gain_vec):
    scaled = source * inverse
    grad_scaled = grad_normed * gain_vec
    grad_gain = jnp.sum(grad_normed * scaled, axis=0)
    mean = jnp.mean(grad_scaled * scaled, axis=-1, keepdims=True)
    return inverse * (grad_scaled - scaled * mean), grad_gain


def dot(left, right, dims):
    return lax.dot_general(left, right, (dims, ((), ())), preferred_element_type=F32)


NT = ((1,), (1,))
NN = ((1,), (0,))
TN = ((0,), (0,))


def total(parts):
    out = parts[0].astype(F32)
    for part in parts[1:]:
        out = out + part.astype(F32)
    return out


def body(tokens, segment_ids, attn_weight, gate_up, down_weight, norm_gains, cotangent):
    z, y, x, c = (lax.axis_index(a) for a in AXES)
    rows = MICRO * TOK
    kv_width = KV_HEADS * HEAD_DIM
    qkv_rows = WIDTH + 2 * kv_width

    gain_row = jnp.pad(norm_gains[None, :], ((0, 15), (0, WIDTH - 15)))
    shard = jnp.concatenate([attn_weight, gate_up[0], gate_up[1], down_weight, gain_row], axis=0)
    near = jnp.stack(fetch_ordered(shard, shift_x))
    ffn_block = near[:, 20:80].reshape(4, 3, 20, WIDTH).transpose(1, 0, 2, 3).reshape(3, BLOCK, WIDTH)
    head = jnp.concatenate([near[:, :20], near[:, 80:81]], axis=1)
    head = lax.dynamic_slice_in_dim(jnp.concatenate([head, head], axis=0), lax.rem(4 - x, 4), 4, axis=0)
    other = permute(head, shift_core())
    both = jnp.stack([jnp.where(c == 0, head, other), jnp.where(c == 0, other, head)], axis=1)
    attn_half = lax.dynamic_slice_in_dim(both[:, :, :20].reshape(2 * BLOCK, WIDTH), c * BLOCK, BLOCK, axis=0)
    gain_near = jnp.pad(both[:, :, 20, :15].reshape(1, 120), ((0, 15), (0, WIDTH - 120)))
    attn_block = jnp.concatenate([attn_half, gain_near], axis=0)

    block = jnp.concatenate([attn_block, ffn_block.reshape(3 * BLOCK, WIDTH)], axis=0)
    got = fetch_ordered(block, lambda s: shift_plane(s, True))
    attn_one = jnp.stack([part[:96] for part in got])
    ffn_one = jnp.stack([part[96:].reshape(3, BLOCK, WIDTH) for part in got], axis=1)
    own = fetch_ordered(attn_one, lambda s: shift_plane(s, False))
    sib = [permute(v, shift_core()) for v in own]
    where = jnp.stack([z, y, c]).astype(jnp.int32)
    w_qkv, w_out, gain_full = place(where, own, sib)
    w_qkv = w_qkv.reshape(qkv_rows, WIDTH)
    w_out = w_out.reshape(WIDTH, WIDTH)
    gain_full = gain_full[:, 0, :120].astype(F32)
    gain_attn, gain_mlp = gain_full[:8].reshape(WIDTH), gain_full[8:].reshape(WIDTH)

    ffn_send, _ = lax.optimization_barrier((ffn_one, own))
    ffn_next = permute(ffn_send, shift_plane(-1, False))
    ffn_last = permute(ffn_send, shift_plane(-3, False))
    ffn_send, ffn_next, ffn_last = lax.optimization_barrier((ffn_send, ffn_next, ffn_last))
    ffn_far = permute(ffn_send, shift_plane(-2, False))

    inputs = tokens.reshape(rows, WIDTH).astype(F32)
    live = (segment_ids.reshape(rows, 1) < TOK).astype(F32)
    grad_out = cotangent.reshape(rows, WIDTH).astype(F32)
    grad_mlp = (live * grad_out).astype(BF)
    grad_mlp_all = jnp.concatenate([grad_mlp, permute(grad_mlp, shift_core())], axis=0)
    scale_one = inv_rms(inputs)
    normed_one = (inputs * scale_one * gain_attn).astype(BF)
    projected = dot(normed_one, w_qkv, NT)
    cosine, sine, allowed = rope_tables(segment_ids)
    allowed = allowed[:, None, None]
    queries = rotate(projected[:, :WIDTH].reshape(MICRO, TOK, HEADS, HEAD_DIM), cosine, sine)
    queries = queries.astype(BF).reshape(MICRO, TOK, KV_HEADS, GROUP, HEAD_DIM)
    keys = projected[:, WIDTH : WIDTH + kv_width].reshape(MICRO, TOK, KV_HEADS, HEAD_DIM)
    keys = rotate(keys, cosine, sine).astype(BF)
    values = projected[:, WIDTH + kv_width :].reshape(MICRO, TOK, KV_HEADS, HEAD_DIM).astype(BF)
    scores = jnp.einsum("bqkgd,btkd->bkgqt", queries, keys, preferred_element_type=F32)
    scores = jnp.where(allowed, scores * HEAD_DIM ** (-0.5), NEG_FILL)
    row_max = jnp.max(scores, axis=-1, keepdims=True)
    expd = jnp.exp(scores - row_max)
    probs = expd / jnp.sum(expd, axis=-1, keepdims=True)
    probs_low = probs.astype(BF)
    attended = jnp.einsum("bkgqt,btkd->bqkgd", probs_low, values, preferred_element_type=F32)
    attended = attended.reshape(rows, WIDTH).astype(BF)
    hidden = inputs + live * dot(attended, w_out, NN)

    scale_two = inv_rms(hidden)
    normed_two = (hidden * scale_two * gain_mlp).astype(BF)
    normed_all = jnp.concatenate([normed_two, permute(normed_two, shift_core())], axis=0)
    (grad_zero,), sums = ffn(normed_all, grad_mlp_all, [ffn_one], [])
    (grad_next, grad_last), sums = ffn(normed_all, grad_mlp_all, [ffn_next, ffn_last], sums)
    (grad_far,), (branch, grad_normed) = ffn(normed_all, grad_mlp_all, [ffn_far], sums)
    grad_normed = grad_normed[:rows] + permute(grad_normed[rows:].astype(BF), shift_core()).astype(F32)
    branch = branch[:rows] + permute(branch[rows:].astype(BF), shift_core()).astype(F32)
    result = (hidden + live * branch).astype(BF)

    got = [
        grad_zero,
        permute(grad_next, shift_plane(1, False)),
        permute(grad_last, shift_plane(3, False)),
        permute(grad_far, shift_plane(2, False)),
    ]
    mine = total(got).astype(BF)
    got = [mine[:, 0]] + [permute(mine[:, r], shift_plane(r, True)) for r in (1, 3, 2)]
    mine = total(got).astype(BF).reshape(3, 4, 20, WIDTH)
    got = [mine[:, 0]] + [permute(mine[:, r], shift_x(r)) for r in (1, 3, 2)]
    ffn_owned = total(got)

    grad_hidden, grad_gain_mlp = norm_back(grad_normed, hidden, scale_two, gain_mlp)
    grad_hidden = grad_out + grad_hidden
    grad_branch = (live * grad_hidden).astype(BF)
    grad_att = dot(grad_branch, w_out, NT).astype(BF)
    grad_att = grad_att.reshape(MICRO, TOK, KV_HEADS, GROUP, HEAD_DIM)
    grad_probs = jnp.einsum("bqkgd,btkd->bkgqt", grad_att, values, preferred_element_type=F32)
    delta = jnp.sum(probs * grad_probs, axis=-1, keepdims=True)
    grad_scores = (HEAD_DIM ** (-0.5) * probs * (grad_probs - delta)).astype(BF)
    grad_q = jnp.einsum("bkgqt,btkd->bqkgd", grad_scores, keys, preferred_element_type=F32)
    grad_k = jnp.einsum("bkgqt,bqkgd->btkd", grad_scores, queries, preferred_element_type=F32)
    grad_v = jnp.einsum("bkgqt,bqkgd->btkd", probs_low, grad_att, preferred_element_type=F32)
    grad_q = rotate(grad_q.reshape(MICRO, TOK, HEADS, HEAD_DIM), cosine, -sine)
    grad_k = rotate(grad_k, cosine, -sine)
    grad_proj = jnp.concatenate(
        [grad_q.reshape(rows, WIDTH), grad_k.reshape(rows, kv_width), grad_v.reshape(rows, kv_width)], axis=1
    ).astype(BF)
    grad_normed_one = dot(grad_proj, w_qkv, NN)
    grad_inputs, grad_gain_attn = norm_back(grad_normed_one, inputs, scale_one, gain_attn)
    grad_inputs = (grad_hidden + grad_inputs).astype(BF)

    def spread(value):
        return jnp.pad(value.astype(BF), ((0, 14), (0, 0)))

    gain_grads = jnp.stack([grad_gain_attn, grad_gain_mlp])
    ours, theirs = attn_grads(where, grad_proj, attended, normed_one, grad_branch, spread(gain_grads))
    swapped = permute(theirs, shift_core())
    mine = total([ours, swapped[:16]]).astype(BF).reshape(4, 4 * BLOCK, WIDTH)
    gain_grads = gain_grads + swapped[16, :2].astype(F32)

    def exchange(blocks, gain_grads, make):
        count = blocks.shape[1]
        low = spread(gain_grads)
        got = [
            permute(jnp.concatenate([blocks[r], low], axis=0), make(r)) for r in (1, 3, 2)
        ]
        blocks = total([blocks[0]] + [part[:count] for part in got])
        return blocks, total([gain_grads] + [part[count : count + 2] for part in got])

    mine, gain_grads = exchange(mine, gain_grads, lambda r: shift_plane(r, False))
    mine = mine.astype(BF).reshape(4, BLOCK, WIDTH)
    mine, gain_grads = exchange(mine, gain_grads, lambda r: shift_plane(r, True))
    mine = mine.astype(BF).reshape(2, 2, 20, WIDTH)
    keep = lax.dynamic_index_in_dim(mine, c, 1, keepdims=False)
    give = lax.dynamic_index_in_dim(mine, 1 - c, 1, keepdims=False)
    take = permute(give, shift_core())
    mine = jnp.concatenate([jnp.where(c == 0, keep, take), jnp.where(c == 0, take, keep)], axis=0)
    mine = lax.dynamic_slice_in_dim(jnp.concatenate([mine, mine], axis=0), x, 4, axis=0)
    attn_owned, gain_grads = exchange(mine, gain_grads, shift_x)
    gain_owned = lax.dynamic_slice_in_dim(gain_grads.reshape(2 * WIDTH), flat_index(z, y, x, c) * 15, 15)
    return (
        result.reshape(MICRO, TOK, WIDTH),
        grad_inputs.reshape(MICRO, TOK, WIDTH),
        attn_owned,
        ffn_owned[:2],
        ffn_owned[2],
        gain_owned,
    )


def flat_index(z, y, x, c):
    return ((z * 4 + y) * 4 + x) * 2 + c


def solution(mesh):
    grid = Mesh(mesh.devices.reshape(4, 4, 4, 2), AXES)
    return jax.shard_map(
        body,
        mesh=grid,
        in_specs=(
            P(None, AXES, None),
            P(None, AXES),
            P(AXES, None),
            P(None, AXES, None),
            P(AXES, None),
            P(AXES),
            P(None, AXES, None),
        ),
        out_specs=(
            P(None, AXES, None),
            P(None, AXES, None),
            P(AXES, None),
            P(None, AXES, None),
            P(AXES, None),
            P(AXES),
        ),
        check_vma=False,
    )
```

```python
import jax
import jax.numpy as jnp
from jax import lax
from jax.experimental import pallas as pl
from jax.experimental.pallas import tpu as pltpu
from jax.sharding import Mesh, PartitionSpec as P

HEADS = 15
KV_HEADS = 5
GROUP = HEADS // KV_HEADS
HEAD_DIM = 64
MICRO = 2
WIDTH = 960
TOK = 128
BLOCK = 80
EPS = 1e-05
THETA = 100000.0
NEG_FILL = -1e30
AXES = ("z", "y", "x", "c")
BF = jnp.bfloat16
F32 = jnp.float32


def flat(z, y, x, c):
    return (((z % 4) * 4 + y % 4) * 4 + x % 4) * 2 + c % 2


def everywhere():
    return [(z, y, x, c) for z in range(4) for y in range(4) for x in range(4) for c in range(2)]


def shift_x(step):
    return [(flat(*d), flat(d[0], d[1], d[2] + step, d[3])) for d in everywhere()]


def shift_core():
    return [(flat(*d), flat(d[0], d[1], d[2], d[3] + 1)) for d in everywhere()]


def shift_plane(step, inner):
    pairs = []
    for z, y, x, c in everywhere():
        along_y = (c == 0) == inner
        pairs.append((flat(z, y, x, c), flat(z, y + step, x, c) if along_y else flat(z + step, y, x, c)))
    return pairs


def to_owner():
    return [(flat(z, y, j, c), flat(z, y, 2 * c + j // 2, j % 2)) for z, y, j, c in everywhere()]


def permute(value, pairs):
    return lax.ppermute(value, AXES, pairs)


def fetch(value, make):
    return [value] + [permute(value, make(-r)) for r in (1, 3, 2)]


def fetch_ordered(value, make):
    got = fetch(value, make)
    return [got[0], got[1], got[3], got[2]]


def move_rows(where_ref, own, sib, weights, gains):
    z, y, c = where_ref[0], where_ref[1], where_ref[2]
    for r2 in range(4):
        for r1 in range(4):
            for which, group in enumerate((own, sib)):
                core = c if which == 0 else 1 - c
                rz = jnp.where(core == 0, r2, r1)
                ry = jnp.where(core == 0, r1, r2)
                row = lax.rem(z + rz, 4) * 4 + lax.rem(y + ry, 4)
                weights[row, core] = group[r2][r1, 0:BLOCK]
                if which == 0:
                    gains[row] = group[r2][r1, BLOCK : BLOCK + 16]


def unpack_gains(gains):
    raw = gains[:, 0, 0:128].astype(BF)
    lane = lax.broadcasted_iota(jnp.int32, (128, WIDTH), 1)
    entry = lax.broadcasted_iota(jnp.int32, (128, WIDTH), 0)
    pick = jnp.where(lane - ((lane * 8739) >> 20) * 120 == entry, 1.0, 0.0).astype(BF)
    spread = dot(raw, pick, NN)
    lane = lax.broadcasted_iota(jnp.int32, (16, WIDTH), 1)
    row = lax.broadcasted_iota(jnp.int32, (16, WIDTH), 0)
    block = (lane * 8739) >> 20
    attn = jnp.sum(jnp.where(row == block, spread, 0.0), axis=0, keepdims=True)
    mlp = jnp.sum(jnp.where(row == block + 8, spread, 0.0), axis=0, keepdims=True)
    return attn, mlp


def heads_of(ref, kv, b):
    lanes = slice(TOK * b, TOK * (b + 1))
    parts = [ref[HEAD_DIM * h : HEAD_DIM * (h + 1), lanes] for h in range(GROUP * kv, GROUP * (kv + 1))]
    return jnp.concatenate(parts, axis=1)


def turn(values, cosine, sine):
    split = values.reshape(-1, 2, HEAD_DIM // 2, values.shape[-1])
    former, latter = split[:, 0], split[:, 1]
    turned = jnp.stack([former * cosine - latter * sine, latter * cosine + former * sine], axis=1)
    return turned.reshape(values.shape)


def attn_forward_kernel(where_ref, tokens, seg_col, seg_row, live, cosine, sine, *refs):
    own, sib = refs[0:4], refs[4:8]
    weights, normed, heads, probs, att, hidden, normed_two, gain_out, gains = refs[8:]
    move_rows(where_ref, own, sib, weights, gains)
    inputs = tokens[...].astype(F32)
    scaled = inputs * inv_rms(inputs)
    gain_attn, gain_mlp = unpack_gains(gains)
    gain_out[...] = jnp.concatenate([gain_attn, gain_mlp, jnp.zeros((6, WIDTH), F32)], axis=0)
    normed[...] = (scaled * gain_attn).astype(BF)
    rows = WIDTH + KV_HEADS * HEAD_DIM
    projected = dot(weights[0:10].reshape(-1, WIDTH), normed[...], NT)
    heads[0:rows] = turn(projected[0:rows], cosine[...], sine[...]).astype(BF)
    heads[rows:] = projected[rows:].astype(BF)
    key_place = lax.broadcasted_iota(jnp.int32, (TOK, TOK), 0)
    query_place = lax.broadcasted_iota(jnp.int32, (TOK, TOK), 1)
    for b in range(MICRO):
        lanes = slice(TOK * b, TOK * (b + 1))
        same = seg_col[lanes, :] == seg_row[b : b + 1, :]
        allowed = jnp.where(same & (key_place <= query_place), 1.0, 0.0)
        allowed = jnp.concatenate([allowed] * GROUP, axis=1)
        for kv in range(KV_HEADS):
            key = heads[WIDTH + HEAD_DIM * kv : WIDTH + HEAD_DIM * (kv + 1), lanes]
            value = heads[rows + HEAD_DIM * kv : rows + HEAD_DIM * (kv + 1), lanes]
            scores = dot(key, heads_of(heads, kv, b), TN) * HEAD_DIM ** (-0.5)
            scores = jnp.where(allowed > 0.5, scores, NEG_FILL)
            expd = jnp.exp(scores - jnp.max(scores, axis=0, keepdims=True))
            prob = expd / jnp.sum(expd, axis=0, keepdims=True)
            probs[b * KV_HEADS + kv] = prob
            attended = dot(value, prob.astype(BF), NN).astype(BF)
            for g in range(GROUP):
                h = GROUP * kv + g
                att[HEAD_DIM * h : HEAD_DIM * (h + 1), lanes] = attended[:, TOK * g : TOK * (g + 1)]
    total_hidden = inputs + live[...] * dot(att[...], weights[10:16].reshape(WIDTH, WIDTH), TN)
    hidden[...] = total_hidden
    normed_two[...] = (total_hidden * inv_rms(total_hidden) * gain_mlp).astype(BF)


def attn_forward(where, tokens, segment_ids, live, cosine, sine, own, sib):
    local = pl.BlockSpec(memory_space=pltpu.VMEM)
    rows = tokens.shape[0]
    qkv_rows = WIDTH + 2 * KV_HEADS * HEAD_DIM
    return pl.pallas_call(
        attn_forward_kernel,
        in_specs=[pl.BlockSpec(memory_space=pltpu.SMEM)] + [local] * 14,
        out_specs=[local] * 8,
        out_shape=[
            jax.ShapeDtypeStruct((16, 2, BLOCK, WIDTH), BF),
            jax.ShapeDtypeStruct((rows, WIDTH), BF),
            jax.ShapeDtypeStruct((qkv_rows, rows), BF),
            jax.ShapeDtypeStruct((MICRO * KV_HEADS, TOK, GROUP * TOK), F32),
            jax.ShapeDtypeStruct((WIDTH, rows), BF),
            jax.ShapeDtypeStruct((rows, WIDTH), F32),
            jax.ShapeDtypeStruct((rows, WIDTH), BF),
            jax.ShapeDtypeStruct((8, WIDTH), F32),
        ],
        scratch_shapes=[pltpu.VMEM((16, 16, WIDTH), BF)],
        compiler_params=pltpu.CompilerParams(vmem_limit_bytes=12 * 2**20),
        name="attn_forward",
    )(where, tokens, segment_ids.reshape(rows, 1), segment_ids, live, cosine, sine, *own, *sib)


def attn_backward_kernel(where_ref, back, back_other, hidden, gains, cot, live, weights, heads, probs, att, normed, cosine, sine,
                         ours, theirs, grad_hidden, grad_proj, gain_grad, raw):
    z, y, c = where_ref[0], where_ref[1], where_ref[2]
    rows = hidden.shape[0]
    grad_normed = back[0:rows] + back_other[...].astype(F32)
    grad, gain_mlp = norm_back(grad_normed, hidden[...], inv_rms(hidden[...]), gains[1:2])
    grad = cot[...].astype(F32) + grad
    grad_hidden[...] = grad
    gain_grad[...] = jnp.concatenate([jnp.zeros((1, WIDTH), F32), gain_mlp, jnp.zeros((6, WIDTH), F32)], axis=0)
    branch = (live[...] * grad).astype(BF)
    grad_att = dot(weights[10:16].reshape(WIDTH, WIDTH), branch, NT).astype(BF)
    base = WIDTH + KV_HEADS * HEAD_DIM
    for b in range(MICRO):
        lanes = slice(TOK * b, TOK * (b + 1))
        for kv in range(KV_HEADS):
            key = heads[WIDTH + HEAD_DIM * kv : WIDTH + HEAD_DIM * (kv + 1), lanes]
            value = heads[base + HEAD_DIM * kv : base + HEAD_DIM * (kv + 1), lanes]
            query, grad_out = heads_of(heads, kv, b), heads_of(grad_att, kv, b)
            prob = probs[b * KV_HEADS + kv]
            grad_prob = dot(value, grad_out, TN)
            delta = jnp.sum(prob * grad_prob, axis=0, keepdims=True)
            grad_score = (HEAD_DIM ** (-0.5) * prob * (grad_prob - delta)).astype(BF)
            grad_query = dot(key, grad_score, NN)
            for g in range(GROUP):
                h = GROUP * kv + g
                raw[HEAD_DIM * h : HEAD_DIM * (h + 1), lanes] = grad_query[:, TOK * g : TOK * (g + 1)]
            raw[WIDTH + HEAD_DIM * kv : WIDTH + HEAD_DIM * (kv + 1), lanes] = dot(query, grad_score, NT)
            raw[base + HEAD_DIM * kv : base + HEAD_DIM * (kv + 1), lanes] = dot(grad_out, prob.astype(BF), NT)
    grad_proj[0:base] = turn(raw[0:base], cosine[...], -sine[...]).astype(BF)
    grad_proj[base:] = raw[base:].astype(BF)

    jobs = [(grad_proj, 0, 640, normed[...]), (grad_proj, 640, 640, normed[...]), (grad_proj, 1280, 320, normed[...])]
    jobs += [(att, 0, 640, branch), (att, 640, 320, branch)]
    row = 0
    for source, start, size, right in jobs:
        block = dot(source[start : start + size], right, NN).astype(BF)
        for k in range(size // 160):
            rz = lax.rem(row // 4 - z + 4, 4)
            ry = lax.rem(row % 4 - y + 4, 4)
            zy, yz = rz * 4 + ry, ry * 4 + rz
            lower = block[160 * k : 160 * k + 80]
            upper = block[160 * k + 80 : 160 * k + 160]

            @pl.when(c == 0)
            def _(lower=lower, upper=upper, zy=zy, yz=yz):
                ours[zy] = lower
                theirs[yz] = upper

            @pl.when(c != 0)
            def _(lower=lower, upper=upper, zy=zy, yz=yz):
                ours[yz] = upper
                theirs[zy] = lower

            row += 1


def attn_backward(where, back, back_other, hidden, gains, cot, live, weights, heads, probs, att, normed, cosine, sine):
    local = pl.BlockSpec(memory_space=pltpu.VMEM)
    return pl.pallas_call(
        attn_backward_kernel,
        in_specs=[pl.BlockSpec(memory_space=pltpu.SMEM)] + [local] * 13,
        out_specs=[local] * 5,
        out_shape=[
            jax.ShapeDtypeStruct((16, BLOCK, WIDTH), BF),
            jax.ShapeDtypeStruct((16, BLOCK, WIDTH), BF),
            jax.ShapeDtypeStruct(hidden.shape, F32),
            jax.ShapeDtypeStruct(heads.shape, BF),
            jax.ShapeDtypeStruct((8, WIDTH), F32),
        ],
        scratch_shapes=[pltpu.VMEM(heads.shape, F32)],
        compiler_params=pltpu.CompilerParams(vmem_limit_bytes=16 * 2**20),
        name="attn_backward",
    )(where, back, back_other, hidden, gains, cot, live, weights, heads, probs, att, normed, cosine, sine)


def attn_inputs_kernel(grad_proj, weights, tokens, gains, grad_hidden, gain_grad, grad_inputs, gain_out):
    inputs = tokens[...].astype(F32)
    grad_normed = dot(grad_proj[...], weights[0:10].reshape(-1, WIDTH), TN)
    grad, gain_attn = norm_back(grad_normed, inputs, inv_rms(inputs), gains[0:1])
    grad_inputs[...] = (grad_hidden[...] + grad).astype(BF)
    gain_out[...] = gain_grad[...] + jnp.concatenate([gain_attn, jnp.zeros((7, WIDTH), F32)], axis=0)


def attn_inputs(grad_proj, weights, tokens, gains, grad_hidden, gain_grad):
    local = pl.BlockSpec(memory_space=pltpu.VMEM)
    return pl.pallas_call(
        attn_inputs_kernel,
        in_specs=[local] * 6,
        out_specs=[local] * 2,
        out_shape=[jax.ShapeDtypeStruct(tokens.shape, BF), jax.ShapeDtypeStruct((8, WIDTH), F32)],
        compiler_params=pltpu.CompilerParams(vmem_limit_bytes=12 * 2**20),
        name="attn_inputs",
    )(grad_proj, weights, tokens, gains, grad_hidden, gain_grad)


def x_payloads_kernel(where_ref, own, got_a, got_b, got_c, gains, kept, sent, blocks):
    rows = 4 * BLOCK
    mine = own[0:rows].astype(F32)
    gain = gains[...]
    for part in (got_a, got_b, got_c):
        mine = mine + part[0:rows].astype(F32)
        gain = gain + part[rows : rows + 2].astype(F32)
    for j in range(4):
        blocks[j, 0:20] = mine[3 * BLOCK + 20 * j : 3 * BLOCK + 20 * j + 20]
    for r in range(4):
        pieces = [mine[BLOCK * w + 20 * r : BLOCK * w + 20 * r + 20] for w in range(3)]
        pieces += [blocks[lax.rem(where_ref[0] + r, 4)][0:20], gain, jnp.zeros((14, WIDTH), F32)]
        block = jnp.concatenate(pieces, axis=0)
        if r == 0:
            kept[...] = block
        else:
            sent[r - 1] = block.astype(BF)


def x_payloads(where, own, got, gains):
    local = pl.BlockSpec(memory_space=pltpu.VMEM)
    return pl.pallas_call(
        x_payloads_kernel,
        in_specs=[pl.BlockSpec(memory_space=pltpu.SMEM)] + [local] * 5,
        out_specs=[local] * 2,
        out_shape=[jax.ShapeDtypeStruct((96, WIDTH), F32), jax.ShapeDtypeStruct((3, 96, WIDTH), BF)],
        scratch_shapes=[pltpu.VMEM((4, 24, WIDTH), F32)],
        compiler_params=pltpu.CompilerParams(vmem_limit_bytes=12 * 2**20),
        name="x_payloads",
    )(where, own, *got, gains)


def ffn_kernel(count, first, normed, cot, *refs):
    chunks, refs = refs[:count], refs[count:]
    if first:
        branch, back = 0.0, 0.0
    else:
        branch, back = refs[0][...], refs[1][...]
        refs = refs[2:]
    grads, branch_out, back_out = refs[:count], refs[count], refs[count + 1]
    for chunk, grad in zip(chunks, grads):
        parts = chunk.shape[1]
        half = parts * BLOCK
        pair = chunk[0:2].reshape(2 * half, WIDTH)
        down = chunk[2].reshape(half, WIDTH)
        both = dot(pair, normed[...], NT)
        grad_prod = dot(down, cot[...], NT)
        gate, up = both[:half], both[half:]
        sigma = 1.0 / (1.0 + jnp.exp(-gate))
        gated = gate * sigma
        product = (gated * up).astype(BF)
        grad_gate = (grad_prod * up * sigma * (1.0 + gate * (1.0 - sigma))).astype(BF)
        grad_up = (grad_prod * gated).astype(BF)
        grad_pair = jnp.concatenate([grad_gate, grad_up], axis=0)
        back = back + dot(grad_pair, pair, TN)
        grad[0:2] = dot(grad_pair, normed[...], NN).astype(BF).reshape(2, parts, BLOCK, WIDTH)
        grad[2] = dot(product, cot[...], NN).astype(BF).reshape(parts, BLOCK, WIDTH)
        branch = branch + dot(product, down, TN)
    branch_out[...] = branch
    back_out[...] = back


def ffn(normed, cot, chunks, sums):
    local = pl.BlockSpec(memory_space=pltpu.VMEM)
    count, tokens = len(chunks), normed.shape[0]
    sums = list(sums)
    held = len(sums)
    units = sum(chunk.shape[1] for chunk in chunks) * BLOCK
    out = pl.pallas_call(
        lambda *refs: ffn_kernel(count, held == 0, *refs),
        in_specs=[local] * (2 + count + held),
        out_specs=[local] * (count + 2),
        out_shape=[jax.ShapeDtypeStruct(chunk.shape, BF) for chunk in chunks]
        + [jax.ShapeDtypeStruct((tokens, WIDTH), F32)] * 2,
        input_output_aliases={2 + count + i: count + i for i in range(held)},
        compiler_params=pltpu.CompilerParams(vmem_limit_bytes=16 * 2**20),
        cost_estimate=pl.CostEstimate(
            flops=18 * tokens * units * WIDTH,
            transcendentals=tokens * units,
            bytes_accessed=12 * units * WIDTH,
        ),
        name="ffn_chunks",
    )(normed, cot, *chunks, *sums)
    return out[:count], out[count:]


def rope_tables(seg):
    places = jnp.arange(TOK)
    allowed = (seg[:, :, None] == seg[:, None, :]) & (places[None, :] <= places[:, None])
    position = jnp.sum(allowed.astype(F32), axis=-1) - 1.0
    freqs = THETA ** (-2.0 * jnp.arange(HEAD_DIM // 2).astype(F32) / HEAD_DIM)
    angles = freqs[:, None] * position.reshape(1, -1)
    return jnp.cos(angles), jnp.sin(angles)


def inv_rms(values):
    return lax.rsqrt(jnp.mean(values * values, axis=-1, keepdims=True) + EPS)


def norm_back(grad_normed, source, inverse, gain_vec):
    scaled = source * inverse
    grad_scaled = grad_normed * gain_vec
    grad_gain = jnp.sum(grad_normed * scaled, axis=0, keepdims=True)
    mean = jnp.mean(grad_scaled * scaled, axis=-1, keepdims=True)
    return inverse * (grad_scaled - scaled * mean), grad_gain


def dot(left, right, dims):
    return lax.dot_general(left, right, (dims, ((), ())), preferred_element_type=F32)


NT = ((1,), (1,))
NN = ((1,), (0,))
TN = ((0,), (0,))


def total(parts):
    out = parts[0].astype(F32)
    for part in parts[1:]:
        out = out + part.astype(F32)
    return out


def body(tokens, segment_ids, attn_weight, gate_up, down_weight, norm_gains, cotangent):
    z, y, x, c = (lax.axis_index(a) for a in AXES)
    rows = MICRO * TOK

    gain_row = jnp.pad(norm_gains[None, :], ((0, 15), (0, WIDTH - 15)))
    shard = jnp.concatenate([attn_weight, gate_up[0], gate_up[1], down_weight, gain_row], axis=0)
    near = jnp.stack(fetch_ordered(shard, shift_x))
    ffn_block = near[:, 20:80].reshape(4, 3, 20, WIDTH).transpose(1, 0, 2, 3).reshape(3, BLOCK, WIDTH)
    head = jnp.concatenate([near[:, :20], near[:, 80:81]], axis=1)
    head = lax.dynamic_slice_in_dim(jnp.concatenate([head, head], axis=0), lax.rem(4 - x, 4), 4, axis=0)
    other = permute(head, shift_core())
    both = jnp.stack([jnp.where(c == 0, head, other), jnp.where(c == 0, other, head)], axis=1)
    attn_half = lax.dynamic_slice_in_dim(both[:, :, :20].reshape(2 * BLOCK, WIDTH), c * BLOCK, BLOCK, axis=0)
    gain_near = jnp.pad(both[:, :, 20, :15].reshape(1, 120), ((0, 15), (0, WIDTH - 120)))
    attn_block = jnp.concatenate([attn_half, gain_near], axis=0)

    block = jnp.concatenate([attn_block, ffn_block.reshape(3 * BLOCK, WIDTH)], axis=0)
    got = fetch_ordered(block, lambda s: shift_plane(s, True))
    attn_one = jnp.stack([part[:96] for part in got])
    ffn_one = jnp.stack([part[96:].reshape(3, BLOCK, WIDTH) for part in got], axis=1)
    own = fetch_ordered(attn_one, lambda s: shift_plane(s, False))
    sib = [permute(v, shift_core()) for v in own]
    where = jnp.stack([z, y, c]).astype(jnp.int32)

    ffn_send, _ = lax.optimization_barrier((ffn_one, own))
    ffn_next = permute(ffn_send, shift_plane(-1, False))
    ffn_last = permute(ffn_send, shift_plane(-3, False))

    live = (segment_ids.reshape(rows, 1) < TOK).astype(F32)
    cot = cotangent.reshape(rows, WIDTH)
    grad_mlp = (live * cot.astype(F32)).astype(BF)
    grad_mlp_all = jnp.concatenate([grad_mlp, permute(grad_mlp, shift_core())], axis=0)
    cosine, sine = rope_tables(segment_ids)
    flat_tokens = tokens.reshape(rows, WIDTH)
    weights, normed_one, heads, probs, att, hidden, normed_two, gains = attn_forward(
        where, flat_tokens, segment_ids, live, cosine, sine, own, sib
    )
    ffn_next, ffn_last, _ = lax.optimization_barrier((ffn_next, ffn_last, normed_two))
    far_low = permute(ffn_next[:, :2], shift_plane(-1, False))
    far_high = permute(ffn_last[:, 2:], shift_plane(1, False))
    far_low, far_high = lax.optimization_barrier((far_low, far_high))

    normed_all = jnp.concatenate([normed_two, permute(normed_two, shift_core())], axis=0)
    (grad_zero,), sums = ffn(normed_all, grad_mlp_all, [ffn_one], [])
    (grad_next, grad_last), sums = ffn(normed_all, grad_mlp_all, [ffn_next, ffn_last], sums)
    (grad_low,), sums = ffn(normed_all, grad_mlp_all, [far_low], sums)
    (grad_high,), (branch, grad_normed) = ffn(normed_all, grad_mlp_all, [far_high], sums)
    back_other = permute(grad_normed[rows:].astype(BF), shift_core())
    branch = branch[:rows] + permute(branch[rows:].astype(BF), shift_core()).astype(F32)
    result = (hidden + live * branch).astype(BF)

    ours, theirs, grad_hidden, grad_proj, gain_grads = attn_backward(
        where, grad_normed, back_other, hidden, gains, cot, live, weights, heads, probs, att, normed_one, cosine, sine
    )
    ffn_next_got = permute(grad_next, shift_plane(1, False))
    ffn_last_got = permute(grad_last, shift_plane(3, False))
    far_low_got = permute(grad_low, shift_plane(2, False))
    far_high_got = permute(grad_high, shift_plane(2, False))
    theirs, ffn_next_got, ffn_last_got, far_low_got = lax.optimization_barrier(
        (theirs, ffn_next_got, ffn_last_got, far_low_got)
    )
    swapped = permute(theirs, shift_core())
    grad_inputs, gain_grads = attn_inputs(grad_proj, weights, flat_tokens, gains, grad_hidden, gain_grads)
    gain_grads = gain_grads[:2]

    def exchange(blocks, gain_grads, make):
        count = blocks.shape[1]
        low = jnp.pad(gain_grads.astype(BF), ((0, 14), (0, 0)))
        got = [permute(jnp.concatenate([blocks[r], low], axis=0), make(r)) for r in (1, 3, 2)]
        blocks = total([blocks[0]] + [part[:count] for part in got])
        return blocks, total([gain_grads] + [part[count : count + 2] for part in got])

    attn_mine = total([ours, swapped]).astype(BF).reshape(4, 4 * BLOCK, WIDTH)
    attn_mine, far_high_got = lax.optimization_barrier((attn_mine, far_high_got))
    attn_next, gain_grads = exchange(attn_mine, gain_grads, lambda r: shift_plane(r, False))
    nearer = [grad_zero, ffn_next_got, ffn_last_got]
    low_mine = total([part[:, :2] for part in nearer] + [far_low_got]).astype(BF)
    high_mine = total([part[:, 2:] for part in nearer] + [far_high_got]).astype(BF)
    attn_next = attn_next.astype(BF).reshape(4, BLOCK, WIDTH)
    low_gains = jnp.pad(gain_grads.astype(BF), ((0, 14), (0, 0)))

    def rows_for(r):
        ffn_rows = (low_mine if r < 2 else high_mine)[:, r % 2].reshape(3 * BLOCK, WIDTH)
        return jnp.concatenate([ffn_rows, attn_next[r], low_gains], axis=0)

    got = [permute(rows_for(r), shift_plane(r, True)) for r in (1, 3, 2)]
    kept, sent = x_payloads(jnp.stack([x, x, x]).astype(jnp.int32), rows_for(0), got, gain_grads)
    got = [permute(sent[r - 1], shift_x(r)) for r in (1, 3, 2)]
    mine = total([kept] + got)
    ffn_owned = mine[:60].reshape(3, 20, WIDTH)
    attn_owned = permute(mine[60:80], to_owner())
    gain_grads = mine[80:82]
    gain_grads = gain_grads + permute(gain_grads, shift_core())
    gain_owned = lax.dynamic_slice_in_dim(gain_grads.reshape(2 * WIDTH), flat_index(z, y, x, c) * 15, 15)
    return (
        result.reshape(MICRO, TOK, WIDTH),
        grad_inputs.reshape(MICRO, TOK, WIDTH),
        attn_owned,
        ffn_owned[:2],
        ffn_owned[2],
        gain_owned,
    )


def flat_index(z, y, x, c):
    return ((z * 4 + y) * 4 + x) * 2 + c


def solution(mesh):
    grid = Mesh(mesh.devices.reshape(4, 4, 4, 2), AXES)
    return jax.shard_map(
        body,
        mesh=grid,
        in_specs=(
            P(None, AXES, None),
            P(None, AXES),
            P(AXES, None),
            P(None, AXES, None),
            P(AXES, None),
            P(AXES),
            P(None, AXES, None),
        ),
        out_specs=(
            P(None, AXES, None),
            P(None, AXES, None),
            P(AXES, None),
            P(None, AXES, None),
            P(AXES, None),
            P(AXES),
        ),
        check_vma=False,
    )
```

```python
import jax
import jax.numpy as jnp
from jax import lax
from jax.experimental import pallas as pl
from jax.experimental.pallas import tpu as pltpu
from jax.sharding import Mesh, PartitionSpec as P

HEADS = 15
KV_HEADS = 5
GROUP = HEADS // KV_HEADS
HEAD_DIM = 64
MICRO = 2
WIDTH = 960
TOK = 128
BLOCK = 80
EPS = 1e-05
THETA = 100000.0
NEG_FILL = -1e30
AXES = ("z", "y", "x", "c")
BF = jnp.bfloat16
F32 = jnp.float32


def flat(z, y, x, c):
    return (((z % 4) * 4 + y % 4) * 4 + x % 4) * 2 + c % 2


def everywhere():
    return [(z, y, x, c) for z in range(4) for y in range(4) for x in range(4) for c in range(2)]


def shift_x(step):
    return [(flat(*d), flat(d[0], d[1], d[2] + step, d[3])) for d in everywhere()]


def shift_core():
    return [(flat(*d), flat(d[0], d[1], d[2], d[3] + 1)) for d in everywhere()]


def shift_plane(step, inner):
    pairs = []
    for z, y, x, c in everywhere():
        along_y = (c == 0) == inner
        pairs.append((flat(z, y, x, c), flat(z, y + step, x, c) if along_y else flat(z + step, y, x, c)))
    return pairs


def to_owner():
    return [(flat(z, y, j, c), flat(z, y, 2 * c + j // 2, j % 2)) for z, y, j, c in everywhere()]


def permute(value, pairs):
    return lax.ppermute(value, AXES, pairs)


def fetch(value, make):
    return [value] + [permute(value, make(-r)) for r in (1, 3, 2)]


def fetch_ordered(value, make):
    got = fetch(value, make)
    return [got[0], got[1], got[3], got[2]]


def move_rows(where_ref, own, sib, weights, gains):
    z, y, c = where_ref[0], where_ref[1], where_ref[2]
    for r2 in range(4):
        for r1 in range(4):
            for which, group in enumerate((own, sib)):
                core = c if which == 0 else 1 - c
                rz = jnp.where(core == 0, r2, r1)
                ry = jnp.where(core == 0, r1, r2)
                row = lax.rem(z + rz, 4) * 4 + lax.rem(y + ry, 4)
                weights[row, core] = group[r2][r1, 0:BLOCK]
                if which == 0:
                    gains[row] = group[r2][r1, BLOCK : BLOCK + 16]


def unpack_gains(gains):
    raw = gains[:, 0, 0:128].astype(BF)
    lane = lax.broadcasted_iota(jnp.int32, (128, WIDTH), 1)
    entry = lax.broadcasted_iota(jnp.int32, (128, WIDTH), 0)
    pick = jnp.where(lane - ((lane * 8739) >> 20) * 120 == entry, 1.0, 0.0).astype(BF)
    spread = dot(raw, pick, NN)
    lane = lax.broadcasted_iota(jnp.int32, (16, WIDTH), 1)
    row = lax.broadcasted_iota(jnp.int32, (16, WIDTH), 0)
    block = (lane * 8739) >> 20
    attn = jnp.sum(jnp.where(row == block, spread, 0.0), axis=0, keepdims=True)
    mlp = jnp.sum(jnp.where(row == block + 8, spread, 0.0), axis=0, keepdims=True)
    return attn, mlp


def heads_of(ref, kv, b):
    lanes = slice(TOK * b, TOK * (b + 1))
    parts = [ref[HEAD_DIM * h : HEAD_DIM * (h + 1), lanes] for h in range(GROUP * kv, GROUP * (kv + 1))]
    return jnp.concatenate(parts, axis=1)


def turn(values, cosine, sine):
    split = values.reshape(-1, 2, HEAD_DIM // 2, values.shape[-1])
    former, latter = split[:, 0], split[:, 1]
    turned = jnp.stack([former * cosine - latter * sine, latter * cosine + former * sine], axis=1)
    return turned.reshape(values.shape)


def attn_forward_kernel(where_ref, tokens, seg_col, seg_row, live, cosine, sine, *refs):
    own, sib = refs[0:4], refs[4:8]
    weights, normed, heads, probs, att, hidden, normed_two, gain_out, gains = refs[8:]
    move_rows(where_ref, own, sib, weights, gains)
    inputs = tokens[...].astype(F32)
    scaled = inputs * inv_rms(inputs)
    gain_attn, gain_mlp = unpack_gains(gains)
    gain_out[...] = jnp.concatenate([gain_attn, gain_mlp, jnp.zeros((6, WIDTH), F32)], axis=0)
    normed[...] = (scaled * gain_attn).astype(BF)
    rows = WIDTH + KV_HEADS * HEAD_DIM
    projected = dot(weights[0:10].reshape(-1, WIDTH), normed[...], NT)
    heads[0:rows] = turn(projected[0:rows], cosine[...], sine[...]).astype(BF)
    heads[rows:] = projected[rows:].astype(BF)
    key_place = lax.broadcasted_iota(jnp.int32, (TOK, TOK), 0)
    query_place = lax.broadcasted_iota(jnp.int32, (TOK, TOK), 1)
    for b in range(MICRO):
        lanes = slice(TOK * b, TOK * (b + 1))
        same = seg_col[lanes, :] == seg_row[b : b + 1, :]
        allowed = jnp.where(same & (key_place <= query_place), 1.0, 0.0)
        allowed = jnp.concatenate([allowed] * GROUP, axis=1)
        for kv in range(KV_HEADS):
            key = heads[WIDTH + HEAD_DIM * kv : WIDTH + HEAD_DIM * (kv + 1), lanes]
            value = heads[rows + HEAD_DIM * kv : rows + HEAD_DIM * (kv + 1), lanes]
            scores = dot(key, heads_of(heads, kv, b), TN) * HEAD_DIM ** (-0.5)
            scores = jnp.where(allowed > 0.5, scores, NEG_FILL)
            expd = jnp.exp(scores - jnp.max(scores, axis=0, keepdims=True))
            prob = expd / jnp.sum(expd, axis=0, keepdims=True)
            probs[b * KV_HEADS + kv] = prob
            attended = dot(value, prob.astype(BF), NN).astype(BF)
            for g in range(GROUP):
                h = GROUP * kv + g
                att[HEAD_DIM * h : HEAD_DIM * (h + 1), lanes] = attended[:, TOK * g : TOK * (g + 1)]
    total_hidden = inputs + live[...] * dot(att[...], weights[10:16].reshape(WIDTH, WIDTH), TN)
    hidden[...] = total_hidden
    normed_two[...] = (total_hidden * inv_rms(total_hidden) * gain_mlp).astype(BF)


def attn_forward(where, tokens, segment_ids, live, cosine, sine, own, sib):
    local = pl.BlockSpec(memory_space=pltpu.VMEM)
    rows = tokens.shape[0]
    qkv_rows = WIDTH + 2 * KV_HEADS * HEAD_DIM
    return pl.pallas_call(
        attn_forward_kernel,
        in_specs=[pl.BlockSpec(memory_space=pltpu.SMEM)] + [local] * 14,
        out_specs=[local] * 8,
        out_shape=[
            jax.ShapeDtypeStruct((16, 2, BLOCK, WIDTH), BF),
            jax.ShapeDtypeStruct((rows, WIDTH), BF),
            jax.ShapeDtypeStruct((qkv_rows, rows), BF),
            jax.ShapeDtypeStruct((MICRO * KV_HEADS, TOK, GROUP * TOK), F32),
            jax.ShapeDtypeStruct((WIDTH, rows), BF),
            jax.ShapeDtypeStruct((rows, WIDTH), F32),
            jax.ShapeDtypeStruct((rows, WIDTH), BF),
            jax.ShapeDtypeStruct((8, WIDTH), F32),
        ],
        scratch_shapes=[pltpu.VMEM((16, 16, WIDTH), BF)],
        compiler_params=pltpu.CompilerParams(vmem_limit_bytes=12 * 2**20),
        name="attn_forward",
    )(where, tokens, segment_ids.reshape(rows, 1), segment_ids, live, cosine, sine, *own, *sib)


def attn_backward_kernel(where_ref, back, back_other, hidden, gains, cot, live, weights, heads, probs, att, normed, cosine, sine,
                         ours, theirs, grad_hidden, grad_proj, gain_grad, raw):
    z, y, c = where_ref[0], where_ref[1], where_ref[2]
    rows = hidden.shape[0]
    grad_normed = back[0:rows] + back_other[...].astype(F32)
    grad, gain_mlp = norm_back(grad_normed, hidden[...], inv_rms(hidden[...]), gains[1:2])
    grad = cot[...].astype(F32) + grad
    grad_hidden[...] = grad
    gain_grad[...] = jnp.concatenate([jnp.zeros((1, WIDTH), F32), gain_mlp, jnp.zeros((6, WIDTH), F32)], axis=0)
    branch = (live[...] * grad).astype(BF)
    grad_att = dot(weights[10:16].reshape(WIDTH, WIDTH), branch, NT).astype(BF)
    base = WIDTH + KV_HEADS * HEAD_DIM
    for b in range(MICRO):
        lanes = slice(TOK * b, TOK * (b + 1))
        for kv in range(KV_HEADS):
            key = heads[WIDTH + HEAD_DIM * kv : WIDTH + HEAD_DIM * (kv + 1), lanes]
            value = heads[base + HEAD_DIM * kv : base + HEAD_DIM * (kv + 1), lanes]
            query, grad_out = heads_of(heads, kv, b), heads_of(grad_att, kv, b)
            prob = probs[b * KV_HEADS + kv]
            grad_prob = dot(value, grad_out, TN)
            delta = jnp.sum(prob * grad_prob, axis=0, keepdims=True)
            grad_score = (HEAD_DIM ** (-0.5) * prob * (grad_prob - delta)).astype(BF)
            grad_query = dot(key, grad_score, NN)
            for g in range(GROUP):
                h = GROUP * kv + g
                raw[HEAD_DIM * h : HEAD_DIM * (h + 1), lanes] = grad_query[:, TOK * g : TOK * (g + 1)]
            raw[WIDTH + HEAD_DIM * kv : WIDTH + HEAD_DIM * (kv + 1), lanes] = dot(query, grad_score, NT)
            raw[base + HEAD_DIM * kv : base + HEAD_DIM * (kv + 1), lanes] = dot(grad_out, prob.astype(BF), NT)
    grad_proj[0:base] = turn(raw[0:base], cosine[...], -sine[...]).astype(BF)
    grad_proj[base:] = raw[base:].astype(BF)

    jobs = [(grad_proj, 0, 640, normed[...]), (grad_proj, 640, 640, normed[...]), (grad_proj, 1280, 320, normed[...])]
    jobs += [(att, 0, 640, branch), (att, 640, 320, branch)]
    row = 0
    for source, start, size, right in jobs:
        block = dot(source[start : start + size], right, NN).astype(BF)
        for k in range(size // 160):
            rz = lax.rem(row // 4 - z + 4, 4)
            ry = lax.rem(row % 4 - y + 4, 4)
            zy, yz = rz * 4 + ry, ry * 4 + rz
            lower = block[160 * k : 160 * k + 80]
            upper = block[160 * k + 80 : 160 * k + 160]

            @pl.when(c == 0)
            def _(lower=lower, upper=upper, zy=zy, yz=yz):
                ours[zy] = lower
                theirs[yz] = upper

            @pl.when(c != 0)
            def _(lower=lower, upper=upper, zy=zy, yz=yz):
                ours[yz] = upper
                theirs[zy] = lower

            row += 1


def attn_backward(where, back, back_other, hidden, gains, cot, live, weights, heads, probs, att, normed, cosine, sine):
    local = pl.BlockSpec(memory_space=pltpu.VMEM)
    return pl.pallas_call(
        attn_backward_kernel,
        in_specs=[pl.BlockSpec(memory_space=pltpu.SMEM)] + [local] * 13,
        out_specs=[local] * 5,
        out_shape=[
            jax.ShapeDtypeStruct((16, BLOCK, WIDTH), BF),
            jax.ShapeDtypeStruct((16, BLOCK, WIDTH), BF),
            jax.ShapeDtypeStruct(hidden.shape, F32),
            jax.ShapeDtypeStruct(heads.shape, BF),
            jax.ShapeDtypeStruct((8, WIDTH), F32),
        ],
        scratch_shapes=[pltpu.VMEM(heads.shape, F32)],
        compiler_params=pltpu.CompilerParams(vmem_limit_bytes=16 * 2**20),
        name="attn_backward",
    )(where, back, back_other, hidden, gains, cot, live, weights, heads, probs, att, normed, cosine, sine)


def attn_inputs_kernel(grad_proj, weights, tokens, gains, grad_hidden, gain_grad, grad_inputs, gain_out):
    inputs = tokens[...].astype(F32)
    grad_normed = dot(grad_proj[...], weights[0:10].reshape(-1, WIDTH), TN)
    grad, gain_attn = norm_back(grad_normed, inputs, inv_rms(inputs), gains[0:1])
    grad_inputs[...] = (grad_hidden[...] + grad).astype(BF)
    gain_out[...] = gain_grad[...] + jnp.concatenate([gain_attn, jnp.zeros((7, WIDTH), F32)], axis=0)


def attn_inputs(grad_proj, weights, tokens, gains, grad_hidden, gain_grad):
    local = pl.BlockSpec(memory_space=pltpu.VMEM)
    return pl.pallas_call(
        attn_inputs_kernel,
        in_specs=[local] * 6,
        out_specs=[local] * 2,
        out_shape=[jax.ShapeDtypeStruct(tokens.shape, BF), jax.ShapeDtypeStruct((8, WIDTH), F32)],
        compiler_params=pltpu.CompilerParams(vmem_limit_bytes=12 * 2**20),
        name="attn_inputs",
    )(grad_proj, weights, tokens, gains, grad_hidden, gain_grad)


def x_payloads_kernel(where_ref, own, got_a, got_b, got_c, gains, kept, sent_a, sent_b, sent_c, blocks):
    rows = 4 * BLOCK
    mine = own[0:rows].astype(F32)
    gain = gains[...]
    for part in (got_a, got_b, got_c):
        mine = mine + part[0:rows].astype(F32)
        gain = gain + part[rows : rows + 2].astype(F32)
    for j in range(4):
        blocks[j, 0:20] = mine[3 * BLOCK + 20 * j : 3 * BLOCK + 20 * j + 20]
    for r in range(4):
        pieces = [mine[BLOCK * w + 20 * r : BLOCK * w + 20 * r + 20] for w in range(3)]
        pieces += [blocks[lax.rem(where_ref[0] + r, 4)][0:20], gain]
        block = jnp.concatenate(pieces, axis=0)
        if r == 0:
            kept[...] = block
        else:
            (sent_a, sent_b, sent_c)[r - 1][...] = block.astype(BF)


def x_payloads(where, own, got, gains):
    local = pl.BlockSpec(memory_space=pltpu.VMEM)
    return pl.pallas_call(
        x_payloads_kernel,
        in_specs=[pl.BlockSpec(memory_space=pltpu.SMEM)] + [local] * 5,
        out_specs=[local] * 4,
        out_shape=[jax.ShapeDtypeStruct((82, WIDTH), F32)] + [jax.ShapeDtypeStruct((82, WIDTH), BF)] * 3,
        scratch_shapes=[pltpu.VMEM((4, 24, WIDTH), F32)],
        compiler_params=pltpu.CompilerParams(vmem_limit_bytes=12 * 2**20),
        name="x_payloads",
    )(where, own, *got, gains)


def ffn_kernel(count, first, normed, cot, *refs):
    chunks, refs = refs[:count], refs[count:]
    if first:
        branch, back = 0.0, 0.0
    else:
        branch, back = refs[0][...], refs[1][...]
        refs = refs[2:]
    grads, branch_out, back_out = refs[:count], refs[count], refs[count + 1]
    for chunk, grad in zip(chunks, grads):
        parts = chunk.shape[1]
        half = parts * BLOCK
        pair = chunk[0:2].reshape(2 * half, WIDTH)
        down = chunk[2].reshape(half, WIDTH)
        both = dot(pair, normed[...], NT)
        grad_prod = dot(down, cot[...], NT)
        gate, up = both[:half], both[half:]
        sigma = 1.0 / (1.0 + jnp.exp(-gate))
        gated = gate * sigma
        product = (gated * up).astype(BF)
        grad_gate = (grad_prod * up * sigma * (1.0 + gate * (1.0 - sigma))).astype(BF)
        grad_up = (grad_prod * gated).astype(BF)
        grad_pair = jnp.concatenate([grad_gate, grad_up], axis=0)
        back = back + dot(grad_pair, pair, TN)
        grad[0:2] = dot(grad_pair, normed[...], NN).astype(BF).reshape(2, parts, BLOCK, WIDTH)
        grad[2] = dot(product, cot[...], NN).astype(BF).reshape(parts, BLOCK, WIDTH)
        branch = branch + dot(product, down, TN)
    branch_out[...] = branch
    back_out[...] = back


def ffn(normed, cot, chunks, sums):
    local = pl.BlockSpec(memory_space=pltpu.VMEM)
    count, tokens = len(chunks), normed.shape[0]
    sums = list(sums)
    held = len(sums)
    units = sum(chunk.shape[1] for chunk in chunks) * BLOCK
    out = pl.pallas_call(
        lambda *refs: ffn_kernel(count, held == 0, *refs),
        in_specs=[local] * (2 + count + held),
        out_specs=[local] * (count + 2),
        out_shape=[jax.ShapeDtypeStruct(chunk.shape, BF) for chunk in chunks]
        + [jax.ShapeDtypeStruct((tokens, WIDTH), F32)] * 2,
        input_output_aliases={2 + count + i: count + i for i in range(held)},
        compiler_params=pltpu.CompilerParams(vmem_limit_bytes=16 * 2**20),
        cost_estimate=pl.CostEstimate(
            flops=18 * tokens * units * WIDTH,
            transcendentals=tokens * units,
            bytes_accessed=12 * units * WIDTH,
        ),
        name="ffn_chunks",
    )(normed, cot, *chunks, *sums)
    return out[:count], out[count:]


def rope_tables(seg):
    places = jnp.arange(TOK)
    allowed = (seg[:, :, None] == seg[:, None, :]) & (places[None, :] <= places[:, None])
    position = jnp.sum(allowed.astype(F32), axis=-1) - 1.0
    freqs = THETA ** (-2.0 * jnp.arange(HEAD_DIM // 2).astype(F32) / HEAD_DIM)
    angles = freqs[:, None] * position.reshape(1, -1)
    return jnp.cos(angles), jnp.sin(angles)


def inv_rms(values):
    return lax.rsqrt(jnp.mean(values * values, axis=-1, keepdims=True) + EPS)


def norm_back(grad_normed, source, inverse, gain_vec):
    scaled = source * inverse
    grad_scaled = grad_normed * gain_vec
    grad_gain = jnp.sum(grad_normed * scaled, axis=0, keepdims=True)
    mean = jnp.mean(grad_scaled * scaled, axis=-1, keepdims=True)
    return inverse * (grad_scaled - scaled * mean), grad_gain


def dot(left, right, dims):
    return lax.dot_general(left, right, (dims, ((), ())), preferred_element_type=F32)


NT = ((1,), (1,))
NN = ((1,), (0,))
TN = ((0,), (0,))


def total(parts):
    out = parts[0].astype(F32)
    for part in parts[1:]:
        out = out + part.astype(F32)
    return out


def body(tokens, segment_ids, attn_weight, gate_up, down_weight, norm_gains, cotangent):
    z, y, x, c = (lax.axis_index(a) for a in AXES)
    rows = MICRO * TOK

    gain_row = jnp.pad(norm_gains[None, :], ((0, 11), (0, WIDTH - 15)))
    near = fetch_ordered(jnp.concatenate([attn_weight, gain_row], axis=0), shift_x)
    ffn_near, near = lax.optimization_barrier((jnp.concatenate([gate_up[0], gate_up[1], down_weight], axis=0), near))
    near = jnp.stack(near)
    head = lax.dynamic_slice_in_dim(jnp.concatenate([near, near], axis=0), lax.rem(4 - x, 4), 4, axis=0)
    other = permute(head, shift_core())
    both = jnp.stack([jnp.where(c == 0, head, other), jnp.where(c == 0, other, head)], axis=1)
    attn_half = lax.dynamic_slice_in_dim(both[:, :, :20].reshape(2 * BLOCK, WIDTH), c * BLOCK, BLOCK, axis=0)
    gain_near = jnp.pad(both[:, :, 20, :15].reshape(1, 120), ((0, 15), (0, WIDTH - 120)))
    attn_block = jnp.concatenate([attn_half, gain_near], axis=0)
    ffn_near = jnp.stack(fetch_ordered(ffn_near, shift_x))
    ffn_block = ffn_near.reshape(4, 3, 20, WIDTH).transpose(1, 0, 2, 3).reshape(3, BLOCK, WIDTH)

    attn_one = fetch_ordered(attn_block, lambda s: shift_plane(s, True))
    attn_one, ffn_block = lax.optimization_barrier((jnp.stack(attn_one), ffn_block))
    own = fetch_ordered(attn_one, lambda s: shift_plane(s, False))
    ffn_block, own[1] = lax.optimization_barrier((ffn_block, own[1]))
    sib = [permute(v, shift_core()) for v in own]
    ffn_one, _ = lax.optimization_barrier((fetch_ordered(ffn_block, lambda s: shift_plane(s, True)), sib))
    ffn_one = jnp.stack(ffn_one, axis=1)
    where = jnp.stack([z, y, c]).astype(jnp.int32)

    ffn_next = permute(ffn_one, shift_plane(-1, False))
    ffn_last = permute(ffn_one, shift_plane(-3, False))

    live = (segment_ids.reshape(rows, 1) < TOK).astype(F32)
    cot = cotangent.reshape(rows, WIDTH)
    grad_mlp = (live * cot.astype(F32)).astype(BF)
    grad_mlp_all = jnp.concatenate([grad_mlp, permute(grad_mlp, shift_core())], axis=0)
    cosine, sine = rope_tables(segment_ids)
    flat_tokens = tokens.reshape(rows, WIDTH)
    weights, normed_one, heads, probs, att, hidden, normed_two, gains = attn_forward(
        where, flat_tokens, segment_ids, live, cosine, sine, own, sib
    )

    normed_all = jnp.concatenate([normed_two, permute(normed_two, shift_core())], axis=0)
    (grad_zero,), sums = ffn(normed_all, grad_mlp_all, [ffn_one], [])
    ffn_next, ffn_last, _ = lax.optimization_barrier((ffn_next, ffn_last, sums[0]))
    far_low = permute(ffn_next[:, :2], shift_plane(-1, False))
    far_high = permute(ffn_last[:, 2:], shift_plane(1, False))
    far_low, far_high = lax.optimization_barrier((far_low, far_high))
    (grad_next, grad_last), sums = ffn(normed_all, grad_mlp_all, [ffn_next, ffn_last], sums)
    grad_next, grad_last, far_low, far_high = lax.optimization_barrier((grad_next, grad_last, far_low, far_high))
    (grad_low,), sums = ffn(normed_all, grad_mlp_all, [far_low], sums)
    (grad_high,), (branch, grad_normed) = ffn(normed_all, grad_mlp_all, [far_high], sums)
    back_other = permute(grad_normed[rows:].astype(BF), shift_core())
    branch = branch[:rows] + permute(branch[rows:].astype(BF), shift_core()).astype(F32)
    result = (hidden + live * branch).astype(BF)

    ours, theirs, grad_hidden, grad_proj, gain_grads = attn_backward(
        where, grad_normed, back_other, hidden, gains, cot, live, weights, heads, probs, att, normed_one, cosine, sine
    )
    ffn_next_got = permute(grad_next, shift_plane(1, False))
    ffn_last_got = permute(grad_last, shift_plane(3, False))
    far_low_got = permute(grad_low, shift_plane(2, False))
    far_high_got = permute(grad_high, shift_plane(2, False))
    theirs, ffn_next_got, ffn_last_got = lax.optimization_barrier((theirs, ffn_next_got, ffn_last_got))
    swapped = permute(theirs, shift_core())
    grad_inputs, gain_grads = attn_inputs(grad_proj, weights, flat_tokens, gains, grad_hidden, gain_grads)
    gain_grads = gain_grads[:2]

    def exchange(blocks, gain_grads, make):
        count = blocks.shape[1]
        low = jnp.pad(gain_grads.astype(BF), ((0, 14), (0, 0)))
        got = [permute(jnp.concatenate([blocks[r], low], axis=0), make(r)) for r in (1, 3, 2)]
        blocks = total([blocks[0]] + [part[:count] for part in got])
        return blocks, total([gain_grads] + [part[count : count + 2] for part in got])

    attn_mine = total([ours, swapped]).astype(BF).reshape(4, 4 * BLOCK, WIDTH)
    attn_next, gain_grads = exchange(attn_mine, gain_grads, lambda r: shift_plane(r, False))
    nearer = [grad_zero, ffn_next_got, ffn_last_got]
    low_mine = total([part[:, :2] for part in nearer] + [far_low_got]).astype(BF)
    high_mine = total([part[:, 2:] for part in nearer] + [far_high_got]).astype(BF)
    attn_next = attn_next.astype(BF).reshape(4, BLOCK, WIDTH)
    low_gains = jnp.pad(gain_grads.astype(BF), ((0, 14), (0, 0)))

    def rows_for(r):
        ffn_rows = (low_mine if r < 2 else high_mine)[:, r % 2].reshape(3 * BLOCK, WIDTH)
        return jnp.concatenate([ffn_rows, attn_next[r], low_gains], axis=0)

    got = [permute(rows_for(r), shift_plane(r, True)) for r in (1, 3, 2)]
    kept, *sent = x_payloads(jnp.stack([x, x, x]).astype(jnp.int32), rows_for(0), got, gain_grads)
    got = [permute(sent[r - 1], shift_x(r)) for r in (1, 3, 2)]
    mine = total([kept] + got)
    ffn_owned = mine[:60].reshape(3, 20, WIDTH)
    attn_owned = permute(mine[60:80], to_owner())
    gain_grads = mine[80:82]
    gain_grads = gain_grads + permute(gain_grads, shift_core())
    gain_owned = lax.dynamic_slice_in_dim(gain_grads.reshape(2 * WIDTH), flat_index(z, y, x, c) * 15, 15)
    return (
        result.reshape(MICRO, TOK, WIDTH),
        grad_inputs.reshape(MICRO, TOK, WIDTH),
        attn_owned,
        ffn_owned[:2],
        ffn_owned[2],
        gain_owned,
    )


def flat_index(z, y, x, c):
    return ((z * 4 + y) * 4 + x) * 2 + c


def solution(mesh):
    grid = Mesh(mesh.devices.reshape(4, 4, 4, 2), AXES)
    return jax.shard_map(
        body,
        mesh=grid,
        in_specs=(
            P(None, AXES, None),
            P(None, AXES),
            P(AXES, None),
            P(None, AXES, None),
            P(AXES, None),
            P(AXES),
            P(None, AXES, None),
        ),
        out_specs=(
            P(None, AXES, None),
            P(None, AXES, None),
            P(AXES, None),
            P(None, AXES, None),
            P(AXES, None),
            P(AXES),
        ),
        check_vma=False,
    )
```

```python
import jax
import jax.numpy as jnp
from jax import lax
from jax.experimental import pallas as pl
from jax.experimental.pallas import tpu as pltpu
from jax.sharding import Mesh, PartitionSpec as P

HEADS = 15
KV_HEADS = 5
GROUP = HEADS // KV_HEADS
HEAD_DIM = 64
MICRO = 2
WIDTH = 960
TOK = 128
BLOCK = 80
EPS = 1e-05
THETA = 100000.0
NEG_FILL = -1e30
AXES = ("z", "y", "x", "c")
BF = jnp.bfloat16
F32 = jnp.float32


def flat(z, y, x, c):
    return (((z % 4) * 4 + y % 4) * 4 + x % 4) * 2 + c % 2


def everywhere():
    return [(z, y, x, c) for z in range(4) for y in range(4) for x in range(4) for c in range(2)]


def shift_x(step):
    return [(flat(*d), flat(d[0], d[1], d[2] + step, d[3])) for d in everywhere()]


def shift_core():
    return [(flat(*d), flat(d[0], d[1], d[2], d[3] + 1)) for d in everywhere()]


def shift_plane(step, inner):
    pairs = []
    for z, y, x, c in everywhere():
        along_y = (c == 0) == inner
        pairs.append((flat(z, y, x, c), flat(z, y + step, x, c) if along_y else flat(z + step, y, x, c)))
    return pairs


def to_owner():
    return [(flat(z, y, j, c), flat(z, y, 2 * c + j // 2, j % 2)) for z, y, j, c in everywhere()]


def permute(value, pairs):
    return lax.ppermute(value, AXES, pairs)


def fetch(value, make):
    return [value] + [permute(value, make(-r)) for r in (1, 3, 2)]


def fetch_ordered(value, make):
    got = fetch(value, make)
    return [got[0], got[1], got[3], got[2]]


def move_rows(where_ref, own, sib, weights, gains):
    z, y, c = where_ref[0], where_ref[1], where_ref[2]
    for r2 in range(4):
        for r1 in range(4):
            for which, group in enumerate((own, sib)):
                core = c if which == 0 else 1 - c
                rz = jnp.where(core == 0, r2, r1)
                ry = jnp.where(core == 0, r1, r2)
                row = lax.rem(z + rz, 4) * 4 + lax.rem(y + ry, 4)
                weights[row, core] = group[r2][r1, 0:BLOCK]
                if which == 0:
                    gains[row] = group[r2][r1, BLOCK : BLOCK + 16]


def unpack_gains(gains):
    raw = gains[:, 0, 0:128].astype(BF)
    lane = lax.broadcasted_iota(jnp.int32, (128, WIDTH), 1)
    entry = lax.broadcasted_iota(jnp.int32, (128, WIDTH), 0)
    pick = jnp.where(lane - ((lane * 8739) >> 20) * 120 == entry, 1.0, 0.0).astype(BF)
    spread = dot(raw, pick, NN)
    lane = lax.broadcasted_iota(jnp.int32, (16, WIDTH), 1)
    row = lax.broadcasted_iota(jnp.int32, (16, WIDTH), 0)
    block = (lane * 8739) >> 20
    attn = jnp.sum(jnp.where(row == block, spread, 0.0), axis=0, keepdims=True)
    mlp = jnp.sum(jnp.where(row == block + 8, spread, 0.0), axis=0, keepdims=True)
    return attn, mlp


def heads_of(ref, kv, b):
    lanes = slice(TOK * b, TOK * (b + 1))
    parts = [ref[HEAD_DIM * h : HEAD_DIM * (h + 1), lanes] for h in range(GROUP * kv, GROUP * (kv + 1))]
    return jnp.concatenate(parts, axis=1)


def turn(values, cosine, sine):
    split = values.reshape(-1, 2, HEAD_DIM // 2, values.shape[-1])
    former, latter = split[:, 0], split[:, 1]
    turned = jnp.stack([former * cosine - latter * sine, latter * cosine + former * sine], axis=1)
    return turned.reshape(values.shape)


def attn_forward_kernel(where_ref, tokens, seg_col, seg_row, live, cosine, sine, *refs):
    own, sib = refs[0:4], refs[4:8]
    weights, normed, heads, probs, att, hidden, normed_two, gain_out, gains = refs[8:]
    move_rows(where_ref, own, sib, weights, gains)
    inputs = tokens[...].astype(F32)
    scaled = inputs * inv_rms(inputs)
    gain_attn, gain_mlp = unpack_gains(gains)
    gain_out[...] = jnp.concatenate([gain_attn, gain_mlp, jnp.zeros((6, WIDTH), F32)], axis=0)
    normed[...] = (scaled * gain_attn).astype(BF)
    rows = WIDTH + KV_HEADS * HEAD_DIM
    projected = dot(weights[0:10].reshape(-1, WIDTH), normed[...], NT)
    heads[0:rows] = turn(projected[0:rows], cosine[...], sine[...]).astype(BF)
    heads[rows:] = projected[rows:].astype(BF)
    key_place = lax.broadcasted_iota(jnp.int32, (TOK, TOK), 0)
    query_place = lax.broadcasted_iota(jnp.int32, (TOK, TOK), 1)
    for b in range(MICRO):
        lanes = slice(TOK * b, TOK * (b + 1))
        same = seg_col[lanes, :] == seg_row[b : b + 1, :]
        allowed = jnp.where(same & (key_place <= query_place), 1.0, 0.0)
        allowed = jnp.concatenate([allowed] * GROUP, axis=1)
        for kv in range(KV_HEADS):
            key = heads[WIDTH + HEAD_DIM * kv : WIDTH + HEAD_DIM * (kv + 1), lanes]
            value = heads[rows + HEAD_DIM * kv : rows + HEAD_DIM * (kv + 1), lanes]
            scores = dot(key, heads_of(heads, kv, b), TN) * HEAD_DIM ** (-0.5)
            scores = jnp.where(allowed > 0.5, scores, NEG_FILL)
            expd = jnp.exp(scores - jnp.max(scores, axis=0, keepdims=True))
            prob = expd / jnp.sum(expd, axis=0, keepdims=True)
            probs[b * KV_HEADS + kv] = prob
            attended = dot(value, prob.astype(BF), NN).astype(BF)
            for g in range(GROUP):
                h = GROUP * kv + g
                att[HEAD_DIM * h : HEAD_DIM * (h + 1), lanes] = attended[:, TOK * g : TOK * (g + 1)]
    total_hidden = inputs + live[...] * dot(att[...], weights[10:16].reshape(WIDTH, WIDTH), TN)
    hidden[...] = total_hidden
    normed_two[...] = (total_hidden * inv_rms(total_hidden) * gain_mlp).astype(BF)


def attn_forward(where, tokens, segment_ids, live, cosine, sine, own, sib):
    local = pl.BlockSpec(memory_space=pltpu.VMEM)
    rows = tokens.shape[0]
    qkv_rows = WIDTH + 2 * KV_HEADS * HEAD_DIM
    return pl.pallas_call(
        attn_forward_kernel,
        in_specs=[pl.BlockSpec(memory_space=pltpu.SMEM)] + [local] * 14,
        out_specs=[local] * 8,
        out_shape=[
            jax.ShapeDtypeStruct((16, 2, BLOCK, WIDTH), BF),
            jax.ShapeDtypeStruct((rows, WIDTH), BF),
            jax.ShapeDtypeStruct((qkv_rows, rows), BF),
            jax.ShapeDtypeStruct((MICRO * KV_HEADS, TOK, GROUP * TOK), F32),
            jax.ShapeDtypeStruct((WIDTH, rows), BF),
            jax.ShapeDtypeStruct((rows, WIDTH), F32),
            jax.ShapeDtypeStruct((rows, WIDTH), BF),
            jax.ShapeDtypeStruct((8, WIDTH), F32),
        ],
        scratch_shapes=[pltpu.VMEM((16, 16, WIDTH), BF)],
        compiler_params=pltpu.CompilerParams(vmem_limit_bytes=12 * 2**20),
        name="attn_forward",
    )(where, tokens, segment_ids.reshape(rows, 1), segment_ids, live, cosine, sine, *own, *sib)


def attn_backward_kernel(where_ref, back, back_other, hidden, gains, cot, live, weights, heads, probs, att, normed, cosine, sine,
                         ours, theirs, grad_hidden, grad_proj, gain_grad, raw):
    z, y, c = where_ref[0], where_ref[1], where_ref[2]
    rows = hidden.shape[0]
    grad_normed = back[0:rows] + back_other[...].astype(F32)
    grad, gain_mlp = norm_back(grad_normed, hidden[...], inv_rms(hidden[...]), gains[1:2])
    grad = cot[...].astype(F32) + grad
    grad_hidden[...] = grad
    gain_grad[...] = jnp.concatenate([jnp.zeros((1, WIDTH), F32), gain_mlp, jnp.zeros((6, WIDTH), F32)], axis=0)
    branch = (live[...] * grad).astype(BF)
    grad_att = dot(weights[10:16].reshape(WIDTH, WIDTH), branch, NT).astype(BF)
    base = WIDTH + KV_HEADS * HEAD_DIM
    for b in range(MICRO):
        lanes = slice(TOK * b, TOK * (b + 1))
        for kv in range(KV_HEADS):
            key = heads[WIDTH + HEAD_DIM * kv : WIDTH + HEAD_DIM * (kv + 1), lanes]
            value = heads[base + HEAD_DIM * kv : base + HEAD_DIM * (kv + 1), lanes]
            query, grad_out = heads_of(heads, kv, b), heads_of(grad_att, kv, b)
            prob = probs[b * KV_HEADS + kv]
            grad_prob = dot(value, grad_out, TN)
            delta = jnp.sum(prob * grad_prob, axis=0, keepdims=True)
            grad_score = (HEAD_DIM ** (-0.5) * prob * (grad_prob - delta)).astype(BF)
            grad_query = dot(key, grad_score, NN)
            for g in range(GROUP):
                h = GROUP * kv + g
                raw[HEAD_DIM * h : HEAD_DIM * (h + 1), lanes] = grad_query[:, TOK * g : TOK * (g + 1)]
            raw[WIDTH + HEAD_DIM * kv : WIDTH + HEAD_DIM * (kv + 1), lanes] = dot(query, grad_score, NT)
            raw[base + HEAD_DIM * kv : base + HEAD_DIM * (kv + 1), lanes] = dot(grad_out, prob.astype(BF), NT)
    grad_proj[0:base] = turn(raw[0:base], cosine[...], -sine[...]).astype(BF)
    grad_proj[base:] = raw[base:].astype(BF)

    jobs = [(grad_proj, 0, 640, normed[...]), (grad_proj, 640, 640, normed[...]), (grad_proj, 1280, 320, normed[...])]
    jobs += [(att, 0, 640, branch), (att, 640, 320, branch)]
    row = 0
    for source, start, size, right in jobs:
        block = dot(source[start : start + size], right, NN).astype(BF)
        for k in range(size // 160):
            rz = lax.rem(row // 4 - z + 4, 4)
            ry = lax.rem(row % 4 - y + 4, 4)
            zy, yz = rz * 4 + ry, ry * 4 + rz
            lower = block[160 * k : 160 * k + 80]
            upper = block[160 * k + 80 : 160 * k + 160]

            @pl.when(c == 0)
            def _(lower=lower, upper=upper, zy=zy, yz=yz):
                ours[zy] = lower
                theirs[yz] = upper

            @pl.when(c != 0)
            def _(lower=lower, upper=upper, zy=zy, yz=yz):
                ours[yz] = upper
                theirs[zy] = lower

            row += 1


def attn_backward(where, back, back_other, hidden, gains, cot, live, weights, heads, probs, att, normed, cosine, sine):
    local = pl.BlockSpec(memory_space=pltpu.VMEM)
    return pl.pallas_call(
        attn_backward_kernel,
        in_specs=[pl.BlockSpec(memory_space=pltpu.SMEM)] + [local] * 13,
        out_specs=[local] * 5,
        out_shape=[
            jax.ShapeDtypeStruct((16, BLOCK, WIDTH), BF),
            jax.ShapeDtypeStruct((16, BLOCK, WIDTH), BF),
            jax.ShapeDtypeStruct(hidden.shape, F32),
            jax.ShapeDtypeStruct(heads.shape, BF),
            jax.ShapeDtypeStruct((8, WIDTH), F32),
        ],
        scratch_shapes=[pltpu.VMEM(heads.shape, F32)],
        compiler_params=pltpu.CompilerParams(vmem_limit_bytes=16 * 2**20),
        name="attn_backward",
    )(where, back, back_other, hidden, gains, cot, live, weights, heads, probs, att, normed, cosine, sine)


def attn_inputs_kernel(grad_proj, weights, tokens, gains, grad_hidden, gain_grad, grad_inputs, gain_out):
    inputs = tokens[...].astype(F32)
    grad_normed = dot(grad_proj[...], weights[0:10].reshape(-1, WIDTH), TN)
    grad, gain_attn = norm_back(grad_normed, inputs, inv_rms(inputs), gains[0:1])
    grad_inputs[...] = (grad_hidden[...] + grad).astype(BF)
    gain_out[...] = gain_grad[...] + jnp.concatenate([gain_attn, jnp.zeros((7, WIDTH), F32)], axis=0)


def attn_inputs(grad_proj, weights, tokens, gains, grad_hidden, gain_grad):
    local = pl.BlockSpec(memory_space=pltpu.VMEM)
    return pl.pallas_call(
        attn_inputs_kernel,
        in_specs=[local] * 6,
        out_specs=[local] * 2,
        out_shape=[jax.ShapeDtypeStruct(tokens.shape, BF), jax.ShapeDtypeStruct((8, WIDTH), F32)],
        compiler_params=pltpu.CompilerParams(vmem_limit_bytes=12 * 2**20),
        name="attn_inputs",
    )(grad_proj, weights, tokens, gains, grad_hidden, gain_grad)


def x_payloads_kernel(where_ref, own, got_a, got_b, got_c, gains, kept, sent_a, sent_b, sent_c, blocks):
    rows = 4 * BLOCK
    mine = own[0:rows].astype(F32)
    gain = gains[...]
    for part in (got_a, got_b, got_c):
        mine = mine + part[0:rows].astype(F32)
        gain = gain + part[rows : rows + 2].astype(F32)
    for j in range(4):
        blocks[j, 0:20] = mine[3 * BLOCK + 20 * j : 3 * BLOCK + 20 * j + 20]
    for r in range(4):
        pieces = [mine[BLOCK * w + 20 * r : BLOCK * w + 20 * r + 20] for w in range(3)]
        pieces += [blocks[lax.rem(where_ref[0] + r, 4)][0:20], gain]
        block = jnp.concatenate(pieces, axis=0)
        if r == 0:
            kept[...] = block
        else:
            (sent_a, sent_b, sent_c)[r - 1][...] = block.astype(BF)


def x_payloads(where, own, got, gains):
    local = pl.BlockSpec(memory_space=pltpu.VMEM)
    return pl.pallas_call(
        x_payloads_kernel,
        in_specs=[pl.BlockSpec(memory_space=pltpu.SMEM)] + [local] * 5,
        out_specs=[local] * 4,
        out_shape=[jax.ShapeDtypeStruct((82, WIDTH), F32)] + [jax.ShapeDtypeStruct((82, WIDTH), BF)] * 3,
        scratch_shapes=[pltpu.VMEM((4, 24, WIDTH), F32)],
        compiler_params=pltpu.CompilerParams(vmem_limit_bytes=12 * 2**20),
        name="x_payloads",
    )(where, own, *got, gains)


def ffn_kernel(count, first, normed, cot, *refs):
    chunks, refs = refs[:count], refs[count:]
    if first:
        branch, back = 0.0, 0.0
    else:
        branch, back = refs[0][...], refs[1][...]
        refs = refs[2:]
    grads, branch_out, back_out = refs[:count], refs[count], refs[count + 1]
    for chunk, grad in zip(chunks, grads):
        parts = chunk.shape[1]
        half = parts * BLOCK
        pair = chunk[0:2].reshape(2 * half, WIDTH)
        down = chunk[2].reshape(half, WIDTH)
        both = dot(pair, normed[...], NT)
        grad_prod = dot(down, cot[...], NT)
        gate, up = both[:half], both[half:]
        sigma = 1.0 / (1.0 + jnp.exp(-gate))
        gated = gate * sigma
        product = (gated * up).astype(BF)
        grad_gate = (grad_prod * up * sigma * (1.0 + gate * (1.0 - sigma))).astype(BF)
        grad_up = (grad_prod * gated).astype(BF)
        grad_pair = jnp.concatenate([grad_gate, grad_up], axis=0)
        back = back + dot(grad_pair, pair, TN)
        grad[0:2] = dot(grad_pair, normed[...], NN).astype(BF).reshape(2, parts, BLOCK, WIDTH)
        grad[2] = dot(product, cot[...], NN).astype(BF).reshape(parts, BLOCK, WIDTH)
        branch = branch + dot(product, down, TN)
    branch_out[...] = branch
    back_out[...] = back


def ffn(normed, cot, chunks, sums):
    local = pl.BlockSpec(memory_space=pltpu.VMEM)
    count, tokens = len(chunks), normed.shape[0]
    sums = list(sums)
    held = len(sums)
    units = sum(chunk.shape[1] for chunk in chunks) * BLOCK
    out = pl.pallas_call(
        lambda *refs: ffn_kernel(count, held == 0, *refs),
        in_specs=[local] * (2 + count + held),
        out_specs=[local] * (count + 2),
        out_shape=[jax.ShapeDtypeStruct(chunk.shape, BF) for chunk in chunks]
        + [jax.ShapeDtypeStruct((tokens, WIDTH), F32)] * 2,
        input_output_aliases={2 + count + i: count + i for i in range(held)},
        compiler_params=pltpu.CompilerParams(vmem_limit_bytes=16 * 2**20),
        cost_estimate=pl.CostEstimate(
            flops=18 * tokens * units * WIDTH,
            transcendentals=tokens * units,
            bytes_accessed=12 * units * WIDTH,
        ),
        name="ffn_chunks",
    )(normed, cot, *chunks, *sums)
    return out[:count], out[count:]


def rope_tables(seg):
    places = jnp.arange(TOK)
    allowed = (seg[:, :, None] == seg[:, None, :]) & (places[None, :] <= places[:, None])
    position = jnp.sum(allowed.astype(F32), axis=-1) - 1.0
    freqs = THETA ** (-2.0 * jnp.arange(HEAD_DIM // 2).astype(F32) / HEAD_DIM)
    angles = freqs[:, None] * position.reshape(1, -1)
    return jnp.cos(angles), jnp.sin(angles)


def inv_rms(values):
    return lax.rsqrt(jnp.mean(values * values, axis=-1, keepdims=True) + EPS)


def norm_back(grad_normed, source, inverse, gain_vec):
    scaled = source * inverse
    grad_scaled = grad_normed * gain_vec
    grad_gain = jnp.sum(grad_normed * scaled, axis=0, keepdims=True)
    mean = jnp.mean(grad_scaled * scaled, axis=-1, keepdims=True)
    return inverse * (grad_scaled - scaled * mean), grad_gain


def dot(left, right, dims):
    return lax.dot_general(left, right, (dims, ((), ())), preferred_element_type=F32)


NT = ((1,), (1,))
NN = ((1,), (0,))
TN = ((0,), (0,))


def total(parts):
    out = parts[0].astype(F32)
    for part in parts[1:]:
        out = out + part.astype(F32)
    return out


def body(tokens, segment_ids, attn_weight, gate_up, down_weight, norm_gains, cotangent):
    z, y, x, c = (lax.axis_index(a) for a in AXES)
    rows = MICRO * TOK

    gain_row = jnp.pad(norm_gains[None, :], ((0, 15), (0, WIDTH - 15)))
    shard = jnp.concatenate([attn_weight, gate_up[0], gate_up[1], down_weight, gain_row], axis=0)
    near = jnp.stack(fetch_ordered(shard, shift_x))
    ffn_block = near[:, 20:80].reshape(4, 3, 20, WIDTH).transpose(1, 0, 2, 3).reshape(3, BLOCK, WIDTH)
    head = jnp.concatenate([near[:, :20], near[:, 80:81]], axis=1)
    head = lax.dynamic_slice_in_dim(jnp.concatenate([head, head], axis=0), lax.rem(4 - x, 4), 4, axis=0)
    other = permute(head, shift_core())
    both = jnp.stack([jnp.where(c == 0, head, other), jnp.where(c == 0, other, head)], axis=1)
    attn_half = lax.dynamic_slice_in_dim(both[:, :, :20].reshape(2 * BLOCK, WIDTH), c * BLOCK, BLOCK, axis=0)
    gain_near = jnp.pad(both[:, :, 20, :15].reshape(1, 120), ((0, 15), (0, WIDTH - 120)))
    attn_block = jnp.concatenate([attn_half, gain_near], axis=0)

    block = jnp.concatenate([attn_block, ffn_block.reshape(3 * BLOCK, WIDTH)], axis=0)
    got = fetch_ordered(block, lambda s: shift_plane(s, True))
    attn_one = jnp.stack([part[:96] for part in got])
    ffn_one = jnp.stack([part[96:].reshape(3, BLOCK, WIDTH) for part in got], axis=1)
    own = fetch_ordered(attn_one, lambda s: shift_plane(s, False))
    sib = [permute(v, shift_core()) for v in own]
    where = jnp.stack([z, y, c]).astype(jnp.int32)

    ffn_next = permute(ffn_one, shift_plane(-1, False))
    ffn_last = permute(ffn_one, shift_plane(-3, False))

    live = (segment_ids.reshape(rows, 1) < TOK).astype(F32)
    cot = cotangent.reshape(rows, WIDTH)
    grad_mlp = (live * cot.astype(F32)).astype(BF)
    grad_mlp_all = jnp.concatenate([grad_mlp, permute(grad_mlp, shift_core())], axis=0)
    cosine, sine = rope_tables(segment_ids)
    flat_tokens = tokens.reshape(rows, WIDTH)
    weights, normed_one, heads, probs, att, hidden, normed_two, gains = attn_forward(
        where, flat_tokens, segment_ids, live, cosine, sine, own, sib
    )

    normed_all = jnp.concatenate([normed_two, permute(normed_two, shift_core())], axis=0)
    (grad_zero,), sums = ffn(normed_all, grad_mlp_all, [ffn_one], [])
    ffn_next, ffn_last, _ = lax.optimization_barrier((ffn_next, ffn_last, sums[0]))
    far_low = permute(ffn_next[:, :2], shift_plane(-1, False))
    far_high = permute(ffn_last[:, 2:], shift_plane(1, False))
    far_low, far_high = lax.optimization_barrier((far_low, far_high))
    (grad_next, grad_last), sums = ffn(normed_all, grad_mlp_all, [ffn_next, ffn_last], sums)
    grad_next, grad_last, far_low, far_high = lax.optimization_barrier((grad_next, grad_last, far_low, far_high))
    (grad_low,), sums = ffn(normed_all, grad_mlp_all, [far_low], sums)
    (grad_high,), (branch, grad_normed) = ffn(normed_all, grad_mlp_all, [far_high], sums)
    back_other = permute(grad_normed[rows:].astype(BF), shift_core())
    branch = branch[:rows] + permute(branch[rows:].astype(BF), shift_core()).astype(F32)
    result = (hidden + live * branch).astype(BF)

    ours, theirs, grad_hidden, grad_proj, gain_grads = attn_backward(
        where, grad_normed, back_other, hidden, gains, cot, live, weights, heads, probs, att, normed_one, cosine, sine
    )
    ffn_next_got = permute(grad_next, shift_plane(1, False))
    ffn_last_got = permute(grad_last, shift_plane(3, False))
    far_low = permute(grad_low, shift_plane(1, False))
    far_high = permute(grad_high, shift_plane(-1, False))
    theirs, ffn_next_got, ffn_last_got, far_low, far_high = lax.optimization_barrier(
        (theirs, ffn_next_got, ffn_last_got, far_low, far_high)
    )
    far_low_got = permute(far_low, shift_plane(1, False))
    far_high_got = permute(far_high, shift_plane(-1, False))
    swapped = permute(theirs, shift_core())
    grad_inputs, gain_grads = attn_inputs(grad_proj, weights, flat_tokens, gains, grad_hidden, gain_grads)
    gain_grads = gain_grads[:2]

    def exchange(blocks, gain_grads, make):
        count = blocks.shape[1]
        low = jnp.pad(gain_grads.astype(BF), ((0, 14), (0, 0)))
        got = [permute(jnp.concatenate([blocks[r], low], axis=0), make(r)) for r in (1, 3, 2)]
        blocks = total([blocks[0]] + [part[:count] for part in got])
        return blocks, total([gain_grads] + [part[count : count + 2] for part in got])

    attn_mine = total([ours, swapped]).astype(BF).reshape(4, 4 * BLOCK, WIDTH)
    attn_next, gain_grads = exchange(attn_mine, gain_grads, lambda r: shift_plane(r, False))
    nearer = [grad_zero, ffn_next_got, ffn_last_got]
    low_mine = total([part[:, :2] for part in nearer] + [far_low_got]).astype(BF)
    high_mine = total([part[:, 2:] for part in nearer] + [far_high_got]).astype(BF)
    attn_next = attn_next.astype(BF).reshape(4, BLOCK, WIDTH)
    low_gains = jnp.pad(gain_grads.astype(BF), ((0, 14), (0, 0)))

    def rows_for(r):
        ffn_rows = (low_mine if r < 2 else high_mine)[:, r % 2].reshape(3 * BLOCK, WIDTH)
        return jnp.concatenate([ffn_rows, attn_next[r], low_gains], axis=0)

    got = [permute(rows_for(r), shift_plane(r, True)) for r in (1, 3, 2)]
    kept, *sent = x_payloads(jnp.stack([x, x, x]).astype(jnp.int32), rows_for(0), got, gain_grads)
    got = [permute(sent[r - 1], shift_x(r)) for r in (1, 3, 2)]
    mine = total([kept] + got)
    ffn_owned = mine[:60].reshape(3, 20, WIDTH)
    attn_owned = permute(mine[60:80], to_owner())
    gain_grads = mine[80:82]
    gain_grads = gain_grads + permute(gain_grads, shift_core())
    gain_owned = lax.dynamic_slice_in_dim(gain_grads.reshape(2 * WIDTH), flat_index(z, y, x, c) * 15, 15)
    return (
        result.reshape(MICRO, TOK, WIDTH),
        grad_inputs.reshape(MICRO, TOK, WIDTH),
        attn_owned,
        ffn_owned[:2],
        ffn_owned[2],
        gain_owned,
    )


def flat_index(z, y, x, c):
    return ((z * 4 + y) * 4 + x) * 2 + c


def solution(mesh):
    grid = Mesh(mesh.devices.reshape(4, 4, 4, 2), AXES)
    return jax.shard_map(
        body,
        mesh=grid,
        in_specs=(
            P(None, AXES, None),
            P(None, AXES),
            P(AXES, None),
            P(None, AXES, None),
            P(AXES, None),
            P(AXES),
            P(None, AXES, None),
        ),
        out_specs=(
            P(None, AXES, None),
            P(None, AXES, None),
            P(AXES, None),
            P(None, AXES, None),
            P(AXES, None),
            P(AXES),
        ),
        check_vma=False,
    )
```

```python
import jax
import jax.numpy as jnp
from jax import lax
from jax.experimental import pallas as pl
from jax.experimental.pallas import tpu as pltpu
from jax.sharding import Mesh, PartitionSpec as P

HEADS = 15
KV_HEADS = 5
GROUP = HEADS // KV_HEADS
HEAD_DIM = 64
MICRO = 2
WIDTH = 960
TOK = 128
BLOCK = 80
EPS = 1e-05
THETA = 100000.0
NEG_FILL = -1e30
AXES = ("z", "y", "x", "c")
BF = jnp.bfloat16
F32 = jnp.float32


def flat(z, y, x, c):
    return (((z % 4) * 4 + y % 4) * 4 + x % 4) * 2 + c % 2


def everywhere():
    return [(z, y, x, c) for z in range(4) for y in range(4) for x in range(4) for c in range(2)]


def shift_x(step):
    return [(flat(*d), flat(d[0], d[1], d[2] + step, d[3])) for d in everywhere()]


def shift_core():
    return [(flat(*d), flat(d[0], d[1], d[2], d[3] + 1)) for d in everywhere()]


def shift_plane(step, inner):
    pairs = []
    for z, y, x, c in everywhere():
        along_y = (c == 0) == inner
        pairs.append((flat(z, y, x, c), flat(z, y + step, x, c) if along_y else flat(z + step, y, x, c)))
    return pairs


def to_owner():
    return [(flat(z, y, j, c), flat(z, y, 2 * c + j // 2, j % 2)) for z, y, j, c in everywhere()]


def permute(value, pairs):
    return lax.ppermute(value, AXES, pairs)


def fetch(value, make):
    return [value] + [permute(value, make(-r)) for r in (1, 3, 2)]


def fetch_ordered(value, make):
    got = fetch(value, make)
    return [got[0], got[1], got[3], got[2]]


def move_rows(where_ref, own, sib, weights, gains):
    z, y, c = where_ref[0], where_ref[1], where_ref[2]
    for r2 in range(4):
        for r1 in range(4):
            for which, group in enumerate((own, sib)):
                core = c if which == 0 else 1 - c
                rz = jnp.where(core == 0, r2, r1)
                ry = jnp.where(core == 0, r1, r2)
                row = lax.rem(z + rz, 4) * 4 + lax.rem(y + ry, 4)
                weights[row, core] = group[r2][r1, 0:BLOCK]
                if which == 0:
                    gains[row] = group[r2][r1, BLOCK : BLOCK + 16]


def unpack_gains(gains):
    raw = gains[:, 0, 0:128].astype(BF)
    lane = lax.broadcasted_iota(jnp.int32, (128, WIDTH), 1)
    entry = lax.broadcasted_iota(jnp.int32, (128, WIDTH), 0)
    pick = jnp.where(lane - ((lane * 8739) >> 20) * 120 == entry, 1.0, 0.0).astype(BF)
    spread = dot(raw, pick, NN)
    lane = lax.broadcasted_iota(jnp.int32, (16, WIDTH), 1)
    row = lax.broadcasted_iota(jnp.int32, (16, WIDTH), 0)
    block = (lane * 8739) >> 20
    attn = jnp.sum(jnp.where(row == block, spread, 0.0), axis=0, keepdims=True)
    mlp = jnp.sum(jnp.where(row == block + 8, spread, 0.0), axis=0, keepdims=True)
    return attn, mlp


def heads_of(ref, kv, b):
    lanes = slice(TOK * b, TOK * (b + 1))
    parts = [ref[HEAD_DIM * h : HEAD_DIM * (h + 1), lanes] for h in range(GROUP * kv, GROUP * (kv + 1))]
    return jnp.concatenate(parts, axis=1)


def turn(values, cosine, sine):
    split = values.reshape(-1, 2, HEAD_DIM // 2, values.shape[-1])
    former, latter = split[:, 0], split[:, 1]
    turned = jnp.stack([former * cosine - latter * sine, latter * cosine + former * sine], axis=1)
    return turned.reshape(values.shape)


def attn_forward_kernel(where_ref, tokens, seg_col, seg_row, live, cosine, sine, *refs):
    own, sib = refs[0:4], refs[4:8]
    weights, normed, heads, probs, att, hidden, normed_two, gain_out, gains = refs[8:]
    move_rows(where_ref, own, sib, weights, gains)
    inputs = tokens[...].astype(F32)
    scaled = inputs * inv_rms(inputs)
    gain_attn, gain_mlp = unpack_gains(gains)
    gain_out[...] = jnp.concatenate([gain_attn, gain_mlp, jnp.zeros((6, WIDTH), F32)], axis=0)
    normed[...] = (scaled * gain_attn).astype(BF)
    rows = WIDTH + KV_HEADS * HEAD_DIM
    projected = dot(weights[0:10].reshape(-1, WIDTH), normed[...], NT)
    heads[0:rows] = turn(projected[0:rows], cosine[...], sine[...]).astype(BF)
    heads[rows:] = projected[rows:].astype(BF)
    key_place = lax.broadcasted_iota(jnp.int32, (TOK, TOK), 0)
    query_place = lax.broadcasted_iota(jnp.int32, (TOK, TOK), 1)
    for b in range(MICRO):
        lanes = slice(TOK * b, TOK * (b + 1))
        same = seg_col[lanes, :] == seg_row[b : b + 1, :]
        allowed = jnp.where(same & (key_place <= query_place), 1.0, 0.0)
        allowed = jnp.concatenate([allowed] * GROUP, axis=1)
        for kv in range(KV_HEADS):
            key = heads[WIDTH + HEAD_DIM * kv : WIDTH + HEAD_DIM * (kv + 1), lanes]
            value = heads[rows + HEAD_DIM * kv : rows + HEAD_DIM * (kv + 1), lanes]
            scores = dot(key, heads_of(heads, kv, b), TN) * HEAD_DIM ** (-0.5)
            scores = jnp.where(allowed > 0.5, scores, NEG_FILL)
            expd = jnp.exp(scores - jnp.max(scores, axis=0, keepdims=True))
            prob = expd / jnp.sum(expd, axis=0, keepdims=True)
            probs[b * KV_HEADS + kv] = prob
            attended = dot(value, prob.astype(BF), NN).astype(BF)
            for g in range(GROUP):
                h = GROUP * kv + g
                att[HEAD_DIM * h : HEAD_DIM * (h + 1), lanes] = attended[:, TOK * g : TOK * (g + 1)]
    total_hidden = inputs + live[...] * dot(att[...], weights[10:16].reshape(WIDTH, WIDTH), TN)
    hidden[...] = total_hidden
    normed_two[...] = (total_hidden * inv_rms(total_hidden) * gain_mlp).astype(BF)


def attn_forward(where, tokens, segment_ids, live, cosine, sine, own, sib):
    local = pl.BlockSpec(memory_space=pltpu.VMEM)
    rows = tokens.shape[0]
    qkv_rows = WIDTH + 2 * KV_HEADS * HEAD_DIM
    return pl.pallas_call(
        attn_forward_kernel,
        in_specs=[pl.BlockSpec(memory_space=pltpu.SMEM)] + [local] * 14,
        out_specs=[local] * 8,
        out_shape=[
            jax.ShapeDtypeStruct((16, 2, BLOCK, WIDTH), BF),
            jax.ShapeDtypeStruct((rows, WIDTH), BF),
            jax.ShapeDtypeStruct((qkv_rows, rows), BF),
            jax.ShapeDtypeStruct((MICRO * KV_HEADS, TOK, GROUP * TOK), F32),
            jax.ShapeDtypeStruct((WIDTH, rows), BF),
            jax.ShapeDtypeStruct((rows, WIDTH), F32),
            jax.ShapeDtypeStruct((rows, WIDTH), BF),
            jax.ShapeDtypeStruct((8, WIDTH), F32),
        ],
        scratch_shapes=[pltpu.VMEM((16, 16, WIDTH), BF)],
        compiler_params=pltpu.CompilerParams(vmem_limit_bytes=12 * 2**20),
        name="attn_forward",
    )(where, tokens, segment_ids.reshape(rows, 1), segment_ids, live, cosine, sine, *own, *sib)


def attn_backward_kernel(where_ref, back, back_other, hidden, gains, cot, live, weights, heads, probs, att, normed, cosine, sine,
                         ours, theirs, grad_hidden, grad_proj, gain_grad, raw):
    z, y, c = where_ref[0], where_ref[1], where_ref[2]
    rows = hidden.shape[0]
    grad_normed = back[0:rows] + back_other[...].astype(F32)
    grad, gain_mlp = norm_back(grad_normed, hidden[...], inv_rms(hidden[...]), gains[1:2])
    grad = cot[...].astype(F32) + grad
    grad_hidden[...] = grad
    gain_grad[...] = jnp.concatenate([jnp.zeros((1, WIDTH), F32), gain_mlp, jnp.zeros((6, WIDTH), F32)], axis=0)
    branch = (live[...] * grad).astype(BF)
    grad_att = dot(weights[10:16].reshape(WIDTH, WIDTH), branch, NT).astype(BF)
    base = WIDTH + KV_HEADS * HEAD_DIM
    for b in range(MICRO):
        lanes = slice(TOK * b, TOK * (b + 1))
        for kv in range(KV_HEADS):
            key = heads[WIDTH + HEAD_DIM * kv : WIDTH + HEAD_DIM * (kv + 1), lanes]
            value = heads[base + HEAD_DIM * kv : base + HEAD_DIM * (kv + 1), lanes]
            query, grad_out = heads_of(heads, kv, b), heads_of(grad_att, kv, b)
            prob = probs[b * KV_HEADS + kv]
            grad_prob = dot(value, grad_out, TN)
            delta = jnp.sum(prob * grad_prob, axis=0, keepdims=True)
            grad_score = (HEAD_DIM ** (-0.5) * prob * (grad_prob - delta)).astype(BF)
            grad_query = dot(key, grad_score, NN)
            for g in range(GROUP):
                h = GROUP * kv + g
                raw[HEAD_DIM * h : HEAD_DIM * (h + 1), lanes] = grad_query[:, TOK * g : TOK * (g + 1)]
            raw[WIDTH + HEAD_DIM * kv : WIDTH + HEAD_DIM * (kv + 1), lanes] = dot(query, grad_score, NT)
            raw[base + HEAD_DIM * kv : base + HEAD_DIM * (kv + 1), lanes] = dot(grad_out, prob.astype(BF), NT)
    grad_proj[0:base] = turn(raw[0:base], cosine[...], -sine[...]).astype(BF)
    grad_proj[base:] = raw[base:].astype(BF)

    jobs = [(grad_proj, 0, 640, normed[...]), (grad_proj, 640, 640, normed[...]), (grad_proj, 1280, 320, normed[...])]
    jobs += [(att, 0, 640, branch), (att, 640, 320, branch)]
    row = 0
    for source, start, size, right in jobs:
        block = dot(source[start : start + size], right, NN).astype(BF)
        for k in range(size // 160):
            rz = lax.rem(row // 4 - z + 4, 4)
            ry = lax.rem(row % 4 - y + 4, 4)
            zy, yz = rz * 4 + ry, ry * 4 + rz
            lower = block[160 * k : 160 * k + 80]
            upper = block[160 * k + 80 : 160 * k + 160]

            @pl.when(c == 0)
            def _(lower=lower, upper=upper, zy=zy, yz=yz):
                ours[zy] = lower
                theirs[yz] = upper

            @pl.when(c != 0)
            def _(lower=lower, upper=upper, zy=zy, yz=yz):
                ours[yz] = upper
                theirs[zy] = lower

            row += 1


def attn_backward(where, back, back_other, hidden, gains, cot, live, weights, heads, probs, att, normed, cosine, sine):
    local = pl.BlockSpec(memory_space=pltpu.VMEM)
    return pl.pallas_call(
        attn_backward_kernel,
        in_specs=[pl.BlockSpec(memory_space=pltpu.SMEM)] + [local] * 13,
        out_specs=[local] * 5,
        out_shape=[
            jax.ShapeDtypeStruct((16, BLOCK, WIDTH), BF),
            jax.ShapeDtypeStruct((16, BLOCK, WIDTH), BF),
            jax.ShapeDtypeStruct(hidden.shape, F32),
            jax.ShapeDtypeStruct(heads.shape, BF),
            jax.ShapeDtypeStruct((8, WIDTH), F32),
        ],
        scratch_shapes=[pltpu.VMEM(heads.shape, F32)],
        compiler_params=pltpu.CompilerParams(vmem_limit_bytes=16 * 2**20),
        name="attn_backward",
    )(where, back, back_other, hidden, gains, cot, live, weights, heads, probs, att, normed, cosine, sine)


def attn_inputs_kernel(grad_proj, weights, tokens, gains, grad_hidden, gain_grad, grad_inputs, gain_out):
    inputs = tokens[...].astype(F32)
    grad_normed = dot(grad_proj[...], weights[0:10].reshape(-1, WIDTH), TN)
    grad, gain_attn = norm_back(grad_normed, inputs, inv_rms(inputs), gains[0:1])
    grad_inputs[...] = (grad_hidden[...] + grad).astype(BF)
    gain_out[...] = gain_grad[...] + jnp.concatenate([gain_attn, jnp.zeros((7, WIDTH), F32)], axis=0)


def attn_inputs(grad_proj, weights, tokens, gains, grad_hidden, gain_grad):
    local = pl.BlockSpec(memory_space=pltpu.VMEM)
    return pl.pallas_call(
        attn_inputs_kernel,
        in_specs=[local] * 6,
        out_specs=[local] * 2,
        out_shape=[jax.ShapeDtypeStruct(tokens.shape, BF), jax.ShapeDtypeStruct((8, WIDTH), F32)],
        compiler_params=pltpu.CompilerParams(vmem_limit_bytes=12 * 2**20),
        name="attn_inputs",
    )(grad_proj, weights, tokens, gains, grad_hidden, gain_grad)


def x_payloads_kernel(where_ref, own, got_a, got_b, got_c, gains, kept, sent_a, sent_b, sent_c, blocks):
    rows = 4 * BLOCK
    mine = own[0:rows].astype(F32)
    gain = gains[...]
    for part in (got_a, got_b, got_c):
        mine = mine + part[0:rows].astype(F32)
        gain = gain + part[rows : rows + 2].astype(F32)
    for j in range(4):
        blocks[j, 0:20] = mine[3 * BLOCK + 20 * j : 3 * BLOCK + 20 * j + 20]
    for r in range(4):
        pieces = [mine[BLOCK * w + 20 * r : BLOCK * w + 20 * r + 20] for w in range(3)]
        pieces += [blocks[lax.rem(where_ref[0] + r, 4)][0:20], gain]
        block = jnp.concatenate(pieces, axis=0)
        if r == 0:
            kept[...] = block
        else:
            (sent_a, sent_b, sent_c)[r - 1][...] = block.astype(BF)


def x_payloads(where, own, got, gains):
    local = pl.BlockSpec(memory_space=pltpu.VMEM)
    return pl.pallas_call(
        x_payloads_kernel,
        in_specs=[pl.BlockSpec(memory_space=pltpu.SMEM)] + [local] * 5,
        out_specs=[local] * 4,
        out_shape=[jax.ShapeDtypeStruct((82, WIDTH), F32)] + [jax.ShapeDtypeStruct((82, WIDTH), BF)] * 3,
        scratch_shapes=[pltpu.VMEM((4, 24, WIDTH), F32)],
        compiler_params=pltpu.CompilerParams(vmem_limit_bytes=12 * 2**20),
        name="x_payloads",
    )(where, own, *got, gains)


def ffn_kernel(count, first, normed, cot, *refs):
    chunks, refs = refs[:count], refs[count:]
    if first:
        branch, back = 0.0, 0.0
    else:
        branch, back = refs[0][...], refs[1][...]
        refs = refs[2:]
    grads, branch_out, back_out = list(refs[:-2]), refs[-2], refs[-1]
    step = 2 * BLOCK
    for chunk in chunks:
        parts = chunk.shape[1]
        half = parts * BLOCK
        pair = chunk[0:2].reshape(2 * half, WIDTH)
        down = chunk[2].reshape(half, WIDTH)
        both = dot(pair, normed[...], NT)
        grad_prod = dot(down, cot[...], NT)
        gate, up = both[:half], both[half:]
        sigma = 1.0 / (1.0 + jnp.exp(-gate))
        gated = gate * sigma
        product = (gated * up).astype(BF)
        grad_gate = (grad_prod * up * sigma * (1.0 + gate * (1.0 - sigma))).astype(BF)
        grad_up = (grad_prod * gated).astype(BF)
        grad_pair = jnp.concatenate([grad_gate, grad_up], axis=0)
        back = back + dot(grad_pair, pair, TN)
        pair_grad = dot(grad_pair, normed[...], NN).astype(BF)
        down_grad = dot(product, cot[...], NN).astype(BF)
        for at in range(0, half, step):
            grad = grads.pop(0)
            grad[0] = pair_grad[at : at + step].reshape(2, BLOCK, WIDTH)
            grad[1] = pair_grad[half + at : half + at + step].reshape(2, BLOCK, WIDTH)
            grad[2] = down_grad[at : at + step].reshape(2, BLOCK, WIDTH)
        branch = branch + dot(product, down, TN)
    branch_out[...] = branch
    back_out[...] = back


def ffn(normed, cot, chunks, sums):
    local = pl.BlockSpec(memory_space=pltpu.VMEM)
    count, tokens = len(chunks), normed.shape[0]
    sums = list(sums)
    held = len(sums)
    units = sum(chunk.shape[1] for chunk in chunks) * BLOCK
    pieces = units // (2 * BLOCK)
    out = pl.pallas_call(
        lambda *refs: ffn_kernel(count, held == 0, *refs),
        in_specs=[local] * (2 + count + held),
        out_specs=[local] * (pieces + 2),
        out_shape=[jax.ShapeDtypeStruct((3, 2, BLOCK, WIDTH), BF)] * pieces
        + [jax.ShapeDtypeStruct((tokens, WIDTH), F32)] * 2,
        input_output_aliases={2 + count + i: pieces + i for i in range(held)},
        compiler_params=pltpu.CompilerParams(vmem_limit_bytes=16 * 2**20),
        cost_estimate=pl.CostEstimate(
            flops=18 * tokens * units * WIDTH,
            transcendentals=tokens * units,
            bytes_accessed=12 * units * WIDTH,
        ),
        name="ffn_chunks",
    )(normed, cot, *chunks, *sums)
    return out[:pieces], out[pieces:]


def rope_tables(seg):
    places = jnp.arange(TOK)
    allowed = (seg[:, :, None] == seg[:, None, :]) & (places[None, :] <= places[:, None])
    position = jnp.sum(allowed.astype(F32), axis=-1) - 1.0
    freqs = THETA ** (-2.0 * jnp.arange(HEAD_DIM // 2).astype(F32) / HEAD_DIM)
    angles = freqs[:, None] * position.reshape(1, -1)
    return jnp.cos(angles), jnp.sin(angles)


def inv_rms(values):
    return lax.rsqrt(jnp.mean(values * values, axis=-1, keepdims=True) + EPS)


def norm_back(grad_normed, source, inverse, gain_vec):
    scaled = source * inverse
    grad_scaled = grad_normed * gain_vec
    grad_gain = jnp.sum(grad_normed * scaled, axis=0, keepdims=True)
    mean = jnp.mean(grad_scaled * scaled, axis=-1, keepdims=True)
    return inverse * (grad_scaled - scaled * mean), grad_gain


def dot(left, right, dims):
    return lax.dot_general(left, right, (dims, ((), ())), preferred_element_type=F32)


NT = ((1,), (1,))
NN = ((1,), (0,))
TN = ((0,), (0,))


def total(parts):
    out = parts[0].astype(F32)
    for part in parts[1:]:
        out = out + part.astype(F32)
    return out


def body(tokens, segment_ids, attn_weight, gate_up, down_weight, norm_gains, cotangent):
    z, y, x, c = (lax.axis_index(a) for a in AXES)
    rows = MICRO * TOK

    gain_row = jnp.pad(norm_gains[None, :], ((0, 15), (0, WIDTH - 15)))
    shard = jnp.concatenate([attn_weight, gate_up[0], gate_up[1], down_weight, gain_row], axis=0)
    near = jnp.stack(fetch_ordered(shard, shift_x))
    ffn_block = near[:, 20:80].reshape(4, 3, 20, WIDTH).transpose(1, 0, 2, 3).reshape(3, BLOCK, WIDTH)
    head = jnp.concatenate([near[:, :20], near[:, 80:81]], axis=1)
    head = lax.dynamic_slice_in_dim(jnp.concatenate([head, head], axis=0), lax.rem(4 - x, 4), 4, axis=0)
    other = permute(head, shift_core())
    both = jnp.stack([jnp.where(c == 0, head, other), jnp.where(c == 0, other, head)], axis=1)
    attn_half = lax.dynamic_slice_in_dim(both[:, :, :20].reshape(2 * BLOCK, WIDTH), c * BLOCK, BLOCK, axis=0)
    gain_near = jnp.pad(both[:, :, 20, :15].reshape(1, 120), ((0, 15), (0, WIDTH - 120)))
    attn_block = jnp.concatenate([attn_half, gain_near], axis=0)

    block = jnp.concatenate([attn_block, ffn_block.reshape(3 * BLOCK, WIDTH)], axis=0)
    got = fetch_ordered(block, lambda s: shift_plane(s, True))
    attn_one = jnp.stack([part[:96] for part in got])
    ffn_one = jnp.stack([part[96:].reshape(3, BLOCK, WIDTH) for part in got], axis=1)
    own = fetch_ordered(attn_one, lambda s: shift_plane(s, False))
    sib = [permute(v, shift_core()) for v in own]
    where = jnp.stack([z, y, c]).astype(jnp.int32)

    ffn_next = permute(ffn_one, shift_plane(-1, False))
    ffn_last = permute(ffn_one, shift_plane(-3, False))

    live = (segment_ids.reshape(rows, 1) < TOK).astype(F32)
    cot = cotangent.reshape(rows, WIDTH)
    grad_mlp = (live * cot.astype(F32)).astype(BF)
    grad_mlp_all = jnp.concatenate([grad_mlp, permute(grad_mlp, shift_core())], axis=0)
    cosine, sine = rope_tables(segment_ids)
    flat_tokens = tokens.reshape(rows, WIDTH)
    weights, normed_one, heads, probs, att, hidden, normed_two, gains = attn_forward(
        where, flat_tokens, segment_ids, live, cosine, sine, own, sib
    )

    normed_all = jnp.concatenate([normed_two, permute(normed_two, shift_core())], axis=0)
    zero_grads, sums = ffn(normed_all, grad_mlp_all, [ffn_one], [])
    ffn_next, ffn_last, _ = lax.optimization_barrier((ffn_next, ffn_last, sums[0]))
    far_low = permute(ffn_next[:, :2], shift_plane(-1, False))
    far_high = permute(ffn_last[:, 2:], shift_plane(1, False))
    far_low, far_high = lax.optimization_barrier((far_low, far_high))
    (next_low, next_high, last_low, last_high), sums = ffn(normed_all, grad_mlp_all, [ffn_next, ffn_last], sums)
    next_high, last_low, far_low, far_high = lax.optimization_barrier((next_high, last_low, far_low, far_high))
    (grad_low,), sums = ffn(normed_all, grad_mlp_all, [far_low], sums)
    (grad_high,), (branch, grad_normed) = ffn(normed_all, grad_mlp_all, [far_high], sums)
    back_other = permute(grad_normed[rows:].astype(BF), shift_core())
    branch = branch[:rows] + permute(branch[rows:].astype(BF), shift_core()).astype(F32)
    result = (hidden + live * branch).astype(BF)

    ours, theirs, grad_hidden, grad_proj, gain_grads = attn_backward(
        where, grad_normed, back_other, hidden, gains, cot, live, weights, heads, probs, att, normed_one, cosine, sine
    )
    next_high_got = permute(next_high, shift_plane(1, False))
    last_low_got = permute(last_low, shift_plane(-1, False))
    far_low = permute(grad_low, shift_plane(1, False))
    far_high = permute(grad_high, shift_plane(-1, False))
    theirs, next_high_got, last_low_got, far_low, far_high = lax.optimization_barrier(
        (theirs, next_high_got, last_low_got, far_low, far_high)
    )
    next_low_got = permute(total([next_low, far_low]).astype(BF), shift_plane(1, False))
    last_high_got = permute(total([last_high, far_high]).astype(BF), shift_plane(-1, False))
    swapped = permute(theirs, shift_core())
    grad_inputs, gain_grads = attn_inputs(grad_proj, weights, flat_tokens, gains, grad_hidden, gain_grads)
    gain_grads = gain_grads[:2]

    def exchange(blocks, gain_grads, make):
        count = blocks.shape[1]
        low = jnp.pad(gain_grads.astype(BF), ((0, 14), (0, 0)))
        got = [permute(jnp.concatenate([blocks[r], low], axis=0), make(r)) for r in (1, 3, 2)]
        blocks = total([blocks[0]] + [part[:count] for part in got])
        return blocks, total([gain_grads] + [part[count : count + 2] for part in got])

    attn_mine = total([ours, swapped]).astype(BF).reshape(4, 4 * BLOCK, WIDTH)
    attn_next, gain_grads = exchange(attn_mine, gain_grads, lambda r: shift_plane(r, False))
    next_low_got, last_high_got, _ = lax.optimization_barrier((next_low_got, last_high_got, attn_next))
    low_mine = total([zero_grads[0], next_low_got, last_low_got]).astype(BF)
    high_mine = total([zero_grads[1], next_high_got, last_high_got]).astype(BF)
    attn_next = attn_next.astype(BF).reshape(4, BLOCK, WIDTH)
    low_gains = jnp.pad(gain_grads.astype(BF), ((0, 14), (0, 0)))

    def rows_for(r):
        ffn_rows = (low_mine if r < 2 else high_mine)[:, r % 2].reshape(3 * BLOCK, WIDTH)
        return jnp.concatenate([ffn_rows, attn_next[r], low_gains], axis=0)

    got = [permute(rows_for(r), shift_plane(r, True)) for r in (1, 3, 2)]
    kept, *sent = x_payloads(jnp.stack([x, x, x]).astype(jnp.int32), rows_for(0), got, gain_grads)
    got = [permute(sent[r - 1], shift_x(r)) for r in (1, 3, 2)]
    mine = total([kept] + got)
    ffn_owned = mine[:60].reshape(3, 20, WIDTH)
    attn_owned = permute(mine[60:80], to_owner())
    gain_grads = mine[80:82]
    gain_grads = gain_grads + permute(gain_grads, shift_core())
    gain_owned = lax.dynamic_slice_in_dim(gain_grads.reshape(2 * WIDTH), flat_index(z, y, x, c) * 15, 15)
    return (
        result.reshape(MICRO, TOK, WIDTH),
        grad_inputs.reshape(MICRO, TOK, WIDTH),
        attn_owned,
        ffn_owned[:2],
        ffn_owned[2],
        gain_owned,
    )


def flat_index(z, y, x, c):
    return ((z * 4 + y) * 4 + x) * 2 + c


def solution(mesh):
    grid = Mesh(mesh.devices.reshape(4, 4, 4, 2), AXES)
    return jax.shard_map(
        body,
        mesh=grid,
        in_specs=(
            P(None, AXES, None),
            P(None, AXES),
            P(AXES, None),
            P(None, AXES, None),
            P(AXES, None),
            P(AXES),
            P(None, AXES, None),
        ),
        out_specs=(
            P(None, AXES, None),
            P(None, AXES, None),
            P(AXES, None),
            P(None, AXES, None),
            P(AXES, None),
            P(AXES),
        ),
        check_vma=False,
    )
```

```python
import jax
import jax.numpy as jnp
from jax import lax
from jax.experimental import pallas as pl
from jax.experimental.pallas import tpu as pltpu
from jax.sharding import Mesh, PartitionSpec as P

HEADS = 15
KV_HEADS = 5
GROUP = HEADS // KV_HEADS
HEAD_DIM = 64
MICRO = 2
WIDTH = 960
TOK = 128
BLOCK = 80
EPS = 1e-05
THETA = 100000.0
NEG_FILL = -1e30
AXES = ("z", "y", "x", "c")
BF = jnp.bfloat16
F32 = jnp.float32


def flat(z, y, x, c):
    return (((z % 4) * 4 + y % 4) * 4 + x % 4) * 2 + c % 2


def everywhere():
    return [(z, y, x, c) for z in range(4) for y in range(4) for x in range(4) for c in range(2)]


def shift_x(step):
    return [(flat(*d), flat(d[0], d[1], d[2] + step, d[3])) for d in everywhere()]


def shift_core():
    return [(flat(*d), flat(d[0], d[1], d[2], d[3] + 1)) for d in everywhere()]


def shift_plane(step, inner):
    pairs = []
    for z, y, x, c in everywhere():
        along_y = (c == 0) == inner
        pairs.append((flat(z, y, x, c), flat(z, y + step, x, c) if along_y else flat(z + step, y, x, c)))
    return pairs


def to_owner():
    return [(flat(z, y, j, c), flat(z, y, 2 * c + j // 2, j % 2)) for z, y, j, c in everywhere()]


def permute(value, pairs):
    return lax.ppermute(value, AXES, pairs)


def fetch(value, make):
    return [value] + [permute(value, make(-r)) for r in (1, 3, 2)]


def fetch_ordered(value, make):
    got = fetch(value, make)
    return [got[0], got[1], got[3], got[2]]


def move_rows(where_ref, own, sib, weights, gains):
    z, y, c = where_ref[0], where_ref[1], where_ref[2]
    for r2 in range(4):
        for r1 in range(4):
            for which, group in enumerate((own, sib)):
                core = c if which == 0 else 1 - c
                rz = jnp.where(core == 0, r2, r1)
                ry = jnp.where(core == 0, r1, r2)
                row = lax.rem(z + rz, 4) * 4 + lax.rem(y + ry, 4)
                weights[row, core] = group[r2][r1, 0:BLOCK]
                if which == 0:
                    gains[row] = group[r2][r1, BLOCK : BLOCK + 16]


def unpack_gains(gains):
    raw = gains[:, 0, 0:128].astype(BF)
    lane = lax.broadcasted_iota(jnp.int32, (128, WIDTH), 1)
    entry = lax.broadcasted_iota(jnp.int32, (128, WIDTH), 0)
    pick = jnp.where(lane - ((lane * 8739) >> 20) * 120 == entry, 1.0, 0.0).astype(BF)
    spread = dot(raw, pick, NN)
    lane = lax.broadcasted_iota(jnp.int32, (16, WIDTH), 1)
    row = lax.broadcasted_iota(jnp.int32, (16, WIDTH), 0)
    block = (lane * 8739) >> 20
    attn = jnp.sum(jnp.where(row == block, spread, 0.0), axis=0, keepdims=True)
    mlp = jnp.sum(jnp.where(row == block + 8, spread, 0.0), axis=0, keepdims=True)
    return attn, mlp


def heads_of(ref, kv, b):
    lanes = slice(TOK * b, TOK * (b + 1))
    parts = [ref[HEAD_DIM * h : HEAD_DIM * (h + 1), lanes] for h in range(GROUP * kv, GROUP * (kv + 1))]
    return jnp.concatenate(parts, axis=1)


def turn(values, cosine, sine):
    split = values.reshape(-1, 2, HEAD_DIM // 2, values.shape[-1])
    former, latter = split[:, 0], split[:, 1]
    turned = jnp.stack([former * cosine - latter * sine, latter * cosine + former * sine], axis=1)
    return turned.reshape(values.shape)


def attn_forward_kernel(where_ref, tokens, seg_col, seg_row, live, cosine, sine, *refs):
    own, sib = refs[0:4], refs[4:8]
    weights, normed, heads, probs, att, hidden, normed_two, gain_out, gains = refs[8:]
    move_rows(where_ref, own, sib, weights, gains)
    inputs = tokens[...].astype(F32)
    scaled = inputs * inv_rms(inputs)
    gain_attn, gain_mlp = unpack_gains(gains)
    gain_out[...] = jnp.concatenate([gain_attn, gain_mlp, jnp.zeros((6, WIDTH), F32)], axis=0)
    normed[...] = (scaled * gain_attn).astype(BF)
    rows = WIDTH + KV_HEADS * HEAD_DIM
    projected = dot(weights[0:10].reshape(-1, WIDTH), normed[...], NT)
    heads[0:rows] = turn(projected[0:rows], cosine[...], sine[...]).astype(BF)
    heads[rows:] = projected[rows:].astype(BF)
    key_place = lax.broadcasted_iota(jnp.int32, (TOK, TOK), 0)
    query_place = lax.broadcasted_iota(jnp.int32, (TOK, TOK), 1)
    for b in range(MICRO):
        lanes = slice(TOK * b, TOK * (b + 1))
        same = seg_col[lanes, :] == seg_row[b : b + 1, :]
        allowed = jnp.where(same & (key_place <= query_place), 1.0, 0.0)
        allowed = jnp.concatenate([allowed] * GROUP, axis=1)
        for kv in range(KV_HEADS):
            key = heads[WIDTH + HEAD_DIM * kv : WIDTH + HEAD_DIM * (kv + 1), lanes]
            value = heads[rows + HEAD_DIM * kv : rows + HEAD_DIM * (kv + 1), lanes]
            scores = dot(key, heads_of(heads, kv, b), TN) * HEAD_DIM ** (-0.5)
            scores = jnp.where(allowed > 0.5, scores, NEG_FILL)
            expd = jnp.exp(scores - jnp.max(scores, axis=0, keepdims=True))
            prob = expd / jnp.sum(expd, axis=0, keepdims=True)
            probs[b * KV_HEADS + kv] = prob
            attended = dot(value, prob.astype(BF), NN).astype(BF)
            for g in range(GROUP):
                h = GROUP * kv + g
                att[HEAD_DIM * h : HEAD_DIM * (h + 1), lanes] = attended[:, TOK * g : TOK * (g + 1)]
    total_hidden = inputs + live[...] * dot(att[...], weights[10:16].reshape(WIDTH, WIDTH), TN)
    hidden[...] = total_hidden
    normed_two[...] = (total_hidden * inv_rms(total_hidden) * gain_mlp).astype(BF)


def attn_forward(where, tokens, segment_ids, live, cosine, sine, own, sib):
    local = pl.BlockSpec(memory_space=pltpu.VMEM)
    rows = tokens.shape[0]
    qkv_rows = WIDTH + 2 * KV_HEADS * HEAD_DIM
    return pl.pallas_call(
        attn_forward_kernel,
        in_specs=[pl.BlockSpec(memory_space=pltpu.SMEM)] + [local] * 14,
        out_specs=[local] * 8,
        out_shape=[
            jax.ShapeDtypeStruct((16, 2, BLOCK, WIDTH), BF),
            jax.ShapeDtypeStruct((rows, WIDTH), BF),
            jax.ShapeDtypeStruct((qkv_rows, rows), BF),
            jax.ShapeDtypeStruct((MICRO * KV_HEADS, TOK, GROUP * TOK), F32),
            jax.ShapeDtypeStruct((WIDTH, rows), BF),
            jax.ShapeDtypeStruct((rows, WIDTH), F32),
            jax.ShapeDtypeStruct((rows, WIDTH), BF),
            jax.ShapeDtypeStruct((8, WIDTH), F32),
        ],
        scratch_shapes=[pltpu.VMEM((16, 16, WIDTH), BF)],
        compiler_params=pltpu.CompilerParams(vmem_limit_bytes=12 * 2**20),
        name="attn_forward",
    )(where, tokens, segment_ids.reshape(rows, 1), segment_ids, live, cosine, sine, *own, *sib)


def attn_backward_kernel(where_ref, back, back_other, hidden, gains, cot, live, weights, heads, probs, att, normed, cosine, sine,
                         ours, theirs, grad_hidden, grad_proj, gain_grad, raw):
    z, y, c = where_ref[0], where_ref[1], where_ref[2]
    rows = hidden.shape[0]
    grad_normed = back[0:rows] + back_other[...].astype(F32)
    grad, gain_mlp = norm_back(grad_normed, hidden[...], inv_rms(hidden[...]), gains[1:2])
    grad = cot[...].astype(F32) + grad
    grad_hidden[...] = grad
    gain_grad[...] = jnp.concatenate([jnp.zeros((1, WIDTH), F32), gain_mlp, jnp.zeros((6, WIDTH), F32)], axis=0)
    branch = (live[...] * grad).astype(BF)
    grad_att = dot(weights[10:16].reshape(WIDTH, WIDTH), branch, NT).astype(BF)
    base = WIDTH + KV_HEADS * HEAD_DIM
    for b in range(MICRO):
        lanes = slice(TOK * b, TOK * (b + 1))
        for kv in range(KV_HEADS):
            key = heads[WIDTH + HEAD_DIM * kv : WIDTH + HEAD_DIM * (kv + 1), lanes]
            value = heads[base + HEAD_DIM * kv : base + HEAD_DIM * (kv + 1), lanes]
            query, grad_out = heads_of(heads, kv, b), heads_of(grad_att, kv, b)
            prob = probs[b * KV_HEADS + kv]
            grad_prob = dot(value, grad_out, TN)
            delta = jnp.sum(prob * grad_prob, axis=0, keepdims=True)
            grad_score = (HEAD_DIM ** (-0.5) * prob * (grad_prob - delta)).astype(BF)
            grad_query = dot(key, grad_score, NN)
            for g in range(GROUP):
                h = GROUP * kv + g
                raw[HEAD_DIM * h : HEAD_DIM * (h + 1), lanes] = grad_query[:, TOK * g : TOK * (g + 1)]
            raw[WIDTH + HEAD_DIM * kv : WIDTH + HEAD_DIM * (kv + 1), lanes] = dot(query, grad_score, NT)
            raw[base + HEAD_DIM * kv : base + HEAD_DIM * (kv + 1), lanes] = dot(grad_out, prob.astype(BF), NT)
    grad_proj[0:base] = turn(raw[0:base], cosine[...], -sine[...]).astype(BF)
    grad_proj[base:] = raw[base:].astype(BF)

    jobs = [(grad_proj, 0, 640, normed[...]), (grad_proj, 640, 640, normed[...]), (grad_proj, 1280, 320, normed[...])]
    jobs += [(att, 0, 640, branch), (att, 640, 320, branch)]
    row = 0
    for source, start, size, right in jobs:
        block = dot(source[start : start + size], right, NN).astype(BF)
        for k in range(size // 160):
            rz = lax.rem(row // 4 - z + 4, 4)
            ry = lax.rem(row % 4 - y + 4, 4)
            zy, yz = rz * 4 + ry, ry * 4 + rz
            lower = block[160 * k : 160 * k + 80]
            upper = block[160 * k + 80 : 160 * k + 160]

            @pl.when(c == 0)
            def _(lower=lower, upper=upper, zy=zy, yz=yz):
                ours[zy] = lower
                theirs[yz] = upper

            @pl.when(c != 0)
            def _(lower=lower, upper=upper, zy=zy, yz=yz):
                ours[yz] = upper
                theirs[zy] = lower

            row += 1


def attn_backward(where, back, back_other, hidden, gains, cot, live, weights, heads, probs, att, normed, cosine, sine):
    local = pl.BlockSpec(memory_space=pltpu.VMEM)
    return pl.pallas_call(
        attn_backward_kernel,
        in_specs=[pl.BlockSpec(memory_space=pltpu.SMEM)] + [local] * 13,
        out_specs=[local] * 5,
        out_shape=[
            jax.ShapeDtypeStruct((16, BLOCK, WIDTH), BF),
            jax.ShapeDtypeStruct((16, BLOCK, WIDTH), BF),
            jax.ShapeDtypeStruct(hidden.shape, F32),
            jax.ShapeDtypeStruct(heads.shape, BF),
            jax.ShapeDtypeStruct((8, WIDTH), F32),
        ],
        scratch_shapes=[pltpu.VMEM(heads.shape, F32)],
        compiler_params=pltpu.CompilerParams(vmem_limit_bytes=16 * 2**20),
        name="attn_backward",
    )(where, back, back_other, hidden, gains, cot, live, weights, heads, probs, att, normed, cosine, sine)


def attn_inputs_kernel(grad_proj, weights, tokens, gains, grad_hidden, gain_grad, grad_inputs, gain_out):
    inputs = tokens[...].astype(F32)
    grad_normed = dot(grad_proj[...], weights[0:10].reshape(-1, WIDTH), TN)
    grad, gain_attn = norm_back(grad_normed, inputs, inv_rms(inputs), gains[0:1])
    grad_inputs[...] = (grad_hidden[...] + grad).astype(BF)
    gain_out[...] = gain_grad[...] + jnp.concatenate([gain_attn, jnp.zeros((7, WIDTH), F32)], axis=0)


def attn_inputs(grad_proj, weights, tokens, gains, grad_hidden, gain_grad):
    local = pl.BlockSpec(memory_space=pltpu.VMEM)
    return pl.pallas_call(
        attn_inputs_kernel,
        in_specs=[local] * 6,
        out_specs=[local] * 2,
        out_shape=[jax.ShapeDtypeStruct(tokens.shape, BF), jax.ShapeDtypeStruct((8, WIDTH), F32)],
        compiler_params=pltpu.CompilerParams(vmem_limit_bytes=12 * 2**20),
        name="attn_inputs",
    )(grad_proj, weights, tokens, gains, grad_hidden, gain_grad)


def x_payloads_kernel(where_ref, own, got_a, got_b, got_c, gains, kept, sent_a, sent_b, sent_c, blocks):
    rows = 4 * BLOCK
    mine = own[0:rows].astype(F32)
    gain = gains[...]
    for part in (got_a, got_b, got_c):
        mine = mine + part[0:rows].astype(F32)
        gain = gain + part[rows : rows + 2].astype(F32)
    for j in range(4):
        blocks[j, 0:20] = mine[3 * BLOCK + 20 * j : 3 * BLOCK + 20 * j + 20]
    for r in range(4):
        pieces = [mine[BLOCK * w + 20 * r : BLOCK * w + 20 * r + 20] for w in range(3)]
        pieces += [blocks[lax.rem(where_ref[0] + r, 4)][0:20], gain]
        block = jnp.concatenate(pieces, axis=0)
        if r == 0:
            kept[...] = block
        else:
            (sent_a, sent_b, sent_c)[r - 1][...] = block.astype(BF)


def x_payloads(where, own, got, gains):
    local = pl.BlockSpec(memory_space=pltpu.VMEM)
    return pl.pallas_call(
        x_payloads_kernel,
        in_specs=[pl.BlockSpec(memory_space=pltpu.SMEM)] + [local] * 5,
        out_specs=[local] * 4,
        out_shape=[jax.ShapeDtypeStruct((82, WIDTH), F32)] + [jax.ShapeDtypeStruct((82, WIDTH), BF)] * 3,
        scratch_shapes=[pltpu.VMEM((4, 24, WIDTH), F32)],
        compiler_params=pltpu.CompilerParams(vmem_limit_bytes=12 * 2**20),
        name="x_payloads",
    )(where, own, *got, gains)


def ffn_kernel(count, first, normed, cot, *refs):
    chunks, refs = refs[:count], refs[count:]
    if first:
        branch, back = 0.0, 0.0
    else:
        branch, back = refs[0][...], refs[1][...]
        refs = refs[2:]
    grads, branch_out, back_out = list(refs[:-2]), refs[-2], refs[-1]
    step = 2 * BLOCK
    for chunk in chunks:
        parts = chunk.shape[1]
        half = parts * BLOCK
        pair = chunk[0:2].reshape(2 * half, WIDTH)
        down = chunk[2].reshape(half, WIDTH)
        both = dot(pair, normed[...], NT)
        grad_prod = dot(down, cot[...], NT)
        gate, up = both[:half], both[half:]
        sigma = 1.0 / (1.0 + jnp.exp(-gate))
        gated = gate * sigma
        product = (gated * up).astype(BF)
        grad_gate = (grad_prod * up * sigma * (1.0 + gate * (1.0 - sigma))).astype(BF)
        grad_up = (grad_prod * gated).astype(BF)
        grad_pair = jnp.concatenate([grad_gate, grad_up], axis=0)
        back = back + dot(grad_pair, pair, TN)
        pair_grad = dot(grad_pair, normed[...], NN).astype(BF)
        down_grad = dot(product, cot[...], NN).astype(BF)
        for at in range(0, half, step):
            grad = grads.pop(0)
            grad[0] = pair_grad[at : at + step].reshape(2, BLOCK, WIDTH)
            grad[1] = pair_grad[half + at : half + at + step].reshape(2, BLOCK, WIDTH)
            grad[2] = down_grad[at : at + step].reshape(2, BLOCK, WIDTH)
        branch = branch + dot(product, down, TN)
    branch_out[...] = branch
    back_out[...] = back


def ffn(normed, cot, chunks, sums):
    local = pl.BlockSpec(memory_space=pltpu.VMEM)
    count, tokens = len(chunks), normed.shape[0]
    sums = list(sums)
    held = len(sums)
    units = sum(chunk.shape[1] for chunk in chunks) * BLOCK
    pieces = units // (2 * BLOCK)
    out = pl.pallas_call(
        lambda *refs: ffn_kernel(count, held == 0, *refs),
        in_specs=[local] * (2 + count + held),
        out_specs=[local] * (pieces + 2),
        out_shape=[jax.ShapeDtypeStruct((3, 2, BLOCK, WIDTH), BF)] * pieces
        + [jax.ShapeDtypeStruct((tokens, WIDTH), F32)] * 2,
        input_output_aliases={2 + count + i: pieces + i for i in range(held)},
        compiler_params=pltpu.CompilerParams(vmem_limit_bytes=16 * 2**20),
        cost_estimate=pl.CostEstimate(
            flops=18 * tokens * units * WIDTH,
            transcendentals=tokens * units,
            bytes_accessed=12 * units * WIDTH,
        ),
        name="ffn_chunks",
    )(normed, cot, *chunks, *sums)
    return out[:pieces], out[pieces:]


def rope_tables(seg):
    places = jnp.arange(TOK)
    allowed = (seg[:, :, None] == seg[:, None, :]) & (places[None, :] <= places[:, None])
    position = jnp.sum(allowed.astype(F32), axis=-1) - 1.0
    freqs = THETA ** (-2.0 * jnp.arange(HEAD_DIM // 2).astype(F32) / HEAD_DIM)
    angles = freqs[:, None] * position.reshape(1, -1)
    return jnp.cos(angles), jnp.sin(angles)


def inv_rms(values):
    return lax.rsqrt(jnp.mean(values * values, axis=-1, keepdims=True) + EPS)


def norm_back(grad_normed, source, inverse, gain_vec):
    scaled = source * inverse
    grad_scaled = grad_normed * gain_vec
    grad_gain = jnp.sum(grad_normed * scaled, axis=0, keepdims=True)
    mean = jnp.mean(grad_scaled * scaled, axis=-1, keepdims=True)
    return inverse * (grad_scaled - scaled * mean), grad_gain


def dot(left, right, dims):
    return lax.dot_general(left, right, (dims, ((), ())), preferred_element_type=F32)


NT = ((1,), (1,))
NN = ((1,), (0,))
TN = ((0,), (0,))


def total(parts):
    out = parts[0].astype(F32)
    for part in parts[1:]:
        out = out + part.astype(F32)
    return out


def body(tokens, segment_ids, attn_weight, gate_up, down_weight, norm_gains, cotangent):
    z, y, x, c = (lax.axis_index(a) for a in AXES)
    rows = MICRO * TOK

    gain_row = jnp.pad(norm_gains[None, :], ((0, 15), (0, WIDTH - 15)))
    shard = jnp.concatenate([attn_weight, gate_up[0], gate_up[1], down_weight, gain_row], axis=0)
    near = jnp.stack(fetch_ordered(shard, shift_x))
    ffn_block = near[:, 20:80].reshape(4, 3, 20, WIDTH).transpose(1, 0, 2, 3).reshape(3, BLOCK, WIDTH)
    head = jnp.concatenate([near[:, :20], near[:, 80:81]], axis=1)
    head = lax.dynamic_slice_in_dim(jnp.concatenate([head, head], axis=0), lax.rem(4 - x, 4), 4, axis=0)
    other = permute(head, shift_core())
    both = jnp.stack([jnp.where(c == 0, head, other), jnp.where(c == 0, other, head)], axis=1)
    attn_half = lax.dynamic_slice_in_dim(both[:, :, :20].reshape(2 * BLOCK, WIDTH), c * BLOCK, BLOCK, axis=0)
    gain_near = jnp.pad(both[:, :, 20, :15].reshape(1, 120), ((0, 15), (0, WIDTH - 120)))
    attn_block = jnp.concatenate([attn_half, gain_near], axis=0)

    block = jnp.concatenate([attn_block, ffn_block.reshape(3 * BLOCK, WIDTH)], axis=0)
    got = fetch_ordered(block, lambda s: shift_plane(s, True))
    attn_one = jnp.stack([part[:96] for part in got])
    ffn_got = [part[96:].reshape(3, BLOCK, WIDTH) for part in got]
    zero_low, zero_high = jnp.stack(ffn_got[:2], axis=1), jnp.stack(ffn_got[2:], axis=1)
    own = fetch_ordered(attn_one, lambda s: shift_plane(s, False))
    sib = [permute(v, shift_core()) for v in own]
    where = jnp.stack([z, y, c]).astype(jnp.int32)

    next_low = permute(zero_low, shift_plane(-1, False))
    last_high = permute(zero_high, shift_plane(1, False))
    next_high = permute(zero_high, shift_plane(-1, False))
    last_low = permute(zero_low, shift_plane(1, False))
    where, next_low, last_high = lax.optimization_barrier((where, next_low, last_high))

    live = (segment_ids.reshape(rows, 1) < TOK).astype(F32)
    cot = cotangent.reshape(rows, WIDTH)
    grad_mlp = (live * cot.astype(F32)).astype(BF)
    grad_mlp_all = jnp.concatenate([grad_mlp, permute(grad_mlp, shift_core())], axis=0)
    cosine, sine = rope_tables(segment_ids)
    flat_tokens = tokens.reshape(rows, WIDTH)
    weights, normed_one, heads, probs, att, hidden, normed_two, gains = attn_forward(
        where, flat_tokens, segment_ids, live, cosine, sine, own, sib
    )

    normed_all = jnp.concatenate([normed_two, permute(normed_two, shift_core())], axis=0)
    far_low = permute(next_low, shift_plane(-1, False))
    far_high = permute(last_high, shift_plane(1, False))
    zero_grads, sums = ffn(normed_all, grad_mlp_all, [zero_low, zero_high], [])
    near_grads, sums = ffn(normed_all, grad_mlp_all, [next_low, next_high, last_low, last_high], sums)
    next_low, next_high, last_low, last_high = near_grads
    next_high, last_low, far_low, far_high = lax.optimization_barrier((next_high, last_low, far_low, far_high))
    (grad_low,), sums = ffn(normed_all, grad_mlp_all, [far_low], sums)
    (grad_high,), (branch, grad_normed) = ffn(normed_all, grad_mlp_all, [far_high], sums)
    back_other = permute(grad_normed[rows:].astype(BF), shift_core())
    next_high_got = permute(next_high, shift_plane(1, False))
    last_low_got = permute(last_low, shift_plane(-1, False))
    back_other, next_high_got, last_low_got = lax.optimization_barrier((back_other, next_high_got, last_low_got))
    branch = branch[:rows] + permute(branch[rows:].astype(BF), shift_core()).astype(F32)
    result = (hidden + live * branch).astype(BF)

    ours, theirs, grad_hidden, grad_proj, gain_grads = attn_backward(
        where, grad_normed, back_other, hidden, gains, cot, live, weights, heads, probs, att, normed_one, cosine, sine
    )
    far_low = permute(grad_low, shift_plane(1, False))
    far_high = permute(grad_high, shift_plane(-1, False))
    theirs, far_low, far_high = lax.optimization_barrier((theirs, far_low, far_high))
    next_low_got = permute(total([next_low, far_low]).astype(BF), shift_plane(1, False))
    last_high_got = permute(total([last_high, far_high]).astype(BF), shift_plane(-1, False))
    swapped = permute(theirs, shift_core())
    grad_inputs, gain_grads = attn_inputs(grad_proj, weights, flat_tokens, gains, grad_hidden, gain_grads)
    gain_grads = gain_grads[:2]

    def exchange(blocks, gain_grads, make):
        count = blocks.shape[1]
        low = jnp.pad(gain_grads.astype(BF), ((0, 14), (0, 0)))
        got = [permute(jnp.concatenate([blocks[r], low], axis=0), make(r)) for r in (1, 3, 2)]
        blocks = total([blocks[0]] + [part[:count] for part in got])
        return blocks, total([gain_grads] + [part[count : count + 2] for part in got])

    attn_mine = total([ours, swapped]).astype(BF).reshape(4, 4 * BLOCK, WIDTH)
    attn_mine, next_low_got, last_high_got = lax.optimization_barrier((attn_mine, next_low_got, last_high_got))
    attn_next, gain_grads = exchange(attn_mine, gain_grads, lambda r: shift_plane(r, False))
    low_mine = total([zero_grads[0], next_low_got, last_low_got]).astype(BF)
    high_mine = total([zero_grads[1], next_high_got, last_high_got]).astype(BF)
    attn_next = attn_next.astype(BF).reshape(4, BLOCK, WIDTH)
    low_gains = jnp.pad(gain_grads.astype(BF), ((0, 14), (0, 0)))

    def rows_for(r):
        ffn_rows = (low_mine if r < 2 else high_mine)[:, r % 2].reshape(3 * BLOCK, WIDTH)
        return jnp.concatenate([ffn_rows, attn_next[r], low_gains], axis=0)

    got = [permute(rows_for(r), shift_plane(r, True)) for r in (1, 3, 2)]
    kept, *sent = x_payloads(jnp.stack([x, x, x]).astype(jnp.int32), rows_for(0), got, gain_grads)
    got = [permute(sent[r - 1], shift_x(r)) for r in (1, 3, 2)]
    mine = total([kept] + got)
    ffn_owned = mine[:60].reshape(3, 20, WIDTH)
    attn_owned = permute(mine[60:80], to_owner())
    gain_grads = mine[80:82]
    gain_grads = gain_grads + permute(gain_grads, shift_core())
    gain_owned = lax.dynamic_slice_in_dim(gain_grads.reshape(2 * WIDTH), flat_index(z, y, x, c) * 15, 15)
    return (
        result.reshape(MICRO, TOK, WIDTH),
        grad_inputs.reshape(MICRO, TOK, WIDTH),
        attn_owned,
        ffn_owned[:2],
        ffn_owned[2],
        gain_owned,
    )


def flat_index(z, y, x, c):
    return ((z * 4 + y) * 4 + x) * 2 + c


def solution(mesh):
    grid = Mesh(mesh.devices.reshape(4, 4, 4, 2), AXES)
    return jax.shard_map(
        body,
        mesh=grid,
        in_specs=(
            P(None, AXES, None),
            P(None, AXES),
            P(AXES, None),
            P(None, AXES, None),
            P(AXES, None),
            P(AXES),
            P(None, AXES, None),
        ),
        out_specs=(
            P(None, AXES, None),
            P(None, AXES, None),
            P(AXES, None),
            P(None, AXES, None),
            P(AXES, None),
            P(AXES),
        ),
        check_vma=False,
    )
```

```python
import jax
import jax.numpy as jnp
from jax import lax
from jax.experimental import pallas as pl
from jax.experimental.pallas import tpu as pltpu
from jax.sharding import Mesh, PartitionSpec as P

HEADS = 15
KV_HEADS = 5
GROUP = HEADS // KV_HEADS
HEAD_DIM = 64
MICRO = 2
WIDTH = 960
TOK = 128
BLOCK = 80
EPS = 1e-05
THETA = 100000.0
NEG_FILL = -1e30
AXES = ("z", "y", "x", "c")
BF = jnp.bfloat16
F32 = jnp.float32


def flat(z, y, x, c):
    return (((z % 4) * 4 + y % 4) * 4 + x % 4) * 2 + c % 2


def everywhere():
    return [(z, y, x, c) for z in range(4) for y in range(4) for x in range(4) for c in range(2)]


def shift_x(step):
    return [(flat(*d), flat(d[0], d[1], d[2] + step, d[3])) for d in everywhere()]


def shift_core():
    return [(flat(*d), flat(d[0], d[1], d[2], d[3] + 1)) for d in everywhere()]


def shift_plane(step, inner):
    pairs = []
    for z, y, x, c in everywhere():
        along_y = (c == 0) == inner
        pairs.append((flat(z, y, x, c), flat(z, y + step, x, c) if along_y else flat(z + step, y, x, c)))
    return pairs


def to_owner():
    return [(flat(z, y, j, c), flat(z, y, 2 * c + j // 2, j % 2)) for z, y, j, c in everywhere()]


def permute(value, pairs):
    return lax.ppermute(value, AXES, pairs)


def fetch(value, make):
    return [value] + [permute(value, make(-r)) for r in (1, 3, 2)]


def fetch_ordered(value, make):
    got = fetch(value, make)
    return [got[0], got[1], got[3], got[2]]


def move_rows(where_ref, own, sib, weights, gains):
    z, y, c = where_ref[0], where_ref[1], where_ref[2]
    for r2 in range(4):
        for r1 in range(4):
            for which, group in enumerate((own, sib)):
                core = c if which == 0 else 1 - c
                rz = jnp.where(core == 0, r2, r1)
                ry = jnp.where(core == 0, r1, r2)
                row = lax.rem(z + rz, 4) * 4 + lax.rem(y + ry, 4)
                weights[row, core] = group[r2][r1, 0:BLOCK]
                if which == 0:
                    gains[row] = group[r2][r1, BLOCK : BLOCK + 16]


def unpack_gains(gains):
    raw = gains[:, 0, 0:128].astype(BF)
    lane = lax.broadcasted_iota(jnp.int32, (128, WIDTH), 1)
    entry = lax.broadcasted_iota(jnp.int32, (128, WIDTH), 0)
    pick = jnp.where(lane - ((lane * 8739) >> 20) * 120 == entry, 1.0, 0.0).astype(BF)
    spread = dot(raw, pick, NN)
    lane = lax.broadcasted_iota(jnp.int32, (16, WIDTH), 1)
    row = lax.broadcasted_iota(jnp.int32, (16, WIDTH), 0)
    block = (lane * 8739) >> 20
    attn = jnp.sum(jnp.where(row == block, spread, 0.0), axis=0, keepdims=True)
    mlp = jnp.sum(jnp.where(row == block + 8, spread, 0.0), axis=0, keepdims=True)
    return attn, mlp


def heads_of(ref, kv, b):
    lanes = slice(TOK * b, TOK * (b + 1))
    parts = [ref[HEAD_DIM * h : HEAD_DIM * (h + 1), lanes] for h in range(GROUP * kv, GROUP * (kv + 1))]
    return jnp.concatenate(parts, axis=1)


def turn(values, cosine, sine):
    split = values.reshape(-1, 2, HEAD_DIM // 2, values.shape[-1])
    former, latter = split[:, 0], split[:, 1]
    turned = jnp.stack([former * cosine - latter * sine, latter * cosine + former * sine], axis=1)
    return turned.reshape(values.shape)


def attn_forward_kernel(where_ref, tokens, seg_col, seg_row, live, cosine, sine, *refs):
    own, sib = refs[0:4], refs[4:8]
    weights, normed, heads, probs, att, hidden, normed_two, gain_out, gains = refs[8:]
    move_rows(where_ref, own, sib, weights, gains)
    inputs = tokens[...].astype(F32)
    scaled = inputs * inv_rms(inputs)
    gain_attn, gain_mlp = unpack_gains(gains)
    gain_out[...] = jnp.concatenate([gain_attn, gain_mlp, jnp.zeros((6, WIDTH), F32)], axis=0)
    normed[...] = (scaled * gain_attn).astype(BF)
    rows = WIDTH + KV_HEADS * HEAD_DIM
    projected = dot(weights[0:10].reshape(-1, WIDTH), normed[...], NT)
    heads[0:rows] = turn(projected[0:rows], cosine[...], sine[...]).astype(BF)
    heads[rows:] = projected[rows:].astype(BF)
    key_place = lax.broadcasted_iota(jnp.int32, (TOK, TOK), 0)
    query_place = lax.broadcasted_iota(jnp.int32, (TOK, TOK), 1)
    for b in range(MICRO):
        lanes = slice(TOK * b, TOK * (b + 1))
        same = seg_col[lanes, :] == seg_row[b : b + 1, :]
        allowed = jnp.where(same & (key_place <= query_place), 1.0, 0.0)
        allowed = jnp.concatenate([allowed] * GROUP, axis=1)
        for kv in range(KV_HEADS):
            key = heads[WIDTH + HEAD_DIM * kv : WIDTH + HEAD_DIM * (kv + 1), lanes]
            value = heads[rows + HEAD_DIM * kv : rows + HEAD_DIM * (kv + 1), lanes]
            scores = dot(key, heads_of(heads, kv, b), TN) * HEAD_DIM ** (-0.5)
            scores = jnp.where(allowed > 0.5, scores, NEG_FILL)
            expd = jnp.exp(scores - jnp.max(scores, axis=0, keepdims=True))
            prob = expd / jnp.sum(expd, axis=0, keepdims=True)
            probs[b * KV_HEADS + kv] = prob
            attended = dot(value, prob.astype(BF), NN).astype(BF)
            for g in range(GROUP):
                h = GROUP * kv + g
                att[HEAD_DIM * h : HEAD_DIM * (h + 1), lanes] = attended[:, TOK * g : TOK * (g + 1)]
    total_hidden = inputs + live[...] * dot(att[...], weights[10:16].reshape(WIDTH, WIDTH), TN)
    hidden[...] = total_hidden
    normed_two[...] = (total_hidden * inv_rms(total_hidden) * gain_mlp).astype(BF)


def attn_forward(where, tokens, segment_ids, live, cosine, sine, own, sib):
    local = pl.BlockSpec(memory_space=pltpu.VMEM)
    rows = tokens.shape[0]
    qkv_rows = WIDTH + 2 * KV_HEADS * HEAD_DIM
    return pl.pallas_call(
        attn_forward_kernel,
        in_specs=[pl.BlockSpec(memory_space=pltpu.SMEM)] + [local] * 14,
        out_specs=[local] * 8,
        out_shape=[
            jax.ShapeDtypeStruct((16, 2, BLOCK, WIDTH), BF),
            jax.ShapeDtypeStruct((rows, WIDTH), BF),
            jax.ShapeDtypeStruct((qkv_rows, rows), BF),
            jax.ShapeDtypeStruct((MICRO * KV_HEADS, TOK, GROUP * TOK), F32),
            jax.ShapeDtypeStruct((WIDTH, rows), BF),
            jax.ShapeDtypeStruct((rows, WIDTH), F32),
            jax.ShapeDtypeStruct((rows, WIDTH), BF),
            jax.ShapeDtypeStruct((8, WIDTH), F32),
        ],
        scratch_shapes=[pltpu.VMEM((16, 16, WIDTH), BF)],
        compiler_params=pltpu.CompilerParams(vmem_limit_bytes=12 * 2**20),
        name="attn_forward",
    )(where, tokens, segment_ids.reshape(rows, 1), segment_ids, live, cosine, sine, *own, *sib)


def attn_backward_kernel(where_ref, back, back_other, hidden, gains, cot, live, weights, heads, probs, att, normed, cosine, sine,
                         ours, theirs, grad_hidden, grad_proj, gain_grad, raw):
    z, y, c = where_ref[0], where_ref[1], where_ref[2]
    rows = hidden.shape[0]
    grad_normed = back[0:rows] + back_other[...].astype(F32)
    grad, gain_mlp = norm_back(grad_normed, hidden[...], inv_rms(hidden[...]), gains[1:2])
    grad = cot[...].astype(F32) + grad
    grad_hidden[...] = grad
    gain_grad[...] = jnp.concatenate([jnp.zeros((1, WIDTH), F32), gain_mlp, jnp.zeros((6, WIDTH), F32)], axis=0)
    branch = (live[...] * grad).astype(BF)
    grad_att = dot(weights[10:16].reshape(WIDTH, WIDTH), branch, NT).astype(BF)
    base = WIDTH + KV_HEADS * HEAD_DIM
    for b in range(MICRO):
        lanes = slice(TOK * b, TOK * (b + 1))
        for kv in range(KV_HEADS):
            key = heads[WIDTH + HEAD_DIM * kv : WIDTH + HEAD_DIM * (kv + 1), lanes]
            value = heads[base + HEAD_DIM * kv : base + HEAD_DIM * (kv + 1), lanes]
            query, grad_out = heads_of(heads, kv, b), heads_of(grad_att, kv, b)
            prob = probs[b * KV_HEADS + kv]
            grad_prob = dot(value, grad_out, TN)
            delta = jnp.sum(prob * grad_prob, axis=0, keepdims=True)
            grad_score = (HEAD_DIM ** (-0.5) * prob * (grad_prob - delta)).astype(BF)
            grad_query = dot(key, grad_score, NN)
            for g in range(GROUP):
                h = GROUP * kv + g
                raw[HEAD_DIM * h : HEAD_DIM * (h + 1), lanes] = grad_query[:, TOK * g : TOK * (g + 1)]
            raw[WIDTH + HEAD_DIM * kv : WIDTH + HEAD_DIM * (kv + 1), lanes] = dot(query, grad_score, NT)
            raw[base + HEAD_DIM * kv : base + HEAD_DIM * (kv + 1), lanes] = dot(grad_out, prob.astype(BF), NT)
    grad_proj[0:base] = turn(raw[0:base], cosine[...], -sine[...]).astype(BF)
    grad_proj[base:] = raw[base:].astype(BF)

    jobs = [(grad_proj, 0, 640, normed[...]), (grad_proj, 640, 640, normed[...]), (grad_proj, 1280, 320, normed[...])]
    jobs += [(att, 0, 640, branch), (att, 640, 320, branch)]
    row = 0
    for source, start, size, right in jobs:
        block = dot(source[start : start + size], right, NN).astype(BF)
        for k in range(size // 160):
            rz = lax.rem(row // 4 - z + 4, 4)
            ry = lax.rem(row % 4 - y + 4, 4)
            zy, yz = rz * 4 + ry, ry * 4 + rz
            lower = block[160 * k : 160 * k + 80]
            upper = block[160 * k + 80 : 160 * k + 160]

            @pl.when(c == 0)
            def _(lower=lower, upper=upper, zy=zy, yz=yz):
                ours[zy] = lower
                theirs[yz] = upper

            @pl.when(c != 0)
            def _(lower=lower, upper=upper, zy=zy, yz=yz):
                ours[yz] = upper
                theirs[zy] = lower

            row += 1


def attn_backward(where, back, back_other, hidden, gains, cot, live, weights, heads, probs, att, normed, cosine, sine):
    local = pl.BlockSpec(memory_space=pltpu.VMEM)
    return pl.pallas_call(
        attn_backward_kernel,
        in_specs=[pl.BlockSpec(memory_space=pltpu.SMEM)] + [local] * 13,
        out_specs=[local] * 5,
        out_shape=[
            jax.ShapeDtypeStruct((16, BLOCK, WIDTH), BF),
            jax.ShapeDtypeStruct((16, BLOCK, WIDTH), BF),
            jax.ShapeDtypeStruct(hidden.shape, F32),
            jax.ShapeDtypeStruct(heads.shape, BF),
            jax.ShapeDtypeStruct((8, WIDTH), F32),
        ],
        scratch_shapes=[pltpu.VMEM(heads.shape, F32)],
        compiler_params=pltpu.CompilerParams(vmem_limit_bytes=16 * 2**20),
        name="attn_backward",
    )(where, back, back_other, hidden, gains, cot, live, weights, heads, probs, att, normed, cosine, sine)


def attn_inputs_kernel(grad_proj, weights, tokens, gains, grad_hidden, gain_grad, grad_inputs, gain_out):
    inputs = tokens[...].astype(F32)
    grad_normed = dot(grad_proj[...], weights[0:10].reshape(-1, WIDTH), TN)
    grad, gain_attn = norm_back(grad_normed, inputs, inv_rms(inputs), gains[0:1])
    grad_inputs[...] = (grad_hidden[...] + grad).astype(BF)
    gain_out[...] = gain_grad[...] + jnp.concatenate([gain_attn, jnp.zeros((7, WIDTH), F32)], axis=0)


def attn_inputs(grad_proj, weights, tokens, gains, grad_hidden, gain_grad):
    local = pl.BlockSpec(memory_space=pltpu.VMEM)
    return pl.pallas_call(
        attn_inputs_kernel,
        in_specs=[local] * 6,
        out_specs=[local] * 2,
        out_shape=[jax.ShapeDtypeStruct(tokens.shape, BF), jax.ShapeDtypeStruct((8, WIDTH), F32)],
        compiler_params=pltpu.CompilerParams(vmem_limit_bytes=12 * 2**20),
        name="attn_inputs",
    )(grad_proj, weights, tokens, gains, grad_hidden, gain_grad)


def x_payloads_kernel(where_ref, own, got_a, got_b, got_c, gains, kept, sent_a, sent_b, sent_c, blocks):
    rows = 4 * BLOCK
    mine = own[0:rows].astype(F32)
    gain = gains[...]
    for part in (got_a, got_b, got_c):
        mine = mine + part[0:rows].astype(F32)
        gain = gain + part[rows : rows + 2].astype(F32)
    for j in range(4):
        blocks[j, 0:20] = mine[3 * BLOCK + 20 * j : 3 * BLOCK + 20 * j + 20]
    for r in range(4):
        pieces = [mine[BLOCK * w + 20 * r : BLOCK * w + 20 * r + 20] for w in range(3)]
        pieces += [blocks[lax.rem(where_ref[0] + r, 4)][0:20], gain]
        block = jnp.concatenate(pieces, axis=0)
        if r == 0:
            kept[...] = block
        else:
            (sent_a, sent_b, sent_c)[r - 1][...] = block.astype(BF)


def x_payloads(where, own, got, gains):
    local = pl.BlockSpec(memory_space=pltpu.VMEM)
    return pl.pallas_call(
        x_payloads_kernel,
        in_specs=[pl.BlockSpec(memory_space=pltpu.SMEM)] + [local] * 5,
        out_specs=[local] * 4,
        out_shape=[jax.ShapeDtypeStruct((82, WIDTH), F32)] + [jax.ShapeDtypeStruct((82, WIDTH), BF)] * 3,
        scratch_shapes=[pltpu.VMEM((4, 24, WIDTH), F32)],
        compiler_params=pltpu.CompilerParams(vmem_limit_bytes=12 * 2**20),
        name="x_payloads",
    )(where, own, *got, gains)


def ffn_kernel(count, first, normed, cot, *refs):
    chunks, refs = refs[:count], refs[count:]
    if first:
        branch, back = 0.0, 0.0
    else:
        branch, back = refs[0][...], refs[1][...]
        refs = refs[2:]
    grads, branch_out, back_out = list(refs[:-2]), refs[-2], refs[-1]
    step = 2 * BLOCK
    for chunk in chunks:
        parts = chunk.shape[1]
        half = parts * BLOCK
        pair = chunk[0:2].reshape(2 * half, WIDTH)
        down = chunk[2].reshape(half, WIDTH)
        both = dot(pair, normed[...], NT)
        grad_prod = dot(down, cot[...], NT)
        gate, up = both[:half], both[half:]
        sigma = 1.0 / (1.0 + jnp.exp(-gate))
        gated = gate * sigma
        product = (gated * up).astype(BF)
        grad_gate = (grad_prod * up * sigma * (1.0 + gate * (1.0 - sigma))).astype(BF)
        grad_up = (grad_prod * gated).astype(BF)
        grad_pair = jnp.concatenate([grad_gate, grad_up], axis=0)
        back = back + dot(grad_pair, pair, TN)
        pair_grad = dot(grad_pair, normed[...], NN).astype(BF)
        down_grad = dot(product, cot[...], NN).astype(BF)
        for at in range(0, half, step):
            grad = grads.pop(0)
            grad[0] = pair_grad[at : at + step].reshape(2, BLOCK, WIDTH)
            grad[1] = pair_grad[half + at : half + at + step].reshape(2, BLOCK, WIDTH)
            grad[2] = down_grad[at : at + step].reshape(2, BLOCK, WIDTH)
        branch = branch + dot(product, down, TN)
    branch_out[...] = branch
    back_out[...] = back


def ffn(normed, cot, chunks, sums):
    local = pl.BlockSpec(memory_space=pltpu.VMEM)
    count, tokens = len(chunks), normed.shape[0]
    sums = list(sums)
    held = len(sums)
    units = sum(chunk.shape[1] for chunk in chunks) * BLOCK
    pieces = units // (2 * BLOCK)
    out = pl.pallas_call(
        lambda *refs: ffn_kernel(count, held == 0, *refs),
        in_specs=[local] * (2 + count + held),
        out_specs=[local] * (pieces + 2),
        out_shape=[jax.ShapeDtypeStruct((3, 2, BLOCK, WIDTH), BF)] * pieces
        + [jax.ShapeDtypeStruct((tokens, WIDTH), F32)] * 2,
        input_output_aliases={2 + count + i: pieces + i for i in range(held)},
        compiler_params=pltpu.CompilerParams(vmem_limit_bytes=16 * 2**20),
        cost_estimate=pl.CostEstimate(
            flops=18 * tokens * units * WIDTH,
            transcendentals=tokens * units,
            bytes_accessed=12 * units * WIDTH,
        ),
        name="ffn_chunks",
    )(normed, cot, *chunks, *sums)
    return out[:pieces], out[pieces:]


def rope_tables(seg):
    places = jnp.arange(TOK)
    allowed = (seg[:, :, None] == seg[:, None, :]) & (places[None, :] <= places[:, None])
    position = jnp.sum(allowed.astype(F32), axis=-1) - 1.0
    freqs = THETA ** (-2.0 * jnp.arange(HEAD_DIM // 2).astype(F32) / HEAD_DIM)
    angles = freqs[:, None] * position.reshape(1, -1)
    return jnp.cos(angles), jnp.sin(angles)


def inv_rms(values):
    return lax.rsqrt(jnp.mean(values * values, axis=-1, keepdims=True) + EPS)


def norm_back(grad_normed, source, inverse, gain_vec):
    scaled = source * inverse
    grad_scaled = grad_normed * gain_vec
    grad_gain = jnp.sum(grad_normed * scaled, axis=0, keepdims=True)
    mean = jnp.mean(grad_scaled * scaled, axis=-1, keepdims=True)
    return inverse * (grad_scaled - scaled * mean), grad_gain


def dot(left, right, dims):
    return lax.dot_general(left, right, (dims, ((), ())), preferred_element_type=F32)


NT = ((1,), (1,))
NN = ((1,), (0,))
TN = ((0,), (0,))


def total(parts):
    out = parts[0].astype(F32)
    for part in parts[1:]:
        out = out + part.astype(F32)
    return out


def body(tokens, segment_ids, attn_weight, gate_up, down_weight, norm_gains, cotangent):
    z, y, x, c = (lax.axis_index(a) for a in AXES)
    rows = MICRO * TOK

    gain_row = jnp.pad(norm_gains[None, :], ((0, 15), (0, WIDTH - 15)))
    shard = jnp.concatenate([attn_weight, gate_up[0], gate_up[1], down_weight, gain_row], axis=0)
    near = jnp.stack(fetch_ordered(shard, shift_x))
    ffn_block = near[:, 20:80].reshape(4, 3, 20, WIDTH).transpose(1, 0, 2, 3).reshape(3, BLOCK, WIDTH)
    head = jnp.concatenate([near[:, :20], near[:, 80:81]], axis=1)
    head = lax.dynamic_slice_in_dim(jnp.concatenate([head, head], axis=0), lax.rem(4 - x, 4), 4, axis=0)
    other = permute(head, shift_core())
    both = jnp.stack([jnp.where(c == 0, head, other), jnp.where(c == 0, other, head)], axis=1)
    attn_half = lax.dynamic_slice_in_dim(both[:, :, :20].reshape(2 * BLOCK, WIDTH), c * BLOCK, BLOCK, axis=0)
    gain_near = jnp.pad(both[:, :, 20, :15].reshape(1, 120), ((0, 15), (0, WIDTH - 120)))
    attn_block = jnp.concatenate([attn_half, gain_near], axis=0)

    block = jnp.concatenate([attn_block, ffn_block.reshape(3 * BLOCK, WIDTH)], axis=0)
    got = fetch_ordered(block, lambda s: shift_plane(s, True))
    attn_one = jnp.stack([part[:96] for part in got])
    ffn_got = [part[96:].reshape(3, BLOCK, WIDTH) for part in got]
    zero_low, zero_high = jnp.stack(ffn_got[:2], axis=1), jnp.stack(ffn_got[2:], axis=1)
    own = fetch_ordered(attn_one, lambda s: shift_plane(s, False))
    sib = [permute(v, shift_core()) for v in own]
    where = jnp.stack([z, y, c]).astype(jnp.int32)

    next_low = permute(zero_low, shift_plane(-1, False))
    last_high = permute(zero_high, shift_plane(1, False))
    send_low, send_high, _ = lax.optimization_barrier((zero_low, zero_high, sib))
    next_high = permute(send_high, shift_plane(-1, False))
    last_low = permute(send_low, shift_plane(1, False))

    live = (segment_ids.reshape(rows, 1) < TOK).astype(F32)
    cot = cotangent.reshape(rows, WIDTH)
    grad_mlp = (live * cot.astype(F32)).astype(BF)
    grad_mlp_all = jnp.concatenate([grad_mlp, permute(grad_mlp, shift_core())], axis=0)
    cosine, sine = rope_tables(segment_ids)
    flat_tokens = tokens.reshape(rows, WIDTH)
    weights, normed_one, heads, probs, att, hidden, normed_two, gains = attn_forward(
        where, flat_tokens, segment_ids, live, cosine, sine, own, sib
    )

    normed_all = jnp.concatenate([normed_two, permute(normed_two, shift_core())], axis=0)
    forward_low, forward_high, _ = lax.optimization_barrier((next_low, last_high, normed_two))
    far_low = permute(forward_low, shift_plane(-1, False))
    far_high = permute(forward_high, shift_plane(1, False))
    zero_grads, sums = ffn(normed_all, grad_mlp_all, [zero_low, zero_high], [])
    near_grads, sums = ffn(normed_all, grad_mlp_all, [next_low, next_high, last_low, last_high], sums)
    next_low, next_high, last_low, last_high = near_grads
    next_high, last_low, far_low, far_high = lax.optimization_barrier((next_high, last_low, far_low, far_high))
    (grad_low,), sums = ffn(normed_all, grad_mlp_all, [far_low], sums)
    (grad_high,), (branch, grad_normed) = ffn(normed_all, grad_mlp_all, [far_high], sums)
    back_other = permute(grad_normed[rows:].astype(BF), shift_core())
    next_high_got = permute(next_high, shift_plane(1, False))
    last_low_got = permute(last_low, shift_plane(-1, False))
    back_other, next_high_got, last_low_got = lax.optimization_barrier((back_other, next_high_got, last_low_got))
    branch = branch[:rows] + permute(branch[rows:].astype(BF), shift_core()).astype(F32)
    result = (hidden + live * branch).astype(BF)

    ours, theirs, grad_hidden, grad_proj, gain_grads = attn_backward(
        where, grad_normed, back_other, hidden, gains, cot, live, weights, heads, probs, att, normed_one, cosine, sine
    )
    far_low = permute(grad_low, shift_plane(1, False))
    far_high = permute(grad_high, shift_plane(-1, False))
    theirs, far_low, far_high = lax.optimization_barrier((theirs, far_low, far_high))
    next_low_got = permute(total([next_low, far_low]).astype(BF), shift_plane(1, False))
    last_high_got = permute(total([last_high, far_high]).astype(BF), shift_plane(-1, False))
    swapped = permute(theirs, shift_core())
    grad_inputs, gain_grads = attn_inputs(grad_proj, weights, flat_tokens, gains, grad_hidden, gain_grads)
    gain_grads = gain_grads[:2]

    attn_mine = total([ours, swapped]).astype(BF).reshape(4, 4 * BLOCK, WIDTH)
    low_gains = jnp.pad(gain_grads.astype(BF), ((0, 14), (0, 0)))
    blocks = [jnp.concatenate([attn_mine[r], low_gains], axis=0) for r in (1, 3, 2)]
    got = [permute(block, shift_plane(r, False)) for block, r in zip(blocks, (1, 3, 2))]
    attn_next = total([attn_mine[0]] + [part[: 4 * BLOCK] for part in got])
    gain_grads = total([gain_grads] + [part[4 * BLOCK : 4 * BLOCK + 2] for part in got])
    next_low_got, last_high_got, _ = lax.optimization_barrier((next_low_got, last_high_got, attn_next))
    low_mine = total([zero_grads[0], next_low_got, last_low_got]).astype(BF)
    high_mine = total([zero_grads[1], next_high_got, last_high_got]).astype(BF)
    attn_next = attn_next.astype(BF).reshape(4, BLOCK, WIDTH)
    low_gains = jnp.pad(gain_grads.astype(BF), ((0, 14), (0, 0)))

    def rows_for(r):
        ffn_rows = (low_mine if r < 2 else high_mine)[:, r % 2].reshape(3 * BLOCK, WIDTH)
        return jnp.concatenate([ffn_rows, attn_next[r], low_gains], axis=0)

    got = [permute(rows_for(r), shift_plane(r, True)) for r in (1, 3, 2)]
    kept, *sent = x_payloads(jnp.stack([x, x, x]).astype(jnp.int32), rows_for(0), got, gain_grads)
    got = [permute(sent[r - 1], shift_x(r)) for r in (1, 3, 2)]
    mine = total([kept] + got)
    ffn_owned = mine[:60].reshape(3, 20, WIDTH)
    attn_owned = permute(mine[60:80], to_owner())
    gain_grads = mine[80:82]
    gain_grads = gain_grads + permute(gain_grads, shift_core())
    gain_owned = lax.dynamic_slice_in_dim(gain_grads.reshape(2 * WIDTH), flat_index(z, y, x, c) * 15, 15)
    return (
        result.reshape(MICRO, TOK, WIDTH),
        grad_inputs.reshape(MICRO, TOK, WIDTH),
        attn_owned,
        ffn_owned[:2],
        ffn_owned[2],
        gain_owned,
    )


def flat_index(z, y, x, c):
    return ((z * 4 + y) * 4 + x) * 2 + c


def solution(mesh):
    grid = Mesh(mesh.devices.reshape(4, 4, 4, 2), AXES)
    return jax.shard_map(
        body,
        mesh=grid,
        in_specs=(
            P(None, AXES, None),
            P(None, AXES),
            P(AXES, None),
            P(None, AXES, None),
            P(AXES, None),
            P(AXES),
            P(None, AXES, None),
        ),
        out_specs=(
            P(None, AXES, None),
            P(None, AXES, None),
            P(AXES, None),
            P(None, AXES, None),
            P(AXES, None),
            P(AXES),
        ),
        check_vma=False,
    )
```

```python
import jax
import jax.numpy as jnp
from jax import lax
from jax.experimental import pallas as pl
from jax.experimental.pallas import tpu as pltpu
from jax.sharding import Mesh, PartitionSpec as P

HEADS = 15
KV_HEADS = 5
GROUP = HEADS // KV_HEADS
HEAD_DIM = 64
MICRO = 2
WIDTH = 960
TOK = 128
BLOCK = 80
EPS = 1e-05
THETA = 100000.0
NEG_FILL = -1e30
AXES = ("z", "y", "x", "c")
BF = jnp.bfloat16
F32 = jnp.float32


def flat(z, y, x, c):
    return (((z % 4) * 4 + y % 4) * 4 + x % 4) * 2 + c % 2


def everywhere():
    return [(z, y, x, c) for z in range(4) for y in range(4) for x in range(4) for c in range(2)]


def shift_x(step):
    return [(flat(*d), flat(d[0], d[1], d[2] + step, d[3])) for d in everywhere()]


def shift_core():
    return [(flat(*d), flat(d[0], d[1], d[2], d[3] + 1)) for d in everywhere()]


def shift_plane(step, inner):
    pairs = []
    for z, y, x, c in everywhere():
        along_y = (c == 0) == inner
        pairs.append((flat(z, y, x, c), flat(z, y + step, x, c) if along_y else flat(z + step, y, x, c)))
    return pairs


def to_owner():
    return [(flat(z, y, j, c), flat(z, y, 2 * c + j // 2, j % 2)) for z, y, j, c in everywhere()]


def permute(value, pairs):
    return lax.ppermute(value, AXES, pairs)


def fetch(value, make):
    return [value] + [permute(value, make(-r)) for r in (1, 3, 2)]


def fetch_ordered(value, make):
    got = fetch(value, make)
    return [got[0], got[1], got[3], got[2]]


def move_rows(where_ref, own, sib, weights, gains):
    z, y, c = where_ref[0], where_ref[1], where_ref[2]
    for r2 in range(4):
        for r1 in range(4):
            for which, group in enumerate((own, sib)):
                core = c if which == 0 else 1 - c
                rz = jnp.where(core == 0, r2, r1)
                ry = jnp.where(core == 0, r1, r2)
                row = lax.rem(z + rz, 4) * 4 + lax.rem(y + ry, 4)
                weights[row, core] = group[r2][r1, 0:BLOCK]
                if which == 0:
                    gains[row] = group[r2][r1, BLOCK : BLOCK + 16]


def unpack_gains(gains):
    raw = gains[:, 0, 0:128].astype(BF)
    lane = lax.broadcasted_iota(jnp.int32, (128, WIDTH), 1)
    entry = lax.broadcasted_iota(jnp.int32, (128, WIDTH), 0)
    pick = jnp.where(lane - ((lane * 8739) >> 20) * 120 == entry, 1.0, 0.0).astype(BF)
    spread = dot(raw, pick, NN)
    lane = lax.broadcasted_iota(jnp.int32, (16, WIDTH), 1)
    row = lax.broadcasted_iota(jnp.int32, (16, WIDTH), 0)
    block = (lane * 8739) >> 20
    attn = jnp.sum(jnp.where(row == block, spread, 0.0), axis=0, keepdims=True)
    mlp = jnp.sum(jnp.where(row == block + 8, spread, 0.0), axis=0, keepdims=True)
    return attn, mlp


def heads_of(ref, kv, b):
    lanes = slice(TOK * b, TOK * (b + 1))
    parts = [ref[HEAD_DIM * h : HEAD_DIM * (h + 1), lanes] for h in range(GROUP * kv, GROUP * (kv + 1))]
    return jnp.concatenate(parts, axis=1)


def turn(values, cosine, sine):
    split = values.reshape(-1, 2, HEAD_DIM // 2, values.shape[-1])
    former, latter = split[:, 0], split[:, 1]
    turned = jnp.stack([former * cosine - latter * sine, latter * cosine + former * sine], axis=1)
    return turned.reshape(values.shape)


def attn_forward_kernel(where_ref, tokens, seg_col, seg_row, live, cosine, sine, *refs):
    own, sib = refs[0:4], refs[4:8]
    weights, normed, heads, probs, att, hidden, normed_two, gain_out, gains = refs[8:]
    move_rows(where_ref, own, sib, weights, gains)
    inputs = tokens[...].astype(F32)
    scaled = inputs * inv_rms(inputs)
    gain_attn, gain_mlp = unpack_gains(gains)
    gain_out[...] = jnp.concatenate([gain_attn, gain_mlp, jnp.zeros((6, WIDTH), F32)], axis=0)
    normed[...] = (scaled * gain_attn).astype(BF)
    rows = WIDTH + KV_HEADS * HEAD_DIM
    projected = dot(weights[0:10].reshape(-1, WIDTH), normed[...], NT)
    heads[0:rows] = turn(projected[0:rows], cosine[...], sine[...]).astype(BF)
    heads[rows:] = projected[rows:].astype(BF)
    key_place = lax.broadcasted_iota(jnp.int32, (TOK, TOK), 0)
    query_place = lax.broadcasted_iota(jnp.int32, (TOK, TOK), 1)
    for b in range(MICRO):
        lanes = slice(TOK * b, TOK * (b + 1))
        same = seg_col[lanes, :] == seg_row[b : b + 1, :]
        allowed = jnp.where(same & (key_place <= query_place), 1.0, 0.0)
        allowed = jnp.concatenate([allowed] * GROUP, axis=1)
        for kv in range(KV_HEADS):
            key = heads[WIDTH + HEAD_DIM * kv : WIDTH + HEAD_DIM * (kv + 1), lanes]
            value = heads[rows + HEAD_DIM * kv : rows + HEAD_DIM * (kv + 1), lanes]
            scores = dot(key, heads_of(heads, kv, b), TN) * HEAD_DIM ** (-0.5)
            scores = jnp.where(allowed > 0.5, scores, NEG_FILL)
            expd = jnp.exp(scores - jnp.max(scores, axis=0, keepdims=True))
            prob = expd / jnp.sum(expd, axis=0, keepdims=True)
            probs[b * KV_HEADS + kv] = prob
            attended = dot(value, prob.astype(BF), NN).astype(BF)
            for g in range(GROUP):
                h = GROUP * kv + g
                att[HEAD_DIM * h : HEAD_DIM * (h + 1), lanes] = attended[:, TOK * g : TOK * (g + 1)]
    total_hidden = inputs + live[...] * dot(att[...], weights[10:16].reshape(WIDTH, WIDTH), TN)
    hidden[...] = total_hidden
    normed_two[...] = (total_hidden * inv_rms(total_hidden) * gain_mlp).astype(BF)


def attn_forward(where, tokens, segment_ids, live, cosine, sine, own, sib):
    local = pl.BlockSpec(memory_space=pltpu.VMEM)
    rows = tokens.shape[0]
    qkv_rows = WIDTH + 2 * KV_HEADS * HEAD_DIM
    return pl.pallas_call(
        attn_forward_kernel,
        in_specs=[pl.BlockSpec(memory_space=pltpu.SMEM)] + [local] * 14,
        out_specs=[local] * 8,
        out_shape=[
            jax.ShapeDtypeStruct((16, 2, BLOCK, WIDTH), BF),
            jax.ShapeDtypeStruct((rows, WIDTH), BF),
            jax.ShapeDtypeStruct((qkv_rows, rows), BF),
            jax.ShapeDtypeStruct((MICRO * KV_HEADS, TOK, GROUP * TOK), F32),
            jax.ShapeDtypeStruct((WIDTH, rows), BF),
            jax.ShapeDtypeStruct((rows, WIDTH), F32),
            jax.ShapeDtypeStruct((rows, WIDTH), BF),
            jax.ShapeDtypeStruct((8, WIDTH), F32),
        ],
        scratch_shapes=[pltpu.VMEM((16, 16, WIDTH), BF)],
        compiler_params=pltpu.CompilerParams(vmem_limit_bytes=12 * 2**20),
        name="attn_forward",
    )(where, tokens, segment_ids.reshape(rows, 1), segment_ids, live, cosine, sine, *own, *sib)


def attn_backward_kernel(where_ref, back, back_other, hidden, gains, cot, live, weights, heads, probs, att, normed, cosine, sine,
                         ours, theirs, grad_hidden, grad_proj, gain_grad, raw):
    z, y, c = where_ref[0], where_ref[1], where_ref[2]
    rows = hidden.shape[0]
    grad_normed = back[0:rows] + back_other[...].astype(F32)
    grad, gain_mlp = norm_back(grad_normed, hidden[...], inv_rms(hidden[...]), gains[1:2])
    grad = cot[...].astype(F32) + grad
    grad_hidden[...] = grad
    gain_grad[...] = jnp.concatenate([jnp.zeros((1, WIDTH), F32), gain_mlp, jnp.zeros((6, WIDTH), F32)], axis=0)
    branch = (live[...] * grad).astype(BF)
    grad_att = dot(weights[10:16].reshape(WIDTH, WIDTH), branch, NT).astype(BF)
    base = WIDTH + KV_HEADS * HEAD_DIM
    for b in range(MICRO):
        lanes = slice(TOK * b, TOK * (b + 1))
        for kv in range(KV_HEADS):
            key = heads[WIDTH + HEAD_DIM * kv : WIDTH + HEAD_DIM * (kv + 1), lanes]
            value = heads[base + HEAD_DIM * kv : base + HEAD_DIM * (kv + 1), lanes]
            query, grad_out = heads_of(heads, kv, b), heads_of(grad_att, kv, b)
            prob = probs[b * KV_HEADS + kv]
            grad_prob = dot(value, grad_out, TN)
            delta = jnp.sum(prob * grad_prob, axis=0, keepdims=True)
            grad_score = (HEAD_DIM ** (-0.5) * prob * (grad_prob - delta)).astype(BF)
            grad_query = dot(key, grad_score, NN)
            for g in range(GROUP):
                h = GROUP * kv + g
                raw[HEAD_DIM * h : HEAD_DIM * (h + 1), lanes] = grad_query[:, TOK * g : TOK * (g + 1)]
            raw[WIDTH + HEAD_DIM * kv : WIDTH + HEAD_DIM * (kv + 1), lanes] = dot(query, grad_score, NT)
            raw[base + HEAD_DIM * kv : base + HEAD_DIM * (kv + 1), lanes] = dot(grad_out, prob.astype(BF), NT)
    grad_proj[0:base] = turn(raw[0:base], cosine[...], -sine[...]).astype(BF)
    grad_proj[base:] = raw[base:].astype(BF)

    jobs = [(grad_proj, 0, 640, normed[...]), (grad_proj, 640, 640, normed[...]), (grad_proj, 1280, 320, normed[...])]
    jobs += [(att, 0, 640, branch), (att, 640, 320, branch)]
    row = 0
    for source, start, size, right in jobs:
        block = dot(source[start : start + size], right, NN).astype(BF)
        for k in range(size // 160):
            rz = lax.rem(row // 4 - z + 4, 4)
            ry = lax.rem(row % 4 - y + 4, 4)
            zy, yz = rz * 4 + ry, ry * 4 + rz
            lower = block[160 * k : 160 * k + 80]
            upper = block[160 * k + 80 : 160 * k + 160]

            @pl.when(c == 0)
            def _(lower=lower, upper=upper, zy=zy, yz=yz):
                ours[zy] = lower
                theirs[yz] = upper

            @pl.when(c != 0)
            def _(lower=lower, upper=upper, zy=zy, yz=yz):
                ours[yz] = upper
                theirs[zy] = lower

            row += 1


def attn_backward(where, back, back_other, hidden, gains, cot, live, weights, heads, probs, att, normed, cosine, sine):
    local = pl.BlockSpec(memory_space=pltpu.VMEM)
    return pl.pallas_call(
        attn_backward_kernel,
        in_specs=[pl.BlockSpec(memory_space=pltpu.SMEM)] + [local] * 13,
        out_specs=[local] * 5,
        out_shape=[
            jax.ShapeDtypeStruct((16, BLOCK, WIDTH), BF),
            jax.ShapeDtypeStruct((16, BLOCK, WIDTH), BF),
            jax.ShapeDtypeStruct(hidden.shape, F32),
            jax.ShapeDtypeStruct(heads.shape, BF),
            jax.ShapeDtypeStruct((8, WIDTH), F32),
        ],
        scratch_shapes=[pltpu.VMEM(heads.shape, F32)],
        compiler_params=pltpu.CompilerParams(vmem_limit_bytes=16 * 2**20),
        name="attn_backward",
    )(where, back, back_other, hidden, gains, cot, live, weights, heads, probs, att, normed, cosine, sine)


def attn_inputs_kernel(grad_proj, weights, tokens, gains, grad_hidden, gain_grad, grad_inputs, gain_out):
    inputs = tokens[...].astype(F32)
    grad_normed = dot(grad_proj[...], weights[0:10].reshape(-1, WIDTH), TN)
    grad, gain_attn = norm_back(grad_normed, inputs, inv_rms(inputs), gains[0:1])
    grad_inputs[...] = (grad_hidden[...] + grad).astype(BF)
    gain_out[...] = gain_grad[...] + jnp.concatenate([gain_attn, jnp.zeros((7, WIDTH), F32)], axis=0)


def attn_inputs(grad_proj, weights, tokens, gains, grad_hidden, gain_grad):
    local = pl.BlockSpec(memory_space=pltpu.VMEM)
    return pl.pallas_call(
        attn_inputs_kernel,
        in_specs=[local] * 6,
        out_specs=[local] * 2,
        out_shape=[jax.ShapeDtypeStruct(tokens.shape, BF), jax.ShapeDtypeStruct((8, WIDTH), F32)],
        compiler_params=pltpu.CompilerParams(vmem_limit_bytes=12 * 2**20),
        name="attn_inputs",
    )(grad_proj, weights, tokens, gains, grad_hidden, gain_grad)


def x_payloads_kernel(where_ref, own, got_a, got_b, got_c, gains, kept, sent_a, sent_b, sent_c, blocks):
    rows = 4 * BLOCK
    mine = own[0:rows].astype(F32)
    gain = gains[...]
    for part in (got_a, got_b, got_c):
        mine = mine + part[0:rows].astype(F32)
        gain = gain + part[rows : rows + 2].astype(F32)
    for j in range(4):
        blocks[j, 0:20] = mine[3 * BLOCK + 20 * j : 3 * BLOCK + 20 * j + 20]
    for r in range(4):
        pieces = [mine[BLOCK * w + 20 * r : BLOCK * w + 20 * r + 20] for w in range(3)]
        pieces += [blocks[lax.rem(where_ref[0] + r, 4)][0:20], gain]
        block = jnp.concatenate(pieces, axis=0)
        if r == 0:
            kept[...] = block
        else:
            (sent_a, sent_b, sent_c)[r - 1][...] = block.astype(BF)


def x_payloads(where, own, got, gains):
    local = pl.BlockSpec(memory_space=pltpu.VMEM)
    return pl.pallas_call(
        x_payloads_kernel,
        in_specs=[pl.BlockSpec(memory_space=pltpu.SMEM)] + [local] * 5,
        out_specs=[local] * 4,
        out_shape=[jax.ShapeDtypeStruct((82, WIDTH), F32)] + [jax.ShapeDtypeStruct((82, WIDTH), BF)] * 3,
        scratch_shapes=[pltpu.VMEM((4, 24, WIDTH), F32)],
        compiler_params=pltpu.CompilerParams(vmem_limit_bytes=12 * 2**20),
        name="x_payloads",
    )(where, own, *got, gains)


def ffn_kernel(count, first, normed, cot, *refs):
    chunks, refs = refs[:count], refs[count:]
    if first:
        branch, back = 0.0, 0.0
    else:
        branch, back = refs[0][...], refs[1][...]
        refs = refs[2:]
    grads, branch_out, back_out = list(refs[:-2]), refs[-2], refs[-1]
    step = 2 * BLOCK
    for chunk in chunks:
        parts = chunk.shape[1]
        half = parts * BLOCK
        pair = chunk[0:2].reshape(2 * half, WIDTH)
        down = chunk[2].reshape(half, WIDTH)
        both = dot(pair, normed[...], NT)
        grad_prod = dot(down, cot[...], NT)
        gate, up = both[:half], both[half:]
        sigma = 1.0 / (1.0 + jnp.exp(-gate))
        gated = gate * sigma
        product = (gated * up).astype(BF)
        grad_gate = (grad_prod * up * sigma * (1.0 + gate * (1.0 - sigma))).astype(BF)
        grad_up = (grad_prod * gated).astype(BF)
        grad_pair = jnp.concatenate([grad_gate, grad_up], axis=0)
        back = back + dot(grad_pair, pair, TN)
        pair_grad = dot(grad_pair, normed[...], NN).astype(BF)
        down_grad = dot(product, cot[...], NN).astype(BF)
        for at in range(0, half, step):
            grad = grads.pop(0)
            grad[0] = pair_grad[at : at + step].reshape(2, BLOCK, WIDTH)
            grad[1] = pair_grad[half + at : half + at + step].reshape(2, BLOCK, WIDTH)
            grad[2] = down_grad[at : at + step].reshape(2, BLOCK, WIDTH)
        branch = branch + dot(product, down, TN)
    branch_out[...] = branch
    back_out[...] = back


def ffn(normed, cot, chunks, sums):
    local = pl.BlockSpec(memory_space=pltpu.VMEM)
    count, tokens = len(chunks), normed.shape[0]
    sums = list(sums)
    held = len(sums)
    units = sum(chunk.shape[1] for chunk in chunks) * BLOCK
    pieces = units // (2 * BLOCK)
    out = pl.pallas_call(
        lambda *refs: ffn_kernel(count, held == 0, *refs),
        in_specs=[local] * (2 + count + held),
        out_specs=[local] * (pieces + 2),
        out_shape=[jax.ShapeDtypeStruct((3, 2, BLOCK, WIDTH), BF)] * pieces
        + [jax.ShapeDtypeStruct((tokens, WIDTH), F32)] * 2,
        input_output_aliases={2 + count + i: pieces + i for i in range(held)},
        compiler_params=pltpu.CompilerParams(vmem_limit_bytes=16 * 2**20),
        cost_estimate=pl.CostEstimate(
            flops=18 * tokens * units * WIDTH,
            transcendentals=tokens * units,
            bytes_accessed=12 * units * WIDTH,
        ),
        name="ffn_chunks",
    )(normed, cot, *chunks, *sums)
    return out[:pieces], out[pieces:]


def rope_tables(seg):
    places = jnp.arange(TOK)
    allowed = (seg[:, :, None] == seg[:, None, :]) & (places[None, :] <= places[:, None])
    position = jnp.sum(allowed.astype(F32), axis=-1) - 1.0
    freqs = THETA ** (-2.0 * jnp.arange(HEAD_DIM // 2).astype(F32) / HEAD_DIM)
    angles = freqs[:, None] * position.reshape(1, -1)
    return jnp.cos(angles), jnp.sin(angles)


def inv_rms(values):
    return lax.rsqrt(jnp.mean(values * values, axis=-1, keepdims=True) + EPS)


def norm_back(grad_normed, source, inverse, gain_vec):
    scaled = source * inverse
    grad_scaled = grad_normed * gain_vec
    grad_gain = jnp.sum(grad_normed * scaled, axis=0, keepdims=True)
    mean = jnp.mean(grad_scaled * scaled, axis=-1, keepdims=True)
    return inverse * (grad_scaled - scaled * mean), grad_gain


def dot(left, right, dims):
    return lax.dot_general(left, right, (dims, ((), ())), preferred_element_type=F32)


NT = ((1,), (1,))
NN = ((1,), (0,))
TN = ((0,), (0,))


def total(parts):
    out = parts[0].astype(F32)
    for part in parts[1:]:
        out = out + part.astype(F32)
    return out


def body(tokens, segment_ids, attn_weight, gate_up, down_weight, norm_gains, cotangent):
    z, y, x, c = (lax.axis_index(a) for a in AXES)
    rows = MICRO * TOK

    gain_row = jnp.pad(norm_gains[None, :], ((0, 15), (0, WIDTH - 15)))
    shard = jnp.concatenate([attn_weight, gate_up[0], gate_up[1], down_weight, gain_row], axis=0)
    near = jnp.stack(fetch_ordered(shard, shift_x))
    ffn_block = near[:, 20:80].reshape(4, 3, 20, WIDTH).transpose(1, 0, 2, 3).reshape(3, BLOCK, WIDTH)
    head = jnp.concatenate([near[:, :20], near[:, 80:81]], axis=1)
    head = lax.dynamic_slice_in_dim(jnp.concatenate([head, head], axis=0), lax.rem(4 - x, 4), 4, axis=0)
    other = permute(head, shift_core())
    both = jnp.stack([jnp.where(c == 0, head, other), jnp.where(c == 0, other, head)], axis=1)
    attn_half = lax.dynamic_slice_in_dim(both[:, :, :20].reshape(2 * BLOCK, WIDTH), c * BLOCK, BLOCK, axis=0)
    gain_near = jnp.pad(both[:, :, 20, :15].reshape(1, 120), ((0, 15), (0, WIDTH - 120)))
    attn_block = jnp.concatenate([attn_half, gain_near], axis=0)

    block = jnp.concatenate([attn_block, ffn_block.reshape(3 * BLOCK, WIDTH)], axis=0)
    got = fetch_ordered(block, lambda s: shift_plane(s, True))
    attn_one = jnp.stack([part[:96] for part in got])
    ffn_got = [part[96:].reshape(3, BLOCK, WIDTH) for part in got]
    zero_low, zero_high = jnp.stack(ffn_got[:2], axis=1), jnp.stack(ffn_got[2:], axis=1)
    own = fetch_ordered(attn_one, lambda s: shift_plane(s, False))
    first, zero_low, zero_high = lax.optimization_barrier((own[0], zero_low, zero_high))
    sib = [permute(v, shift_core()) for v in [first] + own[1:]]
    where = jnp.stack([z, y, c]).astype(jnp.int32)

    next_low = permute(zero_low, shift_plane(-1, False))
    last_high = permute(zero_high, shift_plane(1, False))
    send_low, send_high, _ = lax.optimization_barrier((zero_low, zero_high, sib))
    next_high = permute(send_high, shift_plane(-1, False))
    last_low = permute(send_low, shift_plane(1, False))

    live = (segment_ids.reshape(rows, 1) < TOK).astype(F32)
    cot = cotangent.reshape(rows, WIDTH)
    grad_mlp = (live * cot.astype(F32)).astype(BF)
    grad_mlp_all = jnp.concatenate([grad_mlp, permute(grad_mlp, shift_core())], axis=0)
    cosine, sine = rope_tables(segment_ids)
    flat_tokens = tokens.reshape(rows, WIDTH)
    weights, normed_one, heads, probs, att, hidden, normed_two, gains = attn_forward(
        where, flat_tokens, segment_ids, live, cosine, sine, own, sib
    )

    normed_all = jnp.concatenate([normed_two, permute(normed_two, shift_core())], axis=0)
    forward_low, forward_high, _ = lax.optimization_barrier((next_low, last_high, normed_two))
    far_low = permute(forward_low, shift_plane(-1, False))
    far_high = permute(forward_high, shift_plane(1, False))
    zero_grads, sums = ffn(normed_all, grad_mlp_all, [zero_low, zero_high], [])
    near_grads, sums = ffn(normed_all, grad_mlp_all, [next_low, next_high, last_low, last_high], sums)
    next_low, next_high, last_low, last_high = near_grads
    next_high, last_low, far_low, far_high = lax.optimization_barrier((next_high, last_low, far_low, far_high))
    (grad_low,), sums = ffn(normed_all, grad_mlp_all, [far_low], sums)
    (grad_high,), (branch, grad_normed) = ffn(normed_all, grad_mlp_all, [far_high], sums)
    back_other = permute(grad_normed[rows:].astype(BF), shift_core())
    next_high_got = permute(next_high, shift_plane(1, False))
    last_low_got = permute(last_low, shift_plane(-1, False))
    back_other, next_high_got, last_low_got = lax.optimization_barrier((back_other, next_high_got, last_low_got))
    branch = branch[:rows] + permute(branch[rows:].astype(BF), shift_core()).astype(F32)
    result = (hidden + live * branch).astype(BF)

    ours, theirs, grad_hidden, grad_proj, gain_grads = attn_backward(
        where, grad_normed, back_other, hidden, gains, cot, live, weights, heads, probs, att, normed_one, cosine, sine
    )
    far_low = permute(grad_low, shift_plane(1, False))
    far_high = permute(grad_high, shift_plane(-1, False))
    theirs, far_low, far_high = lax.optimization_barrier((theirs, far_low, far_high))
    next_low_got = permute(total([next_low, far_low]).astype(BF), shift_plane(1, False))
    last_high_got = permute(total([last_high, far_high]).astype(BF), shift_plane(-1, False))
    swapped = permute(theirs, shift_core())
    grad_inputs, gain_grads = attn_inputs(grad_proj, weights, flat_tokens, gains, grad_hidden, gain_grads)
    gain_grads = gain_grads[:2] + permute(gain_grads[:2], shift_core())

    attn_mine = total([ours, swapped]).astype(BF).reshape(4, 4 * BLOCK, WIDTH)
    low_gains = jnp.pad(gain_grads.astype(BF), ((0, 14), (0, 0)))
    blocks = [jnp.concatenate([attn_mine[r], low_gains], axis=0) for r in (1, 3, 2)]
    got = [permute(block, shift_plane(r, False)) for block, r in zip(blocks, (1, 3, 2))]
    attn_next = total([attn_mine[0]] + [part[: 4 * BLOCK] for part in got])
    gain_grads = total([gain_grads] + [part[4 * BLOCK : 4 * BLOCK + 2] for part in got])
    next_low_got, last_high_got, _ = lax.optimization_barrier((next_low_got, last_high_got, attn_next))
    low_mine = total([zero_grads[0], next_low_got, last_low_got]).astype(BF)
    high_mine = total([zero_grads[1], next_high_got, last_high_got]).astype(BF)
    attn_next = attn_next.astype(BF).reshape(4, BLOCK, WIDTH)
    low_gains = jnp.pad(gain_grads.astype(BF), ((0, 14), (0, 0)))

    def rows_for(r):
        ffn_rows = (low_mine if r < 2 else high_mine)[:, r % 2].reshape(3 * BLOCK, WIDTH)
        return jnp.concatenate([ffn_rows, attn_next[r], low_gains], axis=0)

    got = [permute(rows_for(r), shift_plane(r, True)) for r in (1, 3, 2)]
    kept, *sent = x_payloads(jnp.stack([x, x, x]).astype(jnp.int32), rows_for(0), got, gain_grads)
    got = [permute(sent[r - 1], shift_x(r)) for r in (1, 3, 2)]
    mine = total([kept] + got)
    ffn_owned = mine[:60].reshape(3, 20, WIDTH)
    attn_owned = permute(mine[60:80], to_owner())
    gain_grads = mine[80:82]
    gain_owned = lax.dynamic_slice_in_dim(gain_grads.reshape(2 * WIDTH), flat_index(z, y, x, c) * 15, 15)
    return (
        result.reshape(MICRO, TOK, WIDTH),
        grad_inputs.reshape(MICRO, TOK, WIDTH),
        attn_owned,
        ffn_owned[:2],
        ffn_owned[2],
        gain_owned,
    )


def flat_index(z, y, x, c):
    return ((z * 4 + y) * 4 + x) * 2 + c


def solution(mesh):
    grid = Mesh(mesh.devices.reshape(4, 4, 4, 2), AXES)
    return jax.shard_map(
        body,
        mesh=grid,
        in_specs=(
            P(None, AXES, None),
            P(None, AXES),
            P(AXES, None),
            P(None, AXES, None),
            P(AXES, None),
            P(AXES),
            P(None, AXES, None),
        ),
        out_specs=(
            P(None, AXES, None),
            P(None, AXES, None),
            P(AXES, None),
            P(None, AXES, None),
            P(AXES, None),
            P(AXES),
        ),
        check_vma=False,
    )
```

```python
import jax
import jax.numpy as jnp
from jax import lax
from jax.experimental import pallas as pl
from jax.experimental.pallas import tpu as pltpu
from jax.sharding import Mesh, PartitionSpec as P

HEADS = 15
KV_HEADS = 5
GROUP = HEADS // KV_HEADS
HEAD_DIM = 64
MICRO = 2
WIDTH = 960
TOK = 128
BLOCK = 80
EPS = 1e-05
THETA = 100000.0
NEG_FILL = -1e30
AXES = ("z", "y", "x", "c")
BF = jnp.bfloat16
F32 = jnp.float32


def flat(z, y, x, c):
    return (((z % 4) * 4 + y % 4) * 4 + x % 4) * 2 + c % 2


def everywhere():
    return [(z, y, x, c) for z in range(4) for y in range(4) for x in range(4) for c in range(2)]


def shift_x(step):
    return [(flat(*d), flat(d[0], d[1], d[2] + step, d[3])) for d in everywhere()]


def shift_core():
    return [(flat(*d), flat(d[0], d[1], d[2], d[3] + 1)) for d in everywhere()]


def shift_plane(step, inner):
    pairs = []
    for z, y, x, c in everywhere():
        along_y = (c == 0) == inner
        pairs.append((flat(z, y, x, c), flat(z, y + step, x, c) if along_y else flat(z + step, y, x, c)))
    return pairs


def to_owner():
    return [(flat(z, y, j, c), flat(z, y, 2 * c + j // 2, j % 2)) for z, y, j, c in everywhere()]


def permute(value, pairs):
    return lax.ppermute(value, AXES, pairs)


def fetch(value, make):
    return [value] + [permute(value, make(-r)) for r in (1, 3, 2)]


def fetch_ordered(value, make):
    got = fetch(value, make)
    return [got[0], got[1], got[3], got[2]]


def move_rows(where_ref, own, sib, weights, gains):
    z, y, c = where_ref[0], where_ref[1], where_ref[2]
    for r2 in range(4):
        for r1 in range(4):
            for which, group in enumerate((own, sib)):
                core = c if which == 0 else 1 - c
                rz = jnp.where(core == 0, r2, r1)
                ry = jnp.where(core == 0, r1, r2)
                row = lax.rem(z + rz, 4) * 4 + lax.rem(y + ry, 4)
                weights[row, core] = group[r2][r1, 0:BLOCK]
                if which == 0:
                    gains[row] = group[r2][r1, BLOCK : BLOCK + 16]


def unpack_gains(gains):
    raw = gains[:, 0, 0:128].astype(BF)
    lane = lax.broadcasted_iota(jnp.int32, (128, WIDTH), 1)
    entry = lax.broadcasted_iota(jnp.int32, (128, WIDTH), 0)
    pick = jnp.where(lane - ((lane * 8739) >> 20) * 120 == entry, 1.0, 0.0).astype(BF)
    spread = dot(raw, pick, NN)
    lane = lax.broadcasted_iota(jnp.int32, (16, WIDTH), 1)
    row = lax.broadcasted_iota(jnp.int32, (16, WIDTH), 0)
    block = (lane * 8739) >> 20
    attn = jnp.sum(jnp.where(row == block, spread, 0.0), axis=0, keepdims=True)
    mlp = jnp.sum(jnp.where(row == block + 8, spread, 0.0), axis=0, keepdims=True)
    return attn, mlp


def heads_of(ref, kv, b):
    lanes = slice(TOK * b, TOK * (b + 1))
    parts = [ref[HEAD_DIM * h : HEAD_DIM * (h + 1), lanes] for h in range(GROUP * kv, GROUP * (kv + 1))]
    return jnp.concatenate(parts, axis=1)


def turn(values, cosine, sine):
    split = values.reshape(-1, 2, HEAD_DIM // 2, values.shape[-1])
    former, latter = split[:, 0], split[:, 1]
    turned = jnp.stack([former * cosine - latter * sine, latter * cosine + former * sine], axis=1)
    return turned.reshape(values.shape)


def attn_forward_kernel(where_ref, tokens, seg_col, seg_row, live, cosine, sine, *refs):
    own, sib = refs[0:4], refs[4:8]
    weights, normed, heads, probs, att, hidden, normed_two, gain_out, gains = refs[8:]
    move_rows(where_ref, own, sib, weights, gains)
    inputs = tokens[...].astype(F32)
    scaled = inputs * inv_rms(inputs)
    gain_attn, gain_mlp = unpack_gains(gains)
    gain_out[...] = jnp.concatenate([gain_attn, gain_mlp, jnp.zeros((6, WIDTH), F32)], axis=0)
    normed[...] = (scaled * gain_attn).astype(BF)
    rows = WIDTH + KV_HEADS * HEAD_DIM
    projected = dot(weights[0:10].reshape(-1, WIDTH), normed[...], NT)
    heads[0:rows] = turn(projected[0:rows], cosine[...], sine[...]).astype(BF)
    heads[rows:] = projected[rows:].astype(BF)
    key_place = lax.broadcasted_iota(jnp.int32, (TOK, TOK), 0)
    query_place = lax.broadcasted_iota(jnp.int32, (TOK, TOK), 1)
    for b in range(MICRO):
        lanes = slice(TOK * b, TOK * (b + 1))
        same = seg_col[lanes, :] == seg_row[b : b + 1, :]
        allowed = jnp.where(same & (key_place <= query_place), 1.0, 0.0)
        allowed = jnp.concatenate([allowed] * GROUP, axis=1)
        for kv in range(KV_HEADS):
            key = heads[WIDTH + HEAD_DIM * kv : WIDTH + HEAD_DIM * (kv + 1), lanes]
            value = heads[rows + HEAD_DIM * kv : rows + HEAD_DIM * (kv + 1), lanes]
            scores = dot(key, heads_of(heads, kv, b), TN) * HEAD_DIM ** (-0.5)
            scores = jnp.where(allowed > 0.5, scores, NEG_FILL)
            expd = jnp.exp(scores - jnp.max(scores, axis=0, keepdims=True))
            prob = expd / jnp.sum(expd, axis=0, keepdims=True)
            probs[b * KV_HEADS + kv] = prob
            attended = dot(value, prob.astype(BF), NN).astype(BF)
            for g in range(GROUP):
                h = GROUP * kv + g
                att[HEAD_DIM * h : HEAD_DIM * (h + 1), lanes] = attended[:, TOK * g : TOK * (g + 1)]
    total_hidden = inputs + live[...] * dot(att[...], weights[10:16].reshape(WIDTH, WIDTH), TN)
    hidden[...] = total_hidden
    normed_two[...] = (total_hidden * inv_rms(total_hidden) * gain_mlp).astype(BF)


def attn_forward(where, tokens, segment_ids, live, cosine, sine, own, sib):
    local = pl.BlockSpec(memory_space=pltpu.VMEM)
    rows = tokens.shape[0]
    qkv_rows = WIDTH + 2 * KV_HEADS * HEAD_DIM
    return pl.pallas_call(
        attn_forward_kernel,
        in_specs=[pl.BlockSpec(memory_space=pltpu.SMEM)] + [local] * 14,
        out_specs=[local] * 8,
        out_shape=[
            jax.ShapeDtypeStruct((16, 2, BLOCK, WIDTH), BF),
            jax.ShapeDtypeStruct((rows, WIDTH), BF),
            jax.ShapeDtypeStruct((qkv_rows, rows), BF),
            jax.ShapeDtypeStruct((MICRO * KV_HEADS, TOK, GROUP * TOK), F32),
            jax.ShapeDtypeStruct((WIDTH, rows), BF),
            jax.ShapeDtypeStruct((rows, WIDTH), F32),
            jax.ShapeDtypeStruct((rows, WIDTH), BF),
            jax.ShapeDtypeStruct((8, WIDTH), F32),
        ],
        scratch_shapes=[pltpu.VMEM((16, 16, WIDTH), BF)],
        compiler_params=pltpu.CompilerParams(vmem_limit_bytes=12 * 2**20),
        name="attn_forward",
    )(where, tokens, segment_ids.reshape(rows, 1), segment_ids, live, cosine, sine, *own, *sib)


def attn_backward_kernel(where_ref, back, back_other, hidden, gains, cot, live, weights, heads, probs, att, normed, cosine, sine,
                         ours, theirs, grad_hidden, grad_proj, gain_grad, raw):
    z, y, c = where_ref[0], where_ref[1], where_ref[2]
    rows = hidden.shape[0]
    grad_normed = back[0:rows] + back_other[...].astype(F32)
    grad, gain_mlp = norm_back(grad_normed, hidden[...], inv_rms(hidden[...]), gains[1:2])
    grad = cot[...].astype(F32) + grad
    grad_hidden[...] = grad
    gain_grad[...] = jnp.concatenate([jnp.zeros((1, WIDTH), F32), gain_mlp, jnp.zeros((6, WIDTH), F32)], axis=0)
    branch = (live[...] * grad).astype(BF)
    grad_att = dot(weights[10:16].reshape(WIDTH, WIDTH), branch, NT).astype(BF)
    base = WIDTH + KV_HEADS * HEAD_DIM
    for b in range(MICRO):
        lanes = slice(TOK * b, TOK * (b + 1))
        for kv in range(KV_HEADS):
            key = heads[WIDTH + HEAD_DIM * kv : WIDTH + HEAD_DIM * (kv + 1), lanes]
            value = heads[base + HEAD_DIM * kv : base + HEAD_DIM * (kv + 1), lanes]
            query, grad_out = heads_of(heads, kv, b), heads_of(grad_att, kv, b)
            prob = probs[b * KV_HEADS + kv]
            grad_prob = dot(value, grad_out, TN)
            delta = jnp.sum(prob * grad_prob, axis=0, keepdims=True)
            grad_score = (HEAD_DIM ** (-0.5) * prob * (grad_prob - delta)).astype(BF)
            grad_query = dot(key, grad_score, NN)
            for g in range(GROUP):
                h = GROUP * kv + g
                raw[HEAD_DIM * h : HEAD_DIM * (h + 1), lanes] = grad_query[:, TOK * g : TOK * (g + 1)]
            raw[WIDTH + HEAD_DIM * kv : WIDTH + HEAD_DIM * (kv + 1), lanes] = dot(query, grad_score, NT)
            raw[base + HEAD_DIM * kv : base + HEAD_DIM * (kv + 1), lanes] = dot(grad_out, prob.astype(BF), NT)
    grad_proj[0:base] = turn(raw[0:base], cosine[...], -sine[...]).astype(BF)
    grad_proj[base:] = raw[base:].astype(BF)

    jobs = [(grad_proj, 0, 640, normed[...]), (grad_proj, 640, 640, normed[...]), (grad_proj, 1280, 320, normed[...])]
    jobs += [(att, 0, 640, branch), (att, 640, 320, branch)]
    row = 0
    for source, start, size, right in jobs:
        block = dot(source[start : start + size], right, NN).astype(BF)
        for k in range(size // 160):
            rz = lax.rem(row // 4 - z + 4, 4)
            ry = lax.rem(row % 4 - y + 4, 4)
            zy, yz = rz * 4 + ry, ry * 4 + rz
            lower = block[160 * k : 160 * k + 80]
            upper = block[160 * k + 80 : 160 * k + 160]

            @pl.when(c == 0)
            def _(lower=lower, upper=upper, zy=zy, yz=yz):
                ours[zy] = lower
                theirs[yz] = upper

            @pl.when(c != 0)
            def _(lower=lower, upper=upper, zy=zy, yz=yz):
                ours[yz] = upper
                theirs[zy] = lower

            row += 1


def attn_backward(where, back, back_other, hidden, gains, cot, live, weights, heads, probs, att, normed, cosine, sine):
    local = pl.BlockSpec(memory_space=pltpu.VMEM)
    return pl.pallas_call(
        attn_backward_kernel,
        in_specs=[pl.BlockSpec(memory_space=pltpu.SMEM)] + [local] * 13,
        out_specs=[local] * 5,
        out_shape=[
            jax.ShapeDtypeStruct((16, BLOCK, WIDTH), BF),
            jax.ShapeDtypeStruct((16, BLOCK, WIDTH), BF),
            jax.ShapeDtypeStruct(hidden.shape, F32),
            jax.ShapeDtypeStruct(heads.shape, BF),
            jax.ShapeDtypeStruct((8, WIDTH), F32),
        ],
        scratch_shapes=[pltpu.VMEM(heads.shape, F32)],
        compiler_params=pltpu.CompilerParams(vmem_limit_bytes=16 * 2**20),
        name="attn_backward",
    )(where, back, back_other, hidden, gains, cot, live, weights, heads, probs, att, normed, cosine, sine)


def store_turned(ref, values):
    for b in range(MICRO):
        ref[b] = values[TOK * b : TOK * (b + 1)].T.astype(BF)


def finish_kernel(hidden, live, branch, other, out):
    store_turned(out, hidden[...] + live[...] * (branch[0 : hidden.shape[0]] + other[...].astype(F32)))


def finish(hidden, live, branch, other):
    local = pl.BlockSpec(memory_space=pltpu.VMEM)
    return pl.pallas_call(
        finish_kernel,
        in_specs=[local] * 4,
        out_specs=local,
        out_shape=jax.ShapeDtypeStruct((MICRO, WIDTH, TOK), BF),
        compiler_params=pltpu.CompilerParams(vmem_limit_bytes=12 * 2**20),
        name="finish",
    )(hidden, live, branch, other)


def attn_inputs_kernel(grad_proj, weights, tokens, gains, grad_hidden, gain_grad, grad_inputs, gain_out):
    inputs = tokens[...].astype(F32)
    grad_normed = dot(grad_proj[...], weights[0:10].reshape(-1, WIDTH), TN)
    grad, gain_attn = norm_back(grad_normed, inputs, inv_rms(inputs), gains[0:1])
    store_turned(grad_inputs, grad_hidden[...] + grad)
    gain_out[...] = gain_grad[...] + jnp.concatenate([gain_attn, jnp.zeros((7, WIDTH), F32)], axis=0)


def attn_inputs(grad_proj, weights, tokens, gains, grad_hidden, gain_grad):
    local = pl.BlockSpec(memory_space=pltpu.VMEM)
    return pl.pallas_call(
        attn_inputs_kernel,
        in_specs=[local] * 6,
        out_specs=[local] * 2,
        out_shape=[jax.ShapeDtypeStruct((MICRO, WIDTH, TOK), BF), jax.ShapeDtypeStruct((8, WIDTH), F32)],
        compiler_params=pltpu.CompilerParams(vmem_limit_bytes=12 * 2**20),
        name="attn_inputs",
    )(grad_proj, weights, tokens, gains, grad_hidden, gain_grad)


def x_payloads_kernel(where_ref, own, got_a, got_b, got_c, gains, kept, sent_a, sent_b, sent_c, blocks):
    rows = 4 * BLOCK
    mine = own[0:rows].astype(F32)
    gain = gains[...]
    for part in (got_a, got_b, got_c):
        mine = mine + part[0:rows].astype(F32)
        gain = gain + part[rows : rows + 2].astype(F32)
    for j in range(4):
        blocks[j, 0:20] = mine[3 * BLOCK + 20 * j : 3 * BLOCK + 20 * j + 20]
    for r in range(4):
        pieces = [mine[BLOCK * w + 20 * r : BLOCK * w + 20 * r + 20] for w in range(3)]
        pieces += [blocks[lax.rem(where_ref[0] + r, 4)][0:20], gain]
        block = jnp.concatenate(pieces, axis=0)
        if r == 0:
            kept[...] = block
        else:
            (sent_a, sent_b, sent_c)[r - 1][...] = block.astype(BF)


def x_payloads(where, own, got, gains):
    local = pl.BlockSpec(memory_space=pltpu.VMEM)
    return pl.pallas_call(
        x_payloads_kernel,
        in_specs=[pl.BlockSpec(memory_space=pltpu.SMEM)] + [local] * 5,
        out_specs=[local] * 4,
        out_shape=[jax.ShapeDtypeStruct((82, WIDTH), F32)] + [jax.ShapeDtypeStruct((82, WIDTH), BF)] * 3,
        scratch_shapes=[pltpu.VMEM((4, 24, WIDTH), F32)],
        compiler_params=pltpu.CompilerParams(vmem_limit_bytes=12 * 2**20),
        name="x_payloads",
    )(where, own, *got, gains)


def ffn_kernel(count, first, normed, cot, *refs):
    chunks, refs = refs[:count], refs[count:]
    if first:
        branch, back = 0.0, 0.0
    else:
        branch, back = refs[0][...], refs[1][...]
        refs = refs[2:]
    grads, branch_out, back_out = list(refs[:-2]), refs[-2], refs[-1]
    step = 2 * BLOCK
    for chunk in chunks:
        parts = chunk.shape[1]
        half = parts * BLOCK
        pair = chunk[0:2].reshape(2 * half, WIDTH)
        down = chunk[2].reshape(half, WIDTH)
        both = dot(pair, normed[...], NT)
        grad_prod = dot(down, cot[...], NT)
        gate, up = both[:half], both[half:]
        sigma = 1.0 / (1.0 + jnp.exp(-gate))
        gated = gate * sigma
        product = (gated * up).astype(BF)
        grad_gate = (grad_prod * up * sigma * (1.0 + gate * (1.0 - sigma))).astype(BF)
        grad_up = (grad_prod * gated).astype(BF)
        grad_pair = jnp.concatenate([grad_gate, grad_up], axis=0)
        back = back + dot(grad_pair, pair, TN)
        pair_grad = dot(grad_pair, normed[...], NN).astype(BF)
        down_grad = dot(product, cot[...], NN).astype(BF)
        for at in range(0, half, step):
            grad = grads.pop(0)
            grad[0] = pair_grad[at : at + step].reshape(2, BLOCK, WIDTH)
            grad[1] = pair_grad[half + at : half + at + step].reshape(2, BLOCK, WIDTH)
            grad[2] = down_grad[at : at + step].reshape(2, BLOCK, WIDTH)
        branch = branch + dot(product, down, TN)
    branch_out[...] = branch
    back_out[...] = back


def ffn(normed, cot, chunks, sums):
    local = pl.BlockSpec(memory_space=pltpu.VMEM)
    count, tokens = len(chunks), normed.shape[0]
    sums = list(sums)
    held = len(sums)
    units = sum(chunk.shape[1] for chunk in chunks) * BLOCK
    pieces = units // (2 * BLOCK)
    out = pl.pallas_call(
        lambda *refs: ffn_kernel(count, held == 0, *refs),
        in_specs=[local] * (2 + count + held),
        out_specs=[local] * (pieces + 2),
        out_shape=[jax.ShapeDtypeStruct((3, 2, BLOCK, WIDTH), BF)] * pieces
        + [jax.ShapeDtypeStruct((tokens, WIDTH), F32)] * 2,
        input_output_aliases={2 + count + i: pieces + i for i in range(held)},
        compiler_params=pltpu.CompilerParams(vmem_limit_bytes=16 * 2**20),
        cost_estimate=pl.CostEstimate(
            flops=18 * tokens * units * WIDTH,
            transcendentals=tokens * units,
            bytes_accessed=12 * units * WIDTH,
        ),
        name="ffn_chunks",
    )(normed, cot, *chunks, *sums)
    return out[:pieces], out[pieces:]


def rope_tables(seg):
    places = jnp.arange(TOK)
    allowed = (seg[:, :, None] == seg[:, None, :]) & (places[None, :] <= places[:, None])
    position = jnp.sum(allowed.astype(F32), axis=-1) - 1.0
    freqs = THETA ** (-2.0 * jnp.arange(HEAD_DIM // 2).astype(F32) / HEAD_DIM)
    angles = freqs[:, None] * position.reshape(1, -1)
    return jnp.cos(angles), jnp.sin(angles)


def inv_rms(values):
    return lax.rsqrt(jnp.mean(values * values, axis=-1, keepdims=True) + EPS)


def norm_back(grad_normed, source, inverse, gain_vec):
    scaled = source * inverse
    grad_scaled = grad_normed * gain_vec
    grad_gain = jnp.sum(grad_normed * scaled, axis=0, keepdims=True)
    mean = jnp.mean(grad_scaled * scaled, axis=-1, keepdims=True)
    return inverse * (grad_scaled - scaled * mean), grad_gain


def dot(left, right, dims):
    return lax.dot_general(left, right, (dims, ((), ())), preferred_element_type=F32)


NT = ((1,), (1,))
NN = ((1,), (0,))
TN = ((0,), (0,))


def total(parts):
    out = parts[0].astype(F32)
    for part in parts[1:]:
        out = out + part.astype(F32)
    return out


def body(tokens, segment_ids, attn_weight, gate_up, down_weight, norm_gains, cotangent):
    z, y, x, c = (lax.axis_index(a) for a in AXES)
    rows = MICRO * TOK

    gain_row = jnp.pad(norm_gains[None, :], ((0, 15), (0, WIDTH - 15)))
    shard = jnp.concatenate([attn_weight, gate_up[0], gate_up[1], down_weight, gain_row], axis=0)
    near = jnp.stack(fetch_ordered(shard, shift_x))
    ffn_block = near[:, 20:80].reshape(4, 3, 20, WIDTH).transpose(1, 0, 2, 3).reshape(3, BLOCK, WIDTH)
    head = jnp.concatenate([near[:, :20], near[:, 80:81]], axis=1)
    head = lax.dynamic_slice_in_dim(jnp.concatenate([head, head], axis=0), lax.rem(4 - x, 4), 4, axis=0)
    other = permute(head, shift_core())
    both = jnp.stack([jnp.where(c == 0, head, other), jnp.where(c == 0, other, head)], axis=1)
    attn_half = lax.dynamic_slice_in_dim(both[:, :, :20].reshape(2 * BLOCK, WIDTH), c * BLOCK, BLOCK, axis=0)
    gain_near = jnp.pad(both[:, :, 20, :15].reshape(1, 120), ((0, 15), (0, WIDTH - 120)))
    attn_block = jnp.concatenate([attn_half, gain_near], axis=0)

    block = jnp.concatenate([attn_block, ffn_block.reshape(3 * BLOCK, WIDTH)], axis=0)
    got = fetch_ordered(block, lambda s: shift_plane(s, True))
    attn_one = jnp.stack([part[:96] for part in got])
    ffn_got = [part[96:].reshape(3, BLOCK, WIDTH) for part in got]
    zero_low, zero_high = jnp.stack(ffn_got[:2], axis=1), jnp.stack(ffn_got[2:], axis=1)
    own = fetch_ordered(attn_one, lambda s: shift_plane(s, False))
    first, zero_low, zero_high = lax.optimization_barrier((own[0], zero_low, zero_high))
    sib = [permute(v, shift_core()) for v in [first] + own[1:]]
    where = jnp.stack([z, y, c]).astype(jnp.int32)

    next_low = permute(zero_low, shift_plane(-1, False))
    last_high = permute(zero_high, shift_plane(1, False))
    send_low, send_high, _ = lax.optimization_barrier((zero_low, zero_high, sib))
    next_high = permute(send_high, shift_plane(-1, False))
    last_low = permute(send_low, shift_plane(1, False))

    live = (segment_ids.reshape(rows, 1) < TOK).astype(F32)
    cot = cotangent.reshape(rows, WIDTH)
    grad_mlp = (live * cot.astype(F32)).astype(BF)
    grad_mlp_all = jnp.concatenate([grad_mlp, permute(grad_mlp, shift_core())], axis=0)
    cosine, sine = rope_tables(segment_ids)
    flat_tokens = tokens.reshape(rows, WIDTH)
    weights, normed_one, heads, probs, att, hidden, normed_two, gains = attn_forward(
        where, flat_tokens, segment_ids, live, cosine, sine, own, sib
    )

    normed_all = jnp.concatenate([normed_two, permute(normed_two, shift_core())], axis=0)
    forward_low, forward_high, _ = lax.optimization_barrier((next_low, last_high, normed_two))
    far_low = permute(forward_low, shift_plane(-1, False))
    far_high = permute(forward_high, shift_plane(1, False))
    zero_grads, sums = ffn(normed_all, grad_mlp_all, [zero_low, zero_high], [])
    near_grads, sums = ffn(normed_all, grad_mlp_all, [next_low, next_high, last_low, last_high], sums)
    next_low, next_high, last_low, last_high = near_grads
    next_high, last_low, far_low, far_high = lax.optimization_barrier((next_high, last_low, far_low, far_high))
    (grad_low,), sums = ffn(normed_all, grad_mlp_all, [far_low], sums)
    (grad_high,), (branch, grad_normed) = ffn(normed_all, grad_mlp_all, [far_high], sums)
    back_other = permute(grad_normed[rows:].astype(BF), shift_core())
    next_high_got = permute(next_high, shift_plane(1, False))
    last_low_got = permute(last_low, shift_plane(-1, False))
    back_other, next_high_got, last_low_got = lax.optimization_barrier((back_other, next_high_got, last_low_got))
    branch_other = permute(branch[rows:].astype(BF), shift_core())

    ours, theirs, grad_hidden, grad_proj, gain_grads = attn_backward(
        where, grad_normed, back_other, hidden, gains, cot, live, weights, heads, probs, att, normed_one, cosine, sine
    )
    far_low = permute(grad_low, shift_plane(1, False))
    far_high = permute(grad_high, shift_plane(-1, False))
    theirs, far_low, far_high = lax.optimization_barrier((theirs, far_low, far_high))
    next_low_got = permute(total([next_low, far_low]).astype(BF), shift_plane(1, False))
    last_high_got = permute(total([last_high, far_high]).astype(BF), shift_plane(-1, False))
    swapped = permute(theirs, shift_core())
    grad_inputs, gain_grads = attn_inputs(grad_proj, weights, flat_tokens, gains, grad_hidden, gain_grads)
    gain_grads = gain_grads[:2] + permute(gain_grads[:2], shift_core())

    attn_mine = total([ours, swapped]).astype(BF).reshape(4, 4 * BLOCK, WIDTH)
    low_gains = jnp.pad(gain_grads.astype(BF), ((0, 14), (0, 0)))
    blocks = [jnp.concatenate([attn_mine[r], low_gains], axis=0) for r in (1, 3, 2)]
    got = [permute(block, shift_plane(r, False)) for block, r in zip(blocks, (1, 3, 2))]
    attn_next = total([attn_mine[0]] + [part[: 4 * BLOCK] for part in got])
    gain_grads = total([gain_grads] + [part[4 * BLOCK : 4 * BLOCK + 2] for part in got])
    next_low_got, last_high_got, _ = lax.optimization_barrier((next_low_got, last_high_got, attn_next))
    low_mine = total([zero_grads[0], next_low_got, last_low_got]).astype(BF)
    high_mine = total([zero_grads[1], next_high_got, last_high_got]).astype(BF)
    attn_next = attn_next.astype(BF).reshape(4, BLOCK, WIDTH)
    low_gains = jnp.pad(gain_grads.astype(BF), ((0, 14), (0, 0)))

    def rows_for(r):
        ffn_rows = (low_mine if r < 2 else high_mine)[:, r % 2].reshape(3 * BLOCK, WIDTH)
        return jnp.concatenate([ffn_rows, attn_next[r], low_gains], axis=0)

    got = [permute(rows_for(r), shift_plane(r, True)) for r in (1, 3, 2)]
    where_x, branch_other = lax.optimization_barrier((jnp.stack([x, x, x]).astype(jnp.int32), branch_other))
    result = finish(hidden, live, branch, branch_other)
    kept, *sent = x_payloads(where_x, rows_for(0), got, gain_grads)
    got = [permute(sent[r - 1], shift_x(r)) for r in (1, 3, 2)]
    mine = total([kept] + got)
    ffn_owned = mine[:60].reshape(3, 20, WIDTH)
    attn_owned = permute(mine[60:80], to_owner())
    gain_grads = mine[80:82]
    gain_owned = lax.dynamic_slice_in_dim(gain_grads.reshape(2 * WIDTH), flat_index(z, y, x, c) * 15, 15)
    return (
        result.transpose(0, 2, 1),
        grad_inputs.transpose(0, 2, 1),
        attn_owned,
        ffn_owned[:2],
        ffn_owned[2],
        gain_owned,
    )


def flat_index(z, y, x, c):
    return ((z * 4 + y) * 4 + x) * 2 + c


def solution(mesh):
    grid = Mesh(mesh.devices.reshape(4, 4, 4, 2), AXES)
    return jax.shard_map(
        body,
        mesh=grid,
        in_specs=(
            P(None, AXES, None),
            P(None, AXES),
            P(AXES, None),
            P(None, AXES, None),
            P(AXES, None),
            P(AXES),
            P(None, AXES, None),
        ),
        out_specs=(
            P(None, AXES, None),
            P(None, AXES, None),
            P(AXES, None),
            P(None, AXES, None),
            P(AXES, None),
            P(AXES),
        ),
        check_vma=False,
    )
```

```python
import jax
import jax.numpy as jnp
from jax import lax
from jax.experimental import pallas as pl
from jax.experimental.pallas import tpu as pltpu
from jax.sharding import Mesh, PartitionSpec as P

HEADS = 15
KV_HEADS = 5
GROUP = HEADS // KV_HEADS
HEAD_DIM = 64
MICRO = 2
WIDTH = 960
TOK = 128
BLOCK = 80
EPS = 1e-05
THETA = 100000.0
NEG_FILL = -1e30
AXES = ("z", "y", "x", "c")
BF = jnp.bfloat16
F32 = jnp.float32


def flat(z, y, x, c):
    return (((z % 4) * 4 + y % 4) * 4 + x % 4) * 2 + c % 2


def everywhere():
    return [(z, y, x, c) for z in range(4) for y in range(4) for x in range(4) for c in range(2)]


def shift_x(step):
    return [(flat(*d), flat(d[0], d[1], d[2] + step, d[3])) for d in everywhere()]


def shift_core():
    return [(flat(*d), flat(d[0], d[1], d[2], d[3] + 1)) for d in everywhere()]


def shift_plane(step, inner):
    pairs = []
    for z, y, x, c in everywhere():
        along_y = (c == 0) == inner
        pairs.append((flat(z, y, x, c), flat(z, y + step, x, c) if along_y else flat(z + step, y, x, c)))
    return pairs


def to_owner():
    return [(flat(z, y, j, c), flat(z, y, 2 * c + j // 2, j % 2)) for z, y, j, c in everywhere()]


def permute(value, pairs):
    return lax.ppermute(value, AXES, pairs)


def fetch(value, make):
    return [value] + [permute(value, make(-r)) for r in (1, 3, 2)]


def fetch_ordered(value, make):
    got = fetch(value, make)
    return [got[0], got[1], got[3], got[2]]


def move_rows(where_ref, own, sib, weights, gains):
    z, y, c = where_ref[0], where_ref[1], where_ref[2]
    for r2 in range(4):
        for r1 in range(4):
            for which, group in enumerate((own, sib)):
                core = c if which == 0 else 1 - c
                rz = jnp.where(core == 0, r2, r1)
                ry = jnp.where(core == 0, r1, r2)
                row = lax.rem(z + rz, 4) * 4 + lax.rem(y + ry, 4)
                weights[row, core] = group[r2][r1, 0:BLOCK]
                if which == 0:
                    gains[row] = group[r2][r1, BLOCK : BLOCK + 16]


def unpack_gains(gains):
    raw = gains[:, 0, 0:128].astype(BF)
    lane = lax.broadcasted_iota(jnp.int32, (128, WIDTH), 1)
    entry = lax.broadcasted_iota(jnp.int32, (128, WIDTH), 0)
    pick = jnp.where(lane - ((lane * 8739) >> 20) * 120 == entry, 1.0, 0.0).astype(BF)
    spread = dot(raw, pick, NN)
    lane = lax.broadcasted_iota(jnp.int32, (16, WIDTH), 1)
    row = lax.broadcasted_iota(jnp.int32, (16, WIDTH), 0)
    block = (lane * 8739) >> 20
    attn = jnp.sum(jnp.where(row == block, spread, 0.0), axis=0, keepdims=True)
    mlp = jnp.sum(jnp.where(row == block + 8, spread, 0.0), axis=0, keepdims=True)
    return attn, mlp


def heads_of(ref, kv, b):
    lanes = slice(TOK * b, TOK * (b + 1))
    parts = [ref[HEAD_DIM * h : HEAD_DIM * (h + 1), lanes] for h in range(GROUP * kv, GROUP * (kv + 1))]
    return jnp.concatenate(parts, axis=1)


def turn(values, cosine, sine):
    split = values.reshape(-1, 2, HEAD_DIM // 2, values.shape[-1])
    former, latter = split[:, 0], split[:, 1]
    turned = jnp.stack([former * cosine - latter * sine, latter * cosine + former * sine], axis=1)
    return turned.reshape(values.shape)


def attn_forward_kernel(where_ref, tokens, seg_col, seg_row, live, cosine, sine, *refs):
    own, sib = refs[0:4], refs[4:8]
    weights, normed, heads, probs, att, hidden, normed_two, gain_out, gains = refs[8:]
    move_rows(where_ref, own, sib, weights, gains)
    inputs = load_turned(tokens)
    scaled = inputs * inv_rms(inputs)
    gain_attn, gain_mlp = unpack_gains(gains)
    gain_out[...] = jnp.concatenate([gain_attn, gain_mlp, jnp.zeros((6, WIDTH), F32)], axis=0)
    normed[...] = (scaled * gain_attn).astype(BF)
    rows = WIDTH + KV_HEADS * HEAD_DIM
    projected = dot(weights[0:10].reshape(-1, WIDTH), normed[...], NT)
    heads[0:rows] = turn(projected[0:rows], cosine[...], sine[...]).astype(BF)
    heads[rows:] = projected[rows:].astype(BF)
    key_place = lax.broadcasted_iota(jnp.int32, (TOK, TOK), 0)
    query_place = lax.broadcasted_iota(jnp.int32, (TOK, TOK), 1)
    for b in range(MICRO):
        lanes = slice(TOK * b, TOK * (b + 1))
        same = seg_col[lanes, :] == seg_row[b : b + 1, :]
        allowed = jnp.where(same & (key_place <= query_place), 1.0, 0.0)
        allowed = jnp.concatenate([allowed] * GROUP, axis=1)
        for kv in range(KV_HEADS):
            key = heads[WIDTH + HEAD_DIM * kv : WIDTH + HEAD_DIM * (kv + 1), lanes]
            value = heads[rows + HEAD_DIM * kv : rows + HEAD_DIM * (kv + 1), lanes]
            scores = dot(key, heads_of(heads, kv, b), TN) * HEAD_DIM ** (-0.5)
            scores = jnp.where(allowed > 0.5, scores, NEG_FILL)
            expd = jnp.exp(scores - jnp.max(scores, axis=0, keepdims=True))
            prob = expd / jnp.sum(expd, axis=0, keepdims=True)
            probs[b * KV_HEADS + kv] = prob
            attended = dot(value, prob.astype(BF), NN).astype(BF)
            for g in range(GROUP):
                h = GROUP * kv + g
                att[HEAD_DIM * h : HEAD_DIM * (h + 1), lanes] = attended[:, TOK * g : TOK * (g + 1)]
    total_hidden = inputs + live[...] * dot(att[...], weights[10:16].reshape(WIDTH, WIDTH), TN)
    hidden[...] = total_hidden
    normed_two[...] = (total_hidden * inv_rms(total_hidden) * gain_mlp).astype(BF)


def attn_forward(where, tokens, segment_ids, live, cosine, sine, own, sib):
    local = pl.BlockSpec(memory_space=pltpu.VMEM)
    rows = MICRO * TOK
    qkv_rows = WIDTH + 2 * KV_HEADS * HEAD_DIM
    return pl.pallas_call(
        attn_forward_kernel,
        in_specs=[pl.BlockSpec(memory_space=pltpu.SMEM)] + [local] * 14,
        out_specs=[local] * 8,
        out_shape=[
            jax.ShapeDtypeStruct((16, 2, BLOCK, WIDTH), BF),
            jax.ShapeDtypeStruct((rows, WIDTH), BF),
            jax.ShapeDtypeStruct((qkv_rows, rows), BF),
            jax.ShapeDtypeStruct((MICRO * KV_HEADS, TOK, GROUP * TOK), F32),
            jax.ShapeDtypeStruct((WIDTH, rows), BF),
            jax.ShapeDtypeStruct((rows, WIDTH), F32),
            jax.ShapeDtypeStruct((rows, WIDTH), BF),
            jax.ShapeDtypeStruct((8, WIDTH), F32),
        ],
        scratch_shapes=[pltpu.VMEM((16, 16, WIDTH), BF)],
        compiler_params=pltpu.CompilerParams(vmem_limit_bytes=12 * 2**20),
        name="attn_forward",
    )(where, tokens, segment_ids.reshape(rows, 1), segment_ids, live, cosine, sine, *own, *sib)


def attn_backward_kernel(where_ref, back, back_other, hidden, gains, cot, live, weights, heads, probs, att, normed, cosine, sine,
                         ours, theirs, grad_hidden, grad_proj, gain_grad, raw):
    z, y, c = where_ref[0], where_ref[1], where_ref[2]
    rows = hidden.shape[0]
    grad_normed = back[0:rows] + back_other[...].astype(F32)
    grad, gain_mlp = norm_back(grad_normed, hidden[...], inv_rms(hidden[...]), gains[1:2])
    grad = cot[...].astype(F32) + grad
    grad_hidden[...] = grad
    gain_grad[...] = jnp.concatenate([jnp.zeros((1, WIDTH), F32), gain_mlp, jnp.zeros((6, WIDTH), F32)], axis=0)
    branch = (live[...] * grad).astype(BF)
    grad_att = dot(weights[10:16].reshape(WIDTH, WIDTH), branch, NT).astype(BF)
    base = WIDTH + KV_HEADS * HEAD_DIM
    for b in range(MICRO):
        lanes = slice(TOK * b, TOK * (b + 1))
        for kv in range(KV_HEADS):
            key = heads[WIDTH + HEAD_DIM * kv : WIDTH + HEAD_DIM * (kv + 1), lanes]
            value = heads[base + HEAD_DIM * kv : base + HEAD_DIM * (kv + 1), lanes]
            query, grad_out = heads_of(heads, kv, b), heads_of(grad_att, kv, b)
            prob = probs[b * KV_HEADS + kv]
            grad_prob = dot(value, grad_out, TN)
            delta = jnp.sum(prob * grad_prob, axis=0, keepdims=True)
            grad_score = (HEAD_DIM ** (-0.5) * prob * (grad_prob - delta)).astype(BF)
            grad_query = dot(key, grad_score, NN)
            for g in range(GROUP):
                h = GROUP * kv + g
                raw[HEAD_DIM * h : HEAD_DIM * (h + 1), lanes] = grad_query[:, TOK * g : TOK * (g + 1)]
            raw[WIDTH + HEAD_DIM * kv : WIDTH + HEAD_DIM * (kv + 1), lanes] = dot(query, grad_score, NT)
            raw[base + HEAD_DIM * kv : base + HEAD_DIM * (kv + 1), lanes] = dot(grad_out, prob.astype(BF), NT)
    grad_proj[0:base] = turn(raw[0:base], cosine[...], -sine[...]).astype(BF)
    grad_proj[base:] = raw[base:].astype(BF)

    jobs = [(grad_proj, 0, 640, normed[...]), (grad_proj, 640, 640, normed[...]), (grad_proj, 1280, 320, normed[...])]
    jobs += [(att, 0, 640, branch), (att, 640, 320, branch)]
    row = 0
    for source, start, size, right in jobs:
        block = dot(source[start : start + size], right, NN).astype(BF)
        for k in range(size // 160):
            rz = lax.rem(row // 4 - z + 4, 4)
            ry = lax.rem(row % 4 - y + 4, 4)
            zy, yz = rz * 4 + ry, ry * 4 + rz
            lower = block[160 * k : 160 * k + 80]
            upper = block[160 * k + 80 : 160 * k + 160]

            @pl.when(c == 0)
            def _(lower=lower, upper=upper, zy=zy, yz=yz):
                ours[zy] = lower
                theirs[yz] = upper

            @pl.when(c != 0)
            def _(lower=lower, upper=upper, zy=zy, yz=yz):
                ours[yz] = upper
                theirs[zy] = lower

            row += 1


def attn_backward(where, back, back_other, hidden, gains, cot, live, weights, heads, probs, att, normed, cosine, sine):
    local = pl.BlockSpec(memory_space=pltpu.VMEM)
    return pl.pallas_call(
        attn_backward_kernel,
        in_specs=[pl.BlockSpec(memory_space=pltpu.SMEM)] + [local] * 13,
        out_specs=[local] * 5,
        out_shape=[
            jax.ShapeDtypeStruct((16, BLOCK, WIDTH), BF),
            jax.ShapeDtypeStruct((16, BLOCK, WIDTH), BF),
            jax.ShapeDtypeStruct(hidden.shape, F32),
            jax.ShapeDtypeStruct(heads.shape, BF),
            jax.ShapeDtypeStruct((8, WIDTH), F32),
        ],
        scratch_shapes=[pltpu.VMEM(heads.shape, F32)],
        compiler_params=pltpu.CompilerParams(vmem_limit_bytes=16 * 2**20),
        name="attn_backward",
    )(where, back, back_other, hidden, gains, cot, live, weights, heads, probs, att, normed, cosine, sine)


def load_turned(ref):
    return jnp.concatenate([ref[b].astype(F32).T for b in range(MICRO)], axis=0)


def store_turned(ref, values):
    for b in range(MICRO):
        ref[b] = values[TOK * b : TOK * (b + 1)].T.astype(BF)


def finish_kernel(hidden, live, branch, other, out):
    store_turned(out, hidden[...] + live[...] * (branch[0 : hidden.shape[0]] + other[...].astype(F32)))


def finish(hidden, live, branch, other):
    local = pl.BlockSpec(memory_space=pltpu.VMEM)
    return pl.pallas_call(
        finish_kernel,
        in_specs=[local] * 4,
        out_specs=local,
        out_shape=jax.ShapeDtypeStruct((MICRO, WIDTH, TOK), BF),
        compiler_params=pltpu.CompilerParams(vmem_limit_bytes=12 * 2**20),
        name="finish",
    )(hidden, live, branch, other)


def attn_inputs_kernel(grad_proj, weights, tokens, gains, grad_hidden, gain_grad, grad_inputs, gain_out):
    inputs = load_turned(tokens)
    grad_normed = dot(grad_proj[...], weights[0:10].reshape(-1, WIDTH), TN)
    grad, gain_attn = norm_back(grad_normed, inputs, inv_rms(inputs), gains[0:1])
    store_turned(grad_inputs, grad_hidden[...] + grad)
    gain_out[...] = gain_grad[...] + jnp.concatenate([gain_attn, jnp.zeros((7, WIDTH), F32)], axis=0)


def attn_inputs(grad_proj, weights, tokens, gains, grad_hidden, gain_grad):
    local = pl.BlockSpec(memory_space=pltpu.VMEM)
    return pl.pallas_call(
        attn_inputs_kernel,
        in_specs=[local] * 6,
        out_specs=[local] * 2,
        out_shape=[jax.ShapeDtypeStruct((MICRO, WIDTH, TOK), BF), jax.ShapeDtypeStruct((8, WIDTH), F32)],
        compiler_params=pltpu.CompilerParams(vmem_limit_bytes=12 * 2**20),
        name="attn_inputs",
    )(grad_proj, weights, tokens, gains, grad_hidden, gain_grad)


def x_payloads_kernel(where_ref, own, got_a, got_b, got_c, gains, kept, sent_a, sent_b, sent_c, blocks):
    rows = 4 * BLOCK
    mine = own[0:rows].astype(F32)
    gain = gains[...]
    for part in (got_a, got_b, got_c):
        mine = mine + part[0:rows].astype(F32)
        gain = gain + part[rows : rows + 2].astype(F32)
    for j in range(4):
        blocks[j, 0:20] = mine[3 * BLOCK + 20 * j : 3 * BLOCK + 20 * j + 20]
    for r in range(4):
        pieces = [mine[BLOCK * w + 20 * r : BLOCK * w + 20 * r + 20] for w in range(3)]
        pieces += [blocks[lax.rem(where_ref[0] + r, 4)][0:20], gain]
        block = jnp.concatenate(pieces, axis=0)
        if r == 0:
            kept[...] = block
        else:
            (sent_a, sent_b, sent_c)[r - 1][...] = block.astype(BF)


def x_payloads(where, own, got, gains):
    local = pl.BlockSpec(memory_space=pltpu.VMEM)
    return pl.pallas_call(
        x_payloads_kernel,
        in_specs=[pl.BlockSpec(memory_space=pltpu.SMEM)] + [local] * 5,
        out_specs=[local] * 4,
        out_shape=[jax.ShapeDtypeStruct((82, WIDTH), F32)] + [jax.ShapeDtypeStruct((82, WIDTH), BF)] * 3,
        scratch_shapes=[pltpu.VMEM((4, 24, WIDTH), F32)],
        compiler_params=pltpu.CompilerParams(vmem_limit_bytes=12 * 2**20),
        name="x_payloads",
    )(where, own, *got, gains)


def ffn_kernel(count, first, normed, cot, *refs):
    chunks, refs = refs[:count], refs[count:]
    if first:
        branch, back = 0.0, 0.0
    else:
        branch, back = refs[0][...], refs[1][...]
        refs = refs[2:]
    grads, branch_out, back_out = list(refs[:-2]), refs[-2], refs[-1]
    step = 2 * BLOCK
    for chunk in chunks:
        parts = chunk.shape[1]
        half = parts * BLOCK
        pair = chunk[0:2].reshape(2 * half, WIDTH)
        down = chunk[2].reshape(half, WIDTH)
        both = dot(pair, normed[...], NT)
        grad_prod = dot(down, cot[...], NT)
        gate, up = both[:half], both[half:]
        sigma = 1.0 / (1.0 + jnp.exp(-gate))
        gated = gate * sigma
        product = (gated * up).astype(BF)
        grad_gate = (grad_prod * up * sigma * (1.0 + gate * (1.0 - sigma))).astype(BF)
        grad_up = (grad_prod * gated).astype(BF)
        grad_pair = jnp.concatenate([grad_gate, grad_up], axis=0)
        back = back + dot(grad_pair, pair, TN)
        pair_grad = dot(grad_pair, normed[...], NN).astype(BF)
        down_grad = dot(product, cot[...], NN).astype(BF)
        for at in range(0, half, step):
            grad = grads.pop(0)
            grad[0] = pair_grad[at : at + step].reshape(2, BLOCK, WIDTH)
            grad[1] = pair_grad[half + at : half + at + step].reshape(2, BLOCK, WIDTH)
            grad[2] = down_grad[at : at + step].reshape(2, BLOCK, WIDTH)
        branch = branch + dot(product, down, TN)
    branch_out[...] = branch
    back_out[...] = back


def ffn(normed, cot, chunks, sums):
    local = pl.BlockSpec(memory_space=pltpu.VMEM)
    count, tokens = len(chunks), normed.shape[0]
    sums = list(sums)
    held = len(sums)
    units = sum(chunk.shape[1] for chunk in chunks) * BLOCK
    pieces = units // (2 * BLOCK)
    out = pl.pallas_call(
        lambda *refs: ffn_kernel(count, held == 0, *refs),
        in_specs=[local] * (2 + count + held),
        out_specs=[local] * (pieces + 2),
        out_shape=[jax.ShapeDtypeStruct((3, 2, BLOCK, WIDTH), BF)] * pieces
        + [jax.ShapeDtypeStruct((tokens, WIDTH), F32)] * 2,
        input_output_aliases={2 + count + i: pieces + i for i in range(held)},
        compiler_params=pltpu.CompilerParams(vmem_limit_bytes=16 * 2**20),
        cost_estimate=pl.CostEstimate(
            flops=18 * tokens * units * WIDTH,
            transcendentals=tokens * units,
            bytes_accessed=12 * units * WIDTH,
        ),
        name="ffn_chunks",
    )(normed, cot, *chunks, *sums)
    return out[:pieces], out[pieces:]


def rope_tables(seg):
    places = jnp.arange(TOK)
    allowed = (seg[:, :, None] == seg[:, None, :]) & (places[None, :] <= places[:, None])
    position = jnp.sum(allowed.astype(F32), axis=-1) - 1.0
    freqs = THETA ** (-2.0 * jnp.arange(HEAD_DIM // 2).astype(F32) / HEAD_DIM)
    angles = freqs[:, None] * position.reshape(1, -1)
    return jnp.cos(angles), jnp.sin(angles)


def inv_rms(values):
    return lax.rsqrt(jnp.mean(values * values, axis=-1, keepdims=True) + EPS)


def norm_back(grad_normed, source, inverse, gain_vec):
    scaled = source * inverse
    grad_scaled = grad_normed * gain_vec
    grad_gain = jnp.sum(grad_normed * scaled, axis=0, keepdims=True)
    mean = jnp.mean(grad_scaled * scaled, axis=-1, keepdims=True)
    return inverse * (grad_scaled - scaled * mean), grad_gain


def dot(left, right, dims):
    return lax.dot_general(left, right, (dims, ((), ())), preferred_element_type=F32)


NT = ((1,), (1,))
NN = ((1,), (0,))
TN = ((0,), (0,))


def total(parts):
    out = parts[0].astype(F32)
    for part in parts[1:]:
        out = out + part.astype(F32)
    return out


def body(tokens, segment_ids, attn_weight, gate_up, down_weight, norm_gains, cotangent):
    z, y, x, c = (lax.axis_index(a) for a in AXES)
    rows = MICRO * TOK

    gain_row = jnp.pad(norm_gains[None, :], ((0, 15), (0, WIDTH - 15)))
    shard = jnp.concatenate([attn_weight, gate_up[0], gate_up[1], down_weight, gain_row], axis=0)
    near = jnp.stack(fetch_ordered(shard, shift_x))
    ffn_block = near[:, 20:80].reshape(4, 3, 20, WIDTH).transpose(1, 0, 2, 3).reshape(3, BLOCK, WIDTH)
    head = jnp.concatenate([near[:, :20], near[:, 80:81]], axis=1)
    head = lax.dynamic_slice_in_dim(jnp.concatenate([head, head], axis=0), lax.rem(4 - x, 4), 4, axis=0)
    other = permute(head, shift_core())
    both = jnp.stack([jnp.where(c == 0, head, other), jnp.where(c == 0, other, head)], axis=1)
    attn_half = lax.dynamic_slice_in_dim(both[:, :, :20].reshape(2 * BLOCK, WIDTH), c * BLOCK, BLOCK, axis=0)
    gain_near = jnp.pad(both[:, :, 20, :15].reshape(1, 120), ((0, 15), (0, WIDTH - 120)))
    attn_block = jnp.concatenate([attn_half, gain_near], axis=0)

    block = jnp.concatenate([attn_block, ffn_block.reshape(3 * BLOCK, WIDTH)], axis=0)
    got = fetch_ordered(block, lambda s: shift_plane(s, True))
    attn_one = jnp.stack([part[:96] for part in got])
    ffn_got = [part[96:].reshape(3, BLOCK, WIDTH) for part in got]
    zero_low, zero_high = jnp.stack(ffn_got[:2], axis=1), jnp.stack(ffn_got[2:], axis=1)
    own = fetch_ordered(attn_one, lambda s: shift_plane(s, False))
    first, zero_low, zero_high = lax.optimization_barrier((own[0], zero_low, zero_high))
    sib = [permute(v, shift_core()) for v in [first] + own[1:]]
    where = jnp.stack([z, y, c]).astype(jnp.int32)

    next_low = permute(zero_low, shift_plane(-1, False))
    last_high = permute(zero_high, shift_plane(1, False))

    live = (segment_ids.reshape(rows, 1) < TOK).astype(F32)
    cot = cotangent.reshape(rows, WIDTH)
    grad_mlp = (live * cot.astype(F32)).astype(BF)
    grad_mlp_all = jnp.concatenate([grad_mlp, permute(grad_mlp, shift_core())], axis=0)
    cosine, sine = rope_tables(segment_ids)
    flat_tokens = tokens.transpose(0, 2, 1)
    weights, normed_one, heads, probs, att, hidden, normed_two, gains = attn_forward(
        where, flat_tokens, segment_ids, live, cosine, sine, own, sib
    )

    normed_all = jnp.concatenate([normed_two, permute(normed_two, shift_core())], axis=0)
    send_low, send_high, _ = lax.optimization_barrier((zero_low, zero_high, normed_two))
    next_high = permute(send_high, shift_plane(-1, False))
    last_low = permute(send_low, shift_plane(1, False))
    forward_low, forward_high, _ = lax.optimization_barrier((next_low, last_high, normed_two))
    far_low = permute(forward_low, shift_plane(-1, False))
    far_high = permute(forward_high, shift_plane(1, False))
    zero_grads, sums = ffn(normed_all, grad_mlp_all, [zero_low, zero_high], [])
    near_grads, sums = ffn(normed_all, grad_mlp_all, [next_low, next_high, last_low, last_high], sums)
    next_low, next_high, last_low, last_high = near_grads
    next_high, last_low, far_low, far_high = lax.optimization_barrier((next_high, last_low, far_low, far_high))
    (grad_low,), sums = ffn(normed_all, grad_mlp_all, [far_low], sums)
    (grad_high,), (branch, grad_normed) = ffn(normed_all, grad_mlp_all, [far_high], sums)
    back_other = permute(grad_normed[rows:].astype(BF), shift_core())
    next_high_got = permute(next_high, shift_plane(1, False))
    last_low_got = permute(last_low, shift_plane(-1, False))
    back_other, next_high_got, last_low_got = lax.optimization_barrier((back_other, next_high_got, last_low_got))
    branch_other = permute(branch[rows:].astype(BF), shift_core())

    ours, theirs, grad_hidden, grad_proj, gain_grads = attn_backward(
        where, grad_normed, back_other, hidden, gains, cot, live, weights, heads, probs, att, normed_one, cosine, sine
    )
    far_low = permute(grad_low, shift_plane(1, False))
    far_high = permute(grad_high, shift_plane(-1, False))
    theirs, far_low, far_high = lax.optimization_barrier((theirs, far_low, far_high))
    next_low_got = permute(total([next_low, far_low]).astype(BF), shift_plane(1, False))
    last_high_got = permute(total([last_high, far_high]).astype(BF), shift_plane(-1, False))
    swapped = permute(theirs, shift_core())
    grad_inputs, gain_grads = attn_inputs(grad_proj, weights, flat_tokens, gains, grad_hidden, gain_grads)
    gain_grads = gain_grads[:2] + permute(gain_grads[:2], shift_core())

    attn_mine = total([ours, swapped]).astype(BF).reshape(4, 4 * BLOCK, WIDTH)
    low_gains = jnp.pad(gain_grads.astype(BF), ((0, 14), (0, 0)))
    blocks = [jnp.concatenate([attn_mine[r], low_gains], axis=0) for r in (1, 3, 2)]
    got = [permute(block, shift_plane(r, False)) for block, r in zip(blocks, (1, 3, 2))]
    attn_next = total([attn_mine[0]] + [part[: 4 * BLOCK] for part in got])
    gain_grads = total([gain_grads] + [part[4 * BLOCK : 4 * BLOCK + 2] for part in got])
    next_low_got, last_high_got, _ = lax.optimization_barrier((next_low_got, last_high_got, attn_next))
    low_mine = total([zero_grads[0], next_low_got, last_low_got]).astype(BF)
    high_mine = total([zero_grads[1], next_high_got, last_high_got]).astype(BF)
    attn_next = attn_next.astype(BF).reshape(4, BLOCK, WIDTH)
    low_gains = jnp.pad(gain_grads.astype(BF), ((0, 14), (0, 0)))

    def rows_for(r):
        ffn_rows = (low_mine if r < 2 else high_mine)[:, r % 2].reshape(3 * BLOCK, WIDTH)
        return jnp.concatenate([ffn_rows, attn_next[r], low_gains], axis=0)

    got = [permute(rows_for(r), shift_plane(r, True)) for r in (1, 3, 2)]
    where_x, branch_other = lax.optimization_barrier((jnp.stack([x, x, x]).astype(jnp.int32), branch_other))
    result = finish(hidden, live, branch, branch_other)
    kept, *sent = x_payloads(where_x, rows_for(0), got, gain_grads)
    got = [permute(sent[r - 1], shift_x(r)) for r in (1, 3, 2)]
    mine = total([kept] + got)
    ffn_owned = mine[:60].reshape(3, 20, WIDTH)
    attn_owned = permute(mine[60:80], to_owner())
    gain_grads = mine[80:82]
    gain_owned = lax.dynamic_slice_in_dim(gain_grads.reshape(2 * WIDTH), flat_index(z, y, x, c) * 15, 15)
    return (
        result.transpose(0, 2, 1),
        grad_inputs.transpose(0, 2, 1),
        attn_owned,
        ffn_owned[:2],
        ffn_owned[2],
        gain_owned,
    )


def flat_index(z, y, x, c):
    return ((z * 4 + y) * 4 + x) * 2 + c


def solution(mesh):
    grid = Mesh(mesh.devices.reshape(4, 4, 4, 2), AXES)
    return jax.shard_map(
        body,
        mesh=grid,
        in_specs=(
            P(None, AXES, None),
            P(None, AXES),
            P(AXES, None),
            P(None, AXES, None),
            P(AXES, None),
            P(AXES),
            P(None, AXES, None),
        ),
        out_specs=(
            P(None, AXES, None),
            P(None, AXES, None),
            P(AXES, None),
            P(None, AXES, None),
            P(AXES, None),
            P(AXES),
        ),
        check_vma=False,
    )
```
